128 devices in a mesh: ctx: 16 (over y_lo, x, core), tp: 8 (over y_hi, z).
Axes of the slice: x: 4, y: 4 (y_hi: 2, y_lo: 2; y = y_hi * 2 + y_lo), z: 4, core: 2. Of those that a mesh axis runs over, the one named last changes fastest.
Arguments:
- tokens: bfloat16 [16384, 4096], P('ctx', 'tp'), may hold values from -6 to 6
- in_weight: bfloat16 [4096, 3, 4096], P('tp', None, 'ctx'), may hold values from -0.09375 to 0.09375
- short_filter: float32 [3, 3, 4096], replicated, may hold values from -3 to 3
- filter_residues: float32 [4096, 16], replicated, may hold values from -1.8 to 1.8
- filter_rates: float32 [4096, 16], replicated, may hold values from 3.0517578e-05 to 0.1
- skip_gain: float32 [4096], replicated, may hold values from -3 to 3
Outputs:
- gated: bfloat16 [16384, 4096], P('ctx', 'tp')
The draws below stay inside these ranges and needn't reach their ends.
All inputs are finite; a program needn't handle non-finite values.
Results may differ from the reference program's by a relative error of at most 0.034.
Values may be sent and summed in bfloat16 or wider, within the bound.
No kernel may reach another device: no remote copies, remote signals or barrier semaphores. Data moves between devices by JAX's collectives and lax.ppermute only.
A program may use at most 192 MiB of HBM per device.

```python
import math
import jax
import jax.numpy as jnp
from jax import lax

D = 4096
ORDER = 16
SEQ = 16384
N_TP = 8


def level_of(stream_key, extent, split, least, largest):
    loudness, own = 1.0, jax.random.fold_in(stream_key, 6)
    for axis_at, shards_of in split:
        draws = jnp.exp(jax.random.uniform(jax.random.fold_in(own, axis_at), (shards_of,), jnp.float32, least / len(split), largest / len(split)))
        loudness = loudness * jnp.repeat(draws, extent[axis_at] // shards_of).reshape([-1 if axis == axis_at else 1 for axis in range(len(extent))])
    return loudness


def noise(stream_key, dims, deviation, most, shards=(), held_as=jnp.bfloat16):
    drawn = jax.random.normal(stream_key, dims, jnp.float32) * deviation
    if len(shards) > 0:
        drawn = level_of(stream_key, dims, shards, -0.22, 0.18) * drawn
    return jnp.clip(drawn, min=-most, max=most).astype(held_as)


def setup_inputs(seed: int = 0) -> dict:
    key_of = jax.random.split(jax.random.key(seed), 7)
    return {
        "tokens": noise(key_of[0], (SEQ, D), 1.0, 6.0, ((0, 16), (1, 8))),
        "in_weight": noise(key_of[1], (D, 3, D), D ** -0.5, 0.09375, ((0, 8), (2, 16))),
        "short_filter": noise(key_of[2], (3, 3, D), 0.5, 3.0, (), jnp.float32),
        "filter_residues": noise(key_of[3], (D, ORDER), 0.3, 1.8, (), jnp.float32),
        "filter_rates": jnp.clip(jnp.exp(jax.random.uniform(key_of[4], (D, ORDER), jnp.float32, math.log(3.0517578125e-05), math.log(0.1))), 3.0517578125e-05, 0.1),
        "skip_gain": noise(key_of[5], (D,), 0.5, 3.0, (), jnp.float32),
    }


def reference(tokens, in_weight, short_filter, filter_residues, filter_rates, skip_gain):
    block_len = D // N_TP
    summed = jnp.zeros((SEQ, 3, D), jnp.float32)
    for tp_index in range(N_TP):
        left = tokens[:, tp_index * block_len:(tp_index + 1) * block_len].astype(jnp.float32)
        right = in_weight[tp_index * block_len:(tp_index + 1) * block_len].astype(jnp.float32)
        partial_value = jnp.einsum('ri,igc->rgc', left, right, precision=lax.Precision.HIGHEST)
        rounded = lax.optimization_barrier(partial_value.astype(jnp.bfloat16))
        summed = summed + rounded.astype(jnp.float32)
    projected = lax.optimization_barrier(summed.astype(jnp.bfloat16))
    fields = projected.astype(jnp.float32)
    padded = jnp.pad(fields, ((2, 0), (0, 0), (0, 0)))
    featured = short_filter[0] * fields + short_filter[1] * padded[1:SEQ + 1] + short_filter[2] * padded[0:SEQ]
    product = featured[:, 1, :] * featured[:, 2, :]
    lag_steps = jnp.arange(SEQ).astype(jnp.float32)
    response = jnp.zeros((D, SEQ), jnp.float32)
    for mode in range(ORDER):
        rate = filter_rates[:, mode][:, None]
        response = response + filter_residues[:, mode][:, None] * jnp.sqrt(rate) * jnp.exp(-rate * lag_steps[None, :])
    length = 2 * SEQ
    spec_data = jnp.fft.rfft(product.T, n=length, axis=1)
    spec_filter = jnp.fft.rfft(response, n=length, axis=1)
    convolution = jnp.fft.irfft(spec_data * spec_filter, n=length, axis=1)[:, :SEQ].T
    convolved = convolution + skip_gain[None, :] * product
    return (featured[:, 0, :] * convolved).astype(jnp.bfloat16)
```

```python
import functools

import jax
import jax.numpy as jnp
from jax import lax
from jax.experimental import pallas as pl
from jax.experimental.pallas import tpu as pltpu
from jax.sharding import PartitionSpec as P

D = 4096
MODES = 16
BLOCK = 512
SEG = 8
HALO = 16
SIZES = (2, 4, 2, 2, 4)
LANES = 128
CHUNKS = 2
F32 = jnp.float32


def route(move):
    pairs = []
    for yl in range(2):
        for x in range(4):
            for c in range(2):
                for yh in range(2):
                    for z in range(4):
                        to = move(yl, x, c, yh, z)
                        if to is None:
                            continue
                        a, b, e, f, g = to
                        pairs.append(
                            (
                                ((yl * 4 + x) * 2 + c) * 8 + yh * 4 + z,
                                (((a % 2) * 4 + b % 4) * 2 + e % 2) * 8 + (f % 2) * 4 + g % 4,
                            )
                        )
    return pairs


def send(value, move):
    return lax.ppermute(value, ("ctx", "tp"), route(move))


def along_z(value, step):
    return send(value, lambda yl, x, c, yh, z: (yl, x, c, yh, z + step))


def along_x(value, step):
    return send(value, lambda yl, x, c, yh, z: (yl, x + step, c, yh, z))


def other_core(value):
    return send(value, lambda yl, x, c, yh, z: (yl, x, c + 1, yh, z))


def other_yhi(value):
    return send(value, lambda yl, x, c, yh, z: (yl, x, c, yh + 1, z))


def other_ylo(value):
    return send(value, lambda yl, x, c, yh, z: (yl + 1, x, c, yh, z))


def transposed_piece(piece, p):
    return send(piece, lambda yl, x, c, yh, z: (yl, z + p, c, yh, x))


Y_A = {0: 1, 2: 0, 1: 3, 3: 2}
Y_B = {0: 0, 2: 1, 1: 2, 3: 3}


def along_y(value, table):
    def move(yl, x, c, yh, z):
        to = table[2 * yh + yl]
        return (to % 2, x, c, to // 2, z)

    return send(value, move)


def shift_down(value, steps):
    rows = lax.broadcasted_iota(jnp.int32, value.shape, 0)
    return jnp.where(rows >= steps, pltpu.roll(value, steps, 0), 0.0)


def project_kernel(rows, *refs):
    where, *refs = refs
    toks, refs = refs[:8], refs[8:]
    weights, refs = refs[:8], refs[8:]
    prm, y_ref, x1_ref, u_ref, lhs, wts, proj, sem_t, sem_w = refs
    seg_len = rows // SEG
    copies = []
    for s in range(8):
        for p in range(4):
            slot = where[s * 4 + p]
            copies.append(
                pltpu.make_async_copy(
                    toks[s].at[:, pl.ds(p * LANES, LANES)],
                    lhs.at[:, pl.ds(pl.multiple_of(slot * LANES, LANES), LANES)],
                    sem_t.at[s * 4 + p],
                )
            )
    width = 3 * LANES
    for k in range(4):
        for o in range(2):
            at = where[32 + o] * width
            copies.append(
                pltpu.make_async_copy(
                    weights[o * 4 + k],
                    wts.at[pl.ds(k * 1024, 1024), pl.ds(pl.multiple_of(at, LANES), width)],
                    sem_w.at[k * 2 + o],
                )
            )
    for copy in copies:
        copy.start()
    for copy in copies:
        copy.wait()

    tile = (rows + HALO) // 5

    def matmul(m, carry):
        at = pl.ds(pl.multiple_of(m * tile, 16), tile)
        out = jnp.dot(lhs[at, :], wts[...], preferred_element_type=F32)
        out = out.astype(jnp.bfloat16).astype(F32)
        for n in range(6):
            proj[n, at, :] = out[:, n * LANES:(n + 1) * LANES]
        return carry

    lax.fori_loop(0, 5, matmul, 0)

    for q in range(2):
        lanes = pl.ds(q * LANES, LANES)
        bcast = lambda r: jnp.broadcast_to(prm[pl.ds(r, 1), lanes], (SEG, LANES))
        decay = [bcast(k) for k in range(MODES)]
        amp = [bcast(MODES + k) for k in range(MODES)]
        taps = [[bcast(2 * MODES + 3 * j + g) for g in range(3)] for j in range(3)]
        gain = bcast(2 * MODES + 9)

        def load(g, at):
            return proj[q * 3 + g, pl.ds(at, SEG, stride=seg_len), :]

        def step(i, carry):
            before, last, states = carry
            now = [load(g, HALO + i) for g in range(3)]
            feat = [
                taps[0][g] * now[g] + taps[1][g] * last[g] + taps[2][g] * before[g]
                for g in range(3)
            ]
            product = feat[1] * feat[2]
            states = [decay[k] * states[k] + product for k in range(MODES)]
            terms = [amp[k] * states[k] for k in range(MODES)] + [gain * product]
            while len(terms) > 1:
                terms = [a + b for a, b in zip(terms[::2], terms[1::2])] + (
                    [terms[-1]] if len(terms) % 2 else []
                )
            at = pl.ds(pl.multiple_of(i * SEG, SEG), SEG)
            y_ref[at, lanes] = terms[0]
            x1_ref[at, lanes] = feat[0]
            return (last, now, states)

        zero = jnp.zeros((SEG, LANES), F32)
        first = ([load(g, HALO - 2) for g in range(3)], [load(g, HALO - 1) for g in range(3)])
        _, _, states = lax.fori_loop(0, seg_len, step, (*first, [zero] * MODES))
        for k in range(MODES):
            rate = prm[pl.ds(48 + k, 1), lanes]
            u = states[k]
            for n in (1, 2, 4):
                u = u + jnp.exp(-rate * (float(n) * seg_len)) * shift_down(u, n)
            u_ref[pl.ds(k * SEG, SEG), lanes] = u


def project(where, toks, weights, prm, rows):
    any_spec = pl.BlockSpec(memory_space=pl.ANY)
    vmem = pl.BlockSpec(memory_space=pltpu.VMEM)
    wide = 2 * LANES
    return pl.pallas_call(
        functools.partial(project_kernel, rows),
        out_shape=[
            jax.ShapeDtypeStruct((rows, wide), F32),
            jax.ShapeDtypeStruct((rows, wide), F32),
            jax.ShapeDtypeStruct((MODES * SEG, wide), F32),
        ],
        in_specs=[pl.BlockSpec(memory_space=pltpu.SMEM)] + [any_spec] * 16 + [vmem],
        out_specs=[vmem] * 3,
        scratch_shapes=[
            pltpu.VMEM((rows + HALO, D), jnp.bfloat16),
            pltpu.VMEM((D, 6 * LANES), jnp.bfloat16),
            pltpu.VMEM((6, rows + HALO, LANES), F32),
            pltpu.SemaphoreType.DMA((32,)),
            pltpu.SemaphoreType.DMA((8,)),
        ],
        compiler_params=pltpu.CompilerParams(vmem_limit_bytes=34 << 20),
        cost_estimate=pl.CostEstimate(
            flops=2 * rows * D * 6 * LANES, bytes_accessed=18 << 20, transcendentals=0
        ),
    )(where, *toks, *weights, prm)


def gate_kernel(rows, y0, y1, x0, x1, u0, u1, state_ref, prm0, prm1, out_ref, wide):
    seg_len = rows // SEG
    seg = lax.broadcasted_iota(jnp.int32, (SEG, LANES), 0).astype(F32) * seg_len
    for j, (y, x, u, prm) in enumerate(((y0, x0, u0, prm0), (y1, x1, u1, prm1))):
        for q in range(2):
            lanes = pl.ds(q * LANES, LANES)
            to = pl.ds(q * 2 * LANES + j * LANES, LANES)
            decay, carried = [], []
            for k in range(MODES):
                d = jnp.broadcast_to(prm[pl.ds(k, 1), lanes], (SEG, LANES))
                rate = prm[pl.ds(48 + k, 1), lanes]
                start = shift_down(u[pl.ds(k * SEG, SEG), lanes], 1)
                start = start + jnp.exp(-rate * seg) * state_ref[pl.ds(k, 1), to]
                decay.append(d)
                carried.append(prm[pl.ds(MODES + k, 1), lanes] * d * start)

            def step(i, carried):
                terms = list(carried)
                while len(terms) > 1:
                    terms = [a + b for a, b in zip(terms[::2], terms[1::2])]
                at = pl.ds(pl.multiple_of(i * SEG, SEG), SEG)
                wide[q * 2 + j, pl.ds(i, SEG, stride=seg_len), :] = x[at, lanes] * (
                    y[at, lanes] + terms[0]
                )
                return [c * d for c, d in zip(carried, decay)]

            lax.fori_loop(0, seg_len, step, carried)
    for n in range(BLOCK // LANES):
        out_ref[:, n * LANES:(n + 1) * LANES] = wide[n].astype(out_ref.dtype)


def gate(ys, xs, us, state, prms, rows):
    vmem = pl.BlockSpec(memory_space=pltpu.VMEM)
    return pl.pallas_call(
        functools.partial(gate_kernel, rows),
        out_shape=jax.ShapeDtypeStruct((rows, BLOCK), jnp.bfloat16),
        in_specs=[vmem] * 9,
        out_specs=vmem,
        scratch_shapes=[pltpu.VMEM((BLOCK // LANES, rows, LANES), F32)],
        compiler_params=pltpu.CompilerParams(vmem_limit_bytes=20 << 20),
    )(*ys, *xs, *us, state, *prms)


def earlier_state(total, rate, rows, x, core, y_lo):
    def fade(n):
        return jnp.exp(-rate * n.astype(F32) if hasattr(n, "astype") else -rate * float(n))

    peer = other_core(total)
    first, second = jnp.where(core == 0, total, peer), jnp.where(core == 0, peer, total)
    chip = fade(rows) * first + second
    behind = [along_x(chip, m) for m in (1, 2, 3)]
    upto = jnp.zeros_like(chip)
    for m in (1, 2, 3):
        upto = upto + jnp.where(x >= m, fade(2 * rows * (m - 1)), 0.0) * behind[m - 1]
    plane = jnp.zeros_like(chip)
    for m, value in enumerate([chip] + behind):
        of = (x - m) % 4
        plane = plane + fade(2 * rows * (3 - of)) * value
    lower = other_ylo(plane)
    start = upto + jnp.where(y_lo == 1, fade(2 * rows * x), 0.0) * lower
    return jnp.where(core == 0, start, fade(rows) * start + peer)


def on_device(tokens, in_weight, short_filter, filter_residues, filter_rates, skip_gain):
    rows = tokens.shape[0]
    ctx, tp = lax.axis_index("ctx"), lax.axis_index("tp")
    y_lo, x, core = ctx // 8, (ctx // 2) % 4, ctx % 2
    y_hi, z = tp // 4, tp % 4

    ordered = in_weight.reshape(BLOCK, 3, CHUNKS, LANES).transpose(0, 2, 1, 3).reshape(BLOCK, -1)
    quarter = BLOCK // 4
    pieces = [transposed_piece(ordered[p * quarter:(p + 1) * quarter], p) for p in range(4)]
    turned = jnp.concatenate(pieces, axis=0)
    from_a, from_b = along_y(turned, Y_A), along_y(turned, Y_B)

    def next_ctx(yl, x, c, yh, z):
        n = (yl * 4 + x) * 2 + c + 1
        return None if n == 16 else (n // 8, (n // 2) % 4, n % 2, yh, z)

    halo = send(tokens[rows - HALO:], next_ctx)
    own = jnp.concatenate([halo, tokens], axis=0)
    mine, theirs = [own], [other_yhi(own)]
    mine += [along_z(own, 1), along_z(own, -1)]
    theirs += [along_z(theirs[0], 1), along_z(theirs[0], -1)]
    mine.append(along_z(mine[1], 1))
    theirs.append(along_z(theirs[2], -1))
    toks = mine + theirs

    slots = []
    for dy in range(2):
        of_y = (y_hi + dy) % 2
        half = jnp.where(of_y == y_lo, 1, 0)
        for dz in (0, -1, 1, 2):
            of_z = (z + dz) % 4
            for p in range(4):
                ring = (of_z + p - x) % 4
                k = jnp.where(ring == 3, 1, jnp.where(ring == 1, 2, jnp.where(ring == 2, 3, 0)))
                slots.append((k * 2 + half) * 4 + p)
    where = jnp.stack(slots + [core, 1 - core]).astype(jnp.int32)

    base = tp * BLOCK
    rates = lax.dynamic_slice_in_dim(filter_rates, base, BLOCK, 0).T
    amps = lax.dynamic_slice_in_dim(filter_residues, base, BLOCK, 0).T * jnp.sqrt(rates)
    taps = lax.dynamic_slice_in_dim(short_filter, base, BLOCK, 2).reshape(9, BLOCK)
    gains = lax.dynamic_slice_in_dim(skip_gain, base, BLOCK, 0)[None]
    prm = jnp.concatenate(
        [jnp.exp(-rates), amps, taps, gains, jnp.zeros((6, BLOCK), F32), rates], axis=0
    )

    width = 3 * LANES
    ys, xs, us, prms = [], [], [], []
    for j in range(CHUNKS):
        cut = slice(j * width, (j + 1) * width)
        held = jnp.concatenate([from_a[:, cut], from_b[:, cut]], axis=0)
        up, down = along_x(held, 1), along_x(held, -1)
        far = along_x(up, 1) if j == 0 else along_x(down, -1)
        ring = [held, up, down, far]
        weights = ring + [other_core(w) for w in ring]
        prm_j = jnp.concatenate(
            [prm[:, c * 2 * LANES + j * LANES:c * 2 * LANES + (j + 1) * LANES] for c in range(2)],
            axis=1,
        )
        y, x1, u = project(where, toks, weights, prm_j, rows)
        ys.append(y)
        xs.append(x1)
        us.append(u)
        prms.append(prm_j)

    ends = [u.reshape(MODES, SEG, 2 * LANES)[:, SEG - 1] for u in us]
    total = jnp.concatenate(
        [ends[j][:, c * LANES:(c + 1) * LANES] for c in range(2) for j in range(CHUNKS)], axis=1
    )
    state = earlier_state(total, rates, rows, x, core, y_lo)
    return gate(ys, xs, us, state, prms, rows)


def solution(mesh):
    placed = (P("ctx", "tp"), P("tp", None, "ctx"), P(), P(), P(), P())
    return jax.shard_map(
        on_device, mesh=mesh, in_specs=placed, out_specs=P("ctx", "tp"), check_vma=False
    )
```

```python
import functools

import jax
import jax.numpy as jnp
from jax import lax
from jax.experimental import pallas as pl
from jax.experimental.pallas import tpu as pltpu
from jax.sharding import PartitionSpec as P

D = 4096
MODES = 16
BLOCK = 512
SEG = 8
HALO = 16
SIZES = (2, 4, 2, 2, 4)
LANES = 128
F32 = jnp.float32


def route(move):
    pairs = []
    for yl in range(2):
        for x in range(4):
            for c in range(2):
                for yh in range(2):
                    for z in range(4):
                        to = move(yl, x, c, yh, z)
                        if to is None:
                            continue
                        a, b, e, f, g = to
                        pairs.append(
                            (
                                ((yl * 4 + x) * 2 + c) * 8 + yh * 4 + z,
                                (((a % 2) * 4 + b % 4) * 2 + e % 2) * 8 + (f % 2) * 4 + g % 4,
                            )
                        )
    return pairs


def send(value, move):
    return lax.ppermute(value, ("ctx", "tp"), route(move))


def along_z(value, step):
    return send(value, lambda yl, x, c, yh, z: (yl, x, c, yh, z + step))


def along_x(value, step):
    return send(value, lambda yl, x, c, yh, z: (yl, x + step, c, yh, z))


def other_core(value):
    return send(value, lambda yl, x, c, yh, z: (yl, x, c + 1, yh, z))


def other_yhi(value):
    return send(value, lambda yl, x, c, yh, z: (yl, x, c, yh + 1, z))


def other_ylo(value):
    return send(value, lambda yl, x, c, yh, z: (yl + 1, x, c, yh, z))


def other_ylo_and_core(value):
    return send(value, lambda yl, x, c, yh, z: (yl + 1, x, c + 1, yh, z))


def transposed(value):
    return send(value, lambda yl, x, c, yh, z: (yh, x + z, c, yl, x))


together = lax.optimization_barrier


def shift_down(value, steps):
    rows = lax.broadcasted_iota(jnp.int32, value.shape, 0)
    return jnp.where(rows >= steps, pltpu.roll(value, steps, 0), 0.0)


def project_kernel(rows, *refs):
    where, *refs = refs
    toks, refs = refs[:8], refs[8:]
    weights, refs = refs[:8], refs[8:]
    prm, y_ref, x1_ref, u_ref, end_ref, lhs, wts, proj, sem_t, sem_w = refs
    seg_len = rows // SEG
    width = 3 * LANES
    copies = []
    for s in range(8):
        copies.append(
            pltpu.make_async_copy(toks[s], lhs.at[:, pl.ds(s * BLOCK, BLOCK)], sem_t.at[s])
        )
    for k in range(8):
        at = pl.multiple_of(where[k] * BLOCK, BLOCK)
        copies.append(pltpu.make_async_copy(weights[k], wts.at[pl.ds(at, BLOCK), :], sem_w.at[k]))
    for copy in copies:
        copy.start()
    for copy in copies:
        copy.wait()

    tile = (rows + HALO) // 5

    def matmul(m, carry):
        at = pl.ds(pl.multiple_of(m * tile, 16), tile)
        out = jnp.dot(lhs[at, :], wts[...], preferred_element_type=F32)
        out = out.astype(jnp.bfloat16).astype(F32)
        for n in range(6):
            proj[n, at, :] = out[:, n * LANES:(n + 1) * LANES]
        return carry

    lax.fori_loop(0, 5, matmul, 0)

    for q in range(2):
        lanes = pl.ds(q * LANES, LANES)
        bcast = lambda r: jnp.broadcast_to(prm[pl.ds(r, 1), lanes], (SEG, LANES))
        decay = [bcast(k) for k in range(MODES)]
        amp = [bcast(MODES + k) for k in range(MODES)]
        taps = [[bcast(2 * MODES + 3 * j + g) for g in range(3)] for j in range(3)]
        gain = bcast(2 * MODES + 9)

        def load(g, at):
            return proj[2 * g + q, pl.ds(at, SEG, stride=seg_len), :]

        def step(i, carry):
            before, last, states = carry
            now = [load(g, HALO + i) for g in range(3)]
            feat = [
                taps[0][g] * now[g] + taps[1][g] * last[g] + taps[2][g] * before[g]
                for g in range(3)
            ]
            product = feat[1] * feat[2]
            states = [decay[k] * states[k] + product for k in range(MODES)]
            terms = [amp[k] * states[k] for k in range(MODES)] + [gain * product]
            while len(terms) > 1:
                terms = [a + b for a, b in zip(terms[::2], terms[1::2])] + (
                    [terms[-1]] if len(terms) % 2 else []
                )
            at = pl.ds(pl.multiple_of(i * SEG, SEG), SEG)
            y_ref[at, lanes] = terms[0]
            x1_ref[at, lanes] = feat[0]
            return (last, now, states)

        zero = jnp.zeros((SEG, LANES), F32)
        first = ([load(g, HALO - 2) for g in range(3)], [load(g, HALO - 1) for g in range(3)])
        _, _, states = lax.fori_loop(0, seg_len, step, (*first, [zero] * MODES), unroll=4)
        for k in range(MODES):
            rate = prm[pl.ds(48 + k, 1), lanes]
            u = states[k]
            for n in (1, 2, 4):
                u = u + jnp.exp(-rate * (float(n) * seg_len)) * shift_down(u, n)
            u_ref[pl.ds(k * SEG, SEG), lanes] = u
            end_ref[pl.ds(k, 1), lanes] = u[SEG - 1:]


def project(where, toks, weights, prm, rows):
    any_spec = pl.BlockSpec(memory_space=pl.ANY)
    vmem = pl.BlockSpec(memory_space=pltpu.VMEM)
    wide = 2 * LANES
    return pl.pallas_call(
        functools.partial(project_kernel, rows),
        out_shape=[
            jax.ShapeDtypeStruct((rows, wide), F32),
            jax.ShapeDtypeStruct((rows, wide), F32),
            jax.ShapeDtypeStruct((MODES * SEG, wide), F32),
            jax.ShapeDtypeStruct((MODES, wide), F32),
        ],
        in_specs=[pl.BlockSpec(memory_space=pltpu.SMEM)] + [any_spec] * 16 + [vmem],
        out_specs=[vmem] * 4,
        scratch_shapes=[
            pltpu.VMEM((rows + HALO, D), jnp.bfloat16),
            pltpu.VMEM((D, 6 * LANES), jnp.bfloat16),
            pltpu.VMEM((6, rows + HALO, LANES), F32),
            pltpu.SemaphoreType.DMA((8,)),
            pltpu.SemaphoreType.DMA((8,)),
        ],
        compiler_params=pltpu.CompilerParams(vmem_limit_bytes=34 << 20),
        cost_estimate=pl.CostEstimate(
            flops=2 * rows * D * 6 * LANES, bytes_accessed=18 << 20, transcendentals=0
        ),
    )(where, *toks, *weights, prm)


def gate_kernel(rows, core_ref, y0, y1, x0, x1, u0, u1, p0, p1, near, sent, same, cross, fades,
                out_ref, ybuf, xbuf, wide, sem):
    seg_len = rows // SEG
    core = core_ref[0]
    copies = []
    for o, (y, x) in enumerate(((y0, x0), (y1, x1))):
        copies.append(
            (
                pltpu.make_async_copy(y, ybuf.at[o], sem.at[2 * o]),
                pltpu.make_async_copy(x, xbuf.at[o], sem.at[2 * o + 1]),
            )
        )
        for copy in copies[o]:
            copy.start()
    seg = lax.broadcasted_iota(jnp.int32, (SEG, LANES), 0).astype(F32) * seg_len
    for o, (u, prm) in enumerate(((u0, p0), (u1, p1))):
        base = lax.rem(core + o, 2) * (2 * LANES)
        for q in range(2):
            lanes = pl.ds(q * LANES, LANES)
            to = pl.ds(pl.multiple_of(base + q * LANES, LANES), LANES)
            shard, straight, across = (
                fades[pl.ds(n * MODES, MODES), to] for n in range(3)
            )
            state = (
                shard * near[:, to] + sent[:, to] + straight * same[:, to] + across * cross[:, to]
            )
            decay, carried = [], []
            for k in range(MODES):
                d = jnp.broadcast_to(prm[pl.ds(k, 1), lanes], (SEG, LANES))
                rate = prm[pl.ds(48 + k, 1), lanes]
                start = shift_down(u[pl.ds(k * SEG, SEG), lanes], 1)
                start = start + jnp.exp(-rate * seg) * state[k:k + 1]
                decay.append(d)
                carried.append(prm[pl.ds(MODES + k, 1), lanes] * d * start)
            if q == 0:
                for copy in copies[o]:
                    copy.wait()

            def step(i, carried):
                terms = list(carried)
                while len(terms) > 1:
                    terms = [a + b for a, b in zip(terms[::2], terms[1::2])]
                at = pl.ds(pl.multiple_of(i * SEG, SEG), SEG)
                wide[pl.ds(i, SEG, stride=seg_len), :] = xbuf[o, at, lanes] * (
                    ybuf[o, at, lanes] + terms[0]
                )
                return [c * d for c, d in zip(carried, decay)]

            lax.fori_loop(0, seg_len, step, carried, unroll=4)
            out_ref[:, to] = wide[...].astype(out_ref.dtype)


def gate(core, ys, xs, us, prms, state, rows):
    vmem = pl.BlockSpec(memory_space=pltpu.VMEM)
    anywhere = pl.BlockSpec(memory_space=pl.ANY)
    wide = 2 * LANES
    return pl.pallas_call(
        functools.partial(gate_kernel, rows),
        out_shape=jax.ShapeDtypeStruct((rows, BLOCK), jnp.bfloat16),
        in_specs=[pl.BlockSpec(memory_space=pltpu.SMEM)] + [anywhere] * 4 + [vmem] * 9,
        out_specs=vmem,
        scratch_shapes=[
            pltpu.VMEM((2, rows, wide), F32),
            pltpu.VMEM((2, rows, wide), F32),
            pltpu.VMEM((rows, LANES), F32),
            pltpu.SemaphoreType.DMA((4,)),
        ],
        compiler_params=pltpu.CompilerParams(vmem_limit_bytes=20 << 20),
    )(core, *ys, *xs, *us, *prms, *state)


def on_device(tokens, in_weight, short_filter, filter_residues, filter_rates, skip_gain):
    rows = tokens.shape[0]
    ctx, tp = lax.axis_index("ctx"), lax.axis_index("tp")
    y_lo, x, core = ctx // 8, (ctx // 2) % 4, ctx % 2
    y_hi, z = tp // 4, tp % 4
    wide = 2 * LANES

    base = tp * BLOCK
    rates = lax.dynamic_slice_in_dim(filter_rates, base, BLOCK, 0).T
    amps = lax.dynamic_slice_in_dim(filter_residues, base, BLOCK, 0).T * jnp.sqrt(rates)
    taps = lax.dynamic_slice_in_dim(short_filter, base, BLOCK, 2).reshape(9, BLOCK)
    gains = lax.dynamic_slice_in_dim(skip_gain, base, BLOCK, 0)[None]
    prm = jnp.concatenate(
        [jnp.exp(-rates), amps, taps, gains, jnp.zeros((6, BLOCK), F32), rates], axis=0
    )
    prms = [lax.dynamic_slice_in_dim(prm, (core + o) % 2 * wide, wide, 1) for o in range(2)]

    def fade(steps):
        return jnp.exp(-rates * jnp.asarray(steps).astype(F32))

    shard = fade(rows)
    behind = [jnp.where(x >= m, fade(2 * rows * (m - 1)), 0.0) for m in (1, 2, 3)]
    plane = [fade(2 * rows * (3 - (x - m) % 4)) for m in range(4)]
    chip = fade(2 * rows)
    lower = jnp.where(y_lo == 1, fade(2 * rows * x), 0.0)
    straight = lower * shard
    across = lower * jnp.where(core == 0, 1.0, shard * shard)
    fades = jnp.concatenate([shard, straight, across], axis=0)
    behind, plane = jnp.stack(behind), jnp.stack(plane)

    slots = []
    for of_y in (y_lo, 1 - y_lo):
        for ring in (0, -1, 1, 2):
            of_z = (x + ring - z) % 4
            step = (of_z - z) % 4
            place = jnp.where(step == 3, 1, jnp.where(step == 1, 2, jnp.where(step == 2, 3, 0)))
            slots.append(jnp.where(of_y == y_hi, 0, 4) + place)
    where = jnp.stack(slots + [core]).astype(jnp.int32)
    core_at = jnp.stack([core]).astype(jnp.int32)

    def next_ctx(yl, x, c, yh, z):
        n = (yl * 4 + x) * 2 + c + 1
        return None if n == 16 else (n // 8, (n // 2) % 4, n % 2, yh, z)

    halo = send(tokens[rows - HALO:], next_ctx)
    b = transposed(in_weight.reshape(BLOCK, 3 * wide))
    t = jnp.concatenate([halo, tokens], axis=0)
    t, b, where, core_at, fades, behind, plane, chip, *prms = together(
        (t, b, where, core_at, fades, behind, plane, chip, *prms)
    )
    tp_, tm, ty = along_z(t, 1), along_z(t, -1), other_yhi(t)
    bp, bm = along_x(b, 1), along_x(b, -1)
    t, b, tp_, tm, ty, bp, bm = together((t, b, tp_, tm, ty, bp, bm))
    typ, tym = along_z(ty, 1), along_z(ty, -1)
    bf, a = along_x(bp, 1), other_ylo(b)
    cb = other_core(b)
    t, b, tp_, tm, ty, bp, bm, typ, tym, bf, a, cb = together(
        (t, b, tp_, tm, ty, bp, bm, typ, tym, bf, a, cb)
    )
    tf, tyf = along_z(tp_, 1), along_z(tym, -1)
    ap, am, af = along_x(a, 1), along_x(a, -1), other_ylo(bf)
    b, bp, bm, bf, a, ap, am, af, tf, tyf = together((b, bp, bm, bf, a, ap, am, af, tf, tyf))
    toks = [t, tp_, tm, tf, ty, typ, tym, tyf]
    mine = [b, bp, bm, bf, a, ap, am, af]
    theirs = [cb] + [other_core(w) for w in mine[1:]]

    ys, xs, us, ends = [], [], [], []
    for o, weights in enumerate((mine, theirs)):
        y, x1, u, end = project(where, toks, weights, prms[o], rows)
        ys.append(y)
        xs.append(x1)
        us.append(u)
        ends.append(end)

    total = jnp.concatenate(
        [jnp.where(core == 0, ends[0], ends[1]), jnp.where(core == 0, ends[1], ends[0])], axis=1
    )
    came = [total] + [along_x(total, m) for m in (1, 2, 3)]
    near = behind[0] * came[1] + behind[1] * came[2] + behind[2] * came[3]
    whole = plane[0] * came[0] + plane[1] * came[1] + plane[2] * came[2] + plane[3] * came[3]
    sent = other_core(jnp.where(core == 0, chip * near + total, near))
    state = [near, sent, other_ylo(whole), other_ylo_and_core(whole), fades]
    return gate(core_at, ys, xs, us, prms, state, rows)


def solution(mesh):
    placed = (P("ctx", "tp"), P("tp", None, "ctx"), P(), P(), P(), P())
    return jax.shard_map(
        on_device, mesh=mesh, in_specs=placed, out_specs=P("ctx", "tp"), check_vma=False
    )
```

```python
import functools

import jax
import jax.numpy as jnp
from jax import lax
from jax.experimental import pallas as pl
from jax.experimental.pallas import tpu as pltpu
from jax.sharding import PartitionSpec as P

D = 4096
MODES = 16
BLOCK = 512
SEG = 8
HALO = 16
SIZES = (2, 4, 2, 2, 4)
LANES = 128
F32 = jnp.float32


def route(move):
    pairs = []
    for yl in range(2):
        for x in range(4):
            for c in range(2):
                for yh in range(2):
                    for z in range(4):
                        to = move(yl, x, c, yh, z)
                        if to is None:
                            continue
                        a, b, e, f, g = to
                        pairs.append(
                            (
                                ((yl * 4 + x) * 2 + c) * 8 + yh * 4 + z,
                                (((a % 2) * 4 + b % 4) * 2 + e % 2) * 8 + (f % 2) * 4 + g % 4,
                            )
                        )
    return pairs


def send(value, move):
    return lax.ppermute(value, ("ctx", "tp"), route(move))


def along_z(value, step):
    return send(value, lambda yl, x, c, yh, z: (yl, x, c, yh, z + step))


def along_x(value, step):
    return send(value, lambda yl, x, c, yh, z: (yl, x + step, c, yh, z))


def other_core(value):
    return send(value, lambda yl, x, c, yh, z: (yl, x, c + 1, yh, z))


def other_yhi(value):
    return send(value, lambda yl, x, c, yh, z: (yl, x, c, yh + 1, z))


def other_ylo(value):
    return send(value, lambda yl, x, c, yh, z: (yl + 1, x, c, yh, z))


def other_ylo_and_core(value):
    return send(value, lambda yl, x, c, yh, z: (yl + 1, x, c + 1, yh, z))


def transposed(value):
    return send(value, lambda yl, x, c, yh, z: (yh, x + z, c, yl, x))


together = lax.optimization_barrier


def shift_down(value, steps):
    rows = lax.broadcasted_iota(jnp.int32, value.shape, 0)
    return jnp.where(rows >= steps, pltpu.roll(value, steps, 0), 0.0)


def row_tiles(rows, body):
    tile = (rows + HALO) // 5

    def step(m, carry):
        body(pl.ds(pl.multiple_of(m * tile, 16), tile))
        return carry

    lax.fori_loop(0, 5, step, 0)


def copy_rows(rows, target, source):
    def body(at):
        target[at, :] = source[at, :]

    row_tiles(rows, body)


def first_half(rows, where, lhs, weights, acc):
    def clear(at):
        acc[at, :] = jnp.zeros((at.size, acc.shape[1]), F32)

    row_tiles(rows, clear)
    for k in range(4):
        slot = where[k]

        @pl.when(lax.rem(slot, 4) != 3)
        def _(k=k, slot=slot):
            def body(at):
                acc[at, :] += jnp.dot(lhs[slot, at, :], weights[k][...], preferred_element_type=F32)

            row_tiles(rows, body)


def begin_kernel(rows, where, *refs):
    toks, weights, (lhs, acc) = refs[:6], refs[6:10], refs[10:]
    for n, s in enumerate((0, 1, 2, 4, 5, 6)):
        copy_rows(rows, lhs.at[s], toks[n])
    first_half(rows, where, lhs, weights, acc)


def also_kernel(rows, where, *refs):
    lhs, weights, acc = refs[0], refs[1:5], refs[5]
    first_half(rows, where, lhs, weights, acc)


def begin(where, toks, weights, rows):
    vmem = pl.BlockSpec(memory_space=pltpu.VMEM)
    tall, width = rows + HALO, weights[0].shape[1]
    return pl.pallas_call(
        functools.partial(begin_kernel, rows),
        out_shape=[
            jax.ShapeDtypeStruct((8, tall, BLOCK), jnp.bfloat16),
            jax.ShapeDtypeStruct((tall, width), F32),
        ],
        in_specs=[pl.BlockSpec(memory_space=pltpu.SMEM)] + [vmem] * 10,
        out_specs=[vmem] * 2,
        compiler_params=pltpu.CompilerParams(vmem_limit_bytes=26 << 20),
        cost_estimate=pl.CostEstimate(
            flops=2 * tall * 3 * BLOCK * width, bytes_accessed=12 << 20, transcendentals=0
        ),
    )(where, *toks, *weights)


def also(where, lhs, weights, rows):
    vmem = pl.BlockSpec(memory_space=pltpu.VMEM)
    tall, width = rows + HALO, weights[0].shape[1]
    return pl.pallas_call(
        functools.partial(also_kernel, rows),
        out_shape=jax.ShapeDtypeStruct((tall, width), F32),
        in_specs=[pl.BlockSpec(memory_space=pltpu.SMEM)] + [vmem] * 5,
        out_specs=vmem,
        compiler_params=pltpu.CompilerParams(vmem_limit_bytes=26 << 20),
        cost_estimate=pl.CostEstimate(
            flops=2 * tall * 3 * BLOCK * width, bytes_accessed=12 << 20, transcendentals=0
        ),
    )(where, lhs, *weights)


def project_kernel(rows, where, *refs):
    lhs, near, far, part, *refs = refs
    weights, refs = refs[:8], refs[8:]
    prm, y_ref, x1_ref, u_ref, end_ref, last, acc, proj = refs
    seg_len = rows // SEG
    for k in range(4):
        slot = where[4 + k]

        @pl.when(lax.rem(slot, 4) != 3)
        def _(k=k, slot=slot):
            copy_rows(rows, last.at[k], lhs.at[slot])

        for s, ref in ((3, near), (7, far)):

            @pl.when(slot == s)
            def _(k=k, ref=ref):
                copy_rows(rows, last.at[k], ref)

            @pl.when(where[k] == s)
            def _(k=k, ref=ref):
                def body(at):
                    acc[at, :] = part[at, :] + jnp.dot(
                        ref[at, :], weights[k][...], preferred_element_type=F32
                    )

                row_tiles(rows, body)

    def finish(at):
        out = acc[at, :]
        for k in range(4):
            out = out + jnp.dot(
                last[k, at, :], weights[4 + k][...], preferred_element_type=F32
            )
        out = out.astype(jnp.bfloat16).astype(F32)
        for n in range(6):
            proj[n, at, :] = out[:, n * LANES:(n + 1) * LANES]

    row_tiles(rows, finish)

    for q in range(2):
        lanes = pl.ds(q * LANES, LANES)
        bcast = lambda r: jnp.broadcast_to(prm[pl.ds(r, 1), lanes], (SEG, LANES))
        decay = [bcast(k) for k in range(MODES)]
        amp = [bcast(MODES + k) for k in range(MODES)]
        taps = [[bcast(2 * MODES + 3 * j + g) for g in range(3)] for j in range(3)]
        gain = bcast(2 * MODES + 9)

        def load(g, at):
            return proj[2 * g + q, pl.ds(at, SEG, stride=seg_len), :]

        def step(i, carry):
            before, last, states = carry
            now = [load(g, HALO + i) for g in range(3)]
            feat = [
                taps[0][g] * now[g] + taps[1][g] * last[g] + taps[2][g] * before[g]
                for g in range(3)
            ]
            product = feat[1] * feat[2]
            states = [decay[k] * states[k] + product for k in range(MODES)]
            terms = [amp[k] * states[k] for k in range(MODES)] + [gain * product]
            while len(terms) > 1:
                terms = [a + b for a, b in zip(terms[::2], terms[1::2])] + (
                    [terms[-1]] if len(terms) % 2 else []
                )
            at = pl.ds(pl.multiple_of(i * SEG, SEG), SEG)
            y_ref[at, lanes] = terms[0]
            x1_ref[at, lanes] = feat[0]
            return (last, now, states)

        zero = jnp.zeros((SEG, LANES), F32)
        first = ([load(g, HALO - 2) for g in range(3)], [load(g, HALO - 1) for g in range(3)])
        _, _, states = lax.fori_loop(0, seg_len, step, (*first, [zero] * MODES), unroll=4)
        for k in range(MODES):
            rate = prm[pl.ds(48 + k, 1), lanes]
            u = states[k]
            for n in (1, 2, 4):
                u = u + jnp.exp(-rate * (float(n) * seg_len)) * shift_down(u, n)
            u_ref[pl.ds(k * SEG, SEG), lanes] = u
            end_ref[pl.ds(k, 1), lanes] = u[SEG - 1:]


def project(where, lhs, near, far, part, weights, prm, rows):
    vmem = pl.BlockSpec(memory_space=pltpu.VMEM)
    wide, tall = 2 * LANES, rows + HALO
    return pl.pallas_call(
        functools.partial(project_kernel, rows),
        out_shape=[
            jax.ShapeDtypeStruct((rows, wide), F32),
            jax.ShapeDtypeStruct((rows, wide), F32),
            jax.ShapeDtypeStruct((MODES * SEG, wide), F32),
            jax.ShapeDtypeStruct((MODES, wide), F32),
        ],
        in_specs=[pl.BlockSpec(memory_space=pltpu.SMEM)] + [vmem] * 13,
        out_specs=[vmem] * 4,
        scratch_shapes=[
            pltpu.VMEM((4, tall, BLOCK), jnp.bfloat16),
            pltpu.VMEM((tall, 3 * wide), F32),
            pltpu.VMEM((6, tall, LANES), F32),
        ],
        compiler_params=pltpu.CompilerParams(vmem_limit_bytes=26 << 20),
        cost_estimate=pl.CostEstimate(
            flops=2 * tall * 5 * BLOCK * 3 * wide, bytes_accessed=12 << 20, transcendentals=0
        ),
    )(where, lhs, near, far, part, *weights, prm)


def gate_kernel(rows, core_ref, y0, y1, x0, x1, u0, u1, p0, p1, near, sent, same, cross, fades,
                out_ref, ybuf, xbuf, wide, sem):
    seg_len = rows // SEG
    core = core_ref[0]
    copies = []
    for o, (y, x) in enumerate(((y0, x0), (y1, x1))):
        copies.append(
            (
                pltpu.make_async_copy(y, ybuf.at[o], sem.at[2 * o]),
                pltpu.make_async_copy(x, xbuf.at[o], sem.at[2 * o + 1]),
            )
        )
        for copy in copies[o]:
            copy.start()
    seg = lax.broadcasted_iota(jnp.int32, (SEG, LANES), 0).astype(F32) * seg_len
    for o, (u, prm) in enumerate(((u0, p0), (u1, p1))):
        base = lax.rem(core + o, 2) * (2 * LANES)
        for q in range(2):
            lanes = pl.ds(q * LANES, LANES)
            to = pl.ds(pl.multiple_of(base + q * LANES, LANES), LANES)
            shard, straight, across = (
                fades[pl.ds(n * MODES, MODES), to] for n in range(3)
            )
            state = (
                shard * near[:, to] + sent[:, to] + straight * same[:, to] + across * cross[:, to]
            )
            decay, carried = [], []
            for k in range(MODES):
                d = jnp.broadcast_to(prm[pl.ds(k, 1), lanes], (SEG, LANES))
                rate = prm[pl.ds(48 + k, 1), lanes]
                start = shift_down(u[pl.ds(k * SEG, SEG), lanes], 1)
                start = start + jnp.exp(-rate * seg) * state[k:k + 1]
                decay.append(d)
                carried.append(prm[pl.ds(MODES + k, 1), lanes] * d * start)
            if q == 0:
                for copy in copies[o]:
                    copy.wait()

            def step(i, carried):
                terms = list(carried)
                while len(terms) > 1:
                    terms = [a + b for a, b in zip(terms[::2], terms[1::2])]
                at = pl.ds(pl.multiple_of(i * SEG, SEG), SEG)
                wide[pl.ds(i, SEG, stride=seg_len), :] = xbuf[o, at, lanes] * (
                    ybuf[o, at, lanes] + terms[0]
                )
                return [c * d for c, d in zip(carried, decay)]

            lax.fori_loop(0, seg_len, step, carried, unroll=4)
            out_ref[:, to] = wide[...].astype(out_ref.dtype)


def gate(core, ys, xs, us, prms, state, rows):
    vmem = pl.BlockSpec(memory_space=pltpu.VMEM)
    anywhere = pl.BlockSpec(memory_space=pl.ANY)
    wide = 2 * LANES
    return pl.pallas_call(
        functools.partial(gate_kernel, rows),
        out_shape=jax.ShapeDtypeStruct((rows, BLOCK), jnp.bfloat16),
        in_specs=[pl.BlockSpec(memory_space=pltpu.SMEM)] + [anywhere] * 4 + [vmem] * 9,
        out_specs=vmem,
        scratch_shapes=[
            pltpu.VMEM((2, rows, wide), F32),
            pltpu.VMEM((2, rows, wide), F32),
            pltpu.VMEM((rows, LANES), F32),
            pltpu.SemaphoreType.DMA((4,)),
        ],
        compiler_params=pltpu.CompilerParams(vmem_limit_bytes=20 << 20),
    )(core, *ys, *xs, *us, *prms, *state)


def on_device(tokens, in_weight, short_filter, filter_residues, filter_rates, skip_gain):
    rows = tokens.shape[0]
    ctx, tp = lax.axis_index("ctx"), lax.axis_index("tp")
    y_lo, x, core = ctx // 8, (ctx // 2) % 4, ctx % 2
    y_hi, z = tp // 4, tp % 4
    wide = 2 * LANES

    base = tp * BLOCK
    rates = lax.dynamic_slice_in_dim(filter_rates, base, BLOCK, 0).T
    amps = lax.dynamic_slice_in_dim(filter_residues, base, BLOCK, 0).T * jnp.sqrt(rates)
    taps = lax.dynamic_slice_in_dim(short_filter, base, BLOCK, 2).reshape(9, BLOCK)
    gains = lax.dynamic_slice_in_dim(skip_gain, base, BLOCK, 0)[None]
    prm = jnp.concatenate(
        [jnp.exp(-rates), amps, taps, gains, jnp.zeros((6, BLOCK), F32), rates], axis=0
    )
    prms = [lax.dynamic_slice_in_dim(prm, (core + o) % 2 * wide, wide, 1) for o in range(2)]

    def fade(steps):
        return jnp.exp(-rates * jnp.asarray(steps).astype(F32))

    shard = fade(rows)
    behind = [jnp.where(x >= m, fade(2 * rows * (m - 1)), 0.0) for m in (1, 2, 3)]
    plane = [fade(2 * rows * (3 - (x - m) % 4)) for m in range(4)]
    chip = fade(2 * rows)
    lower = jnp.where(y_lo == 1, fade(2 * rows * x), 0.0)
    straight = lower * shard
    across = lower * jnp.where(core == 0, 1.0, shard * shard)
    fades = jnp.concatenate([shard, straight, across], axis=0)
    behind, plane = jnp.stack(behind), jnp.stack(plane)

    slots = []
    for of_y in (y_lo, 1 - y_lo):
        for ring in (0, -1, 1, 2):
            of_z = (x + ring - z) % 4
            step = (of_z - z) % 4
            place = jnp.where(step == 3, 1, jnp.where(step == 1, 2, jnp.where(step == 2, 3, 0)))
            slots.append(jnp.where(of_y == y_hi, 0, 4) + place)
    where = jnp.stack(slots + [core]).astype(jnp.int32)
    core_at = jnp.stack([core]).astype(jnp.int32)

    def next_ctx(yl, x, c, yh, z):
        n = (yl * 4 + x) * 2 + c + 1
        return None if n == 16 else (n // 8, (n // 2) % 4, n % 2, yh, z)

    w, tail = together((in_weight.reshape(BLOCK, 3 * wide), tokens[rows - HALO:]))
    b = transposed(w)
    t = jnp.concatenate([send(tail, next_ctx), tokens], axis=0)
    t, b, where, core_at, fades, behind, plane, chip, *prms = together(
        (t, b, where, core_at, fades, behind, plane, chip, *prms)
    )
    tp_, tm, ty = along_z(t, 1), along_z(t, -1), other_yhi(t)
    bp, bm = along_x(b, 1), along_x(b, -1)
    t, b, tp_, tm, ty, bp, bm = together((t, b, tp_, tm, ty, bp, bm))
    typ, tym = along_z(ty, 1), along_z(ty, -1)
    cb, cbp, cbm = other_core(b), other_core(bp), other_core(bm)
    b, bp, cb, cbp, cbm = together((b, bp, cb, cbp, cbm))
    bf, a = along_x(bp, 1), other_ylo(b)
    t, b, tp_, tm, ty, bp, bm, typ, tym, bf, a, cb, cbp, cbm = together(
        (t, b, tp_, tm, ty, bp, bm, typ, tym, bf, a, cb, cbp, cbm)
    )
    tf, tyf = along_z(tp_, 1), along_z(tym, -1)
    ap = along_x(a, 1)
    cbf, ca = other_core(bf), other_core(a)
    bf, a, cbf, ca = together((bf, a, cbf, ca))
    am, af = along_x(a, -1), other_ylo(bf)
    lhs, part = begin(where, [t, tp_, tm, ty, typ, tym], [b, bp, bm, bf], rows)
    part_too = also(where, lhs, [cb, cbp, cbm, cbf], rows)
    lhs, part, part_too, ap, am, af, tf, tyf = together(
        (lhs, part, part_too, ap, am, af, tf, tyf)
    )
    mine = [b, bp, bm, bf, a, ap, am, af]
    theirs = [cb, cbp, cbm, cbf, ca] + [other_core(w) for w in (ap, am, af)]

    ys, xs, us, ends = [], [], [], []
    for o, (weights, done) in enumerate(((mine, part), (theirs, part_too))):
        y, x1, u, end = project(where, lhs, tf, tyf, done, weights, prms[o], rows)
        ys.append(y)
        xs.append(x1)
        us.append(u)
        ends.append(end)

    total = jnp.concatenate(
        [jnp.where(core == 0, ends[0], ends[1]), jnp.where(core == 0, ends[1], ends[0])], axis=1
    )
    came = [total] + [along_x(total, m) for m in (1, 2, 3)]
    near = behind[0] * came[1] + behind[1] * came[2] + behind[2] * came[3]
    whole = plane[0] * came[0] + plane[1] * came[1] + plane[2] * came[2] + plane[3] * came[3]
    sent = other_core(jnp.where(core == 0, chip * near + total, near))
    state = [near, sent, other_ylo(whole), other_ylo_and_core(whole), fades]
    return gate(core_at, ys, xs, us, prms, state, rows)


def solution(mesh):
    placed = (P("ctx", "tp"), P("tp", None, "ctx"), P(), P(), P(), P())
    return jax.shard_map(
        on_device, mesh=mesh, in_specs=placed, out_specs=P("ctx", "tp"), check_vma=False
    )
```

```python
import functools

import jax
import jax.numpy as jnp
from jax import lax
from jax.experimental import pallas as pl
from jax.experimental.pallas import tpu as pltpu
from jax.sharding import PartitionSpec as P

D = 4096
MODES = 16
BLOCK = 512
SEG = 8
HALO = 16
SIZES = (2, 4, 2, 2, 4)
LANES = 128
F32 = jnp.float32


def route(move):
    pairs = []
    for yl in range(2):
        for x in range(4):
            for c in range(2):
                for yh in range(2):
                    for z in range(4):
                        to = move(yl, x, c, yh, z)
                        if to is None:
                            continue
                        a, b, e, f, g = to
                        pairs.append(
                            (
                                ((yl * 4 + x) * 2 + c) * 8 + yh * 4 + z,
                                (((a % 2) * 4 + b % 4) * 2 + e % 2) * 8 + (f % 2) * 4 + g % 4,
                            )
                        )
    return pairs


def send(value, move):
    return lax.ppermute(value, ("ctx", "tp"), route(move))


def along_z(value, step):
    return send(value, lambda yl, x, c, yh, z: (yl, x, c, yh, z + step))


def along_x(value, step):
    return send(value, lambda yl, x, c, yh, z: (yl, x + step, c, yh, z))


def other_core(value):
    return send(value, lambda yl, x, c, yh, z: (yl, x, c + 1, yh, z))


def other_yhi(value):
    return send(value, lambda yl, x, c, yh, z: (yl, x, c, yh + 1, z))


def other_ylo(value):
    return send(value, lambda yl, x, c, yh, z: (yl + 1, x, c, yh, z))


def other_ylo_and_core(value):
    return send(value, lambda yl, x, c, yh, z: (yl + 1, x, c + 1, yh, z))


def transposed(value):
    return send(value, lambda yl, x, c, yh, z: (yh, x + z, c, yl, x))


together = lax.optimization_barrier


def shift_down(value, steps):
    rows = lax.broadcasted_iota(jnp.int32, value.shape, 0)
    return jnp.where(rows >= steps, pltpu.roll(value, steps, 0), 0.0)


def row_tiles(rows, body):
    tile = (rows + HALO) // 5

    def step(m, carry):
        body(pl.ds(pl.multiple_of(m * tile, 16), tile))
        return carry

    lax.fori_loop(0, 5, step, 0)


def copy_rows(rows, target, source):
    def body(at):
        target[at, :] = source[at, :]

    row_tiles(rows, body)


def first_half(rows, where, lhs, weights, acc):
    def clear(at):
        acc[at, :] = jnp.zeros((at.size, acc.shape[1]), F32)

    row_tiles(rows, clear)
    for k in range(4):
        slot = where[k]

        @pl.when(lax.rem(slot, 4) != 3)
        def _(k=k, slot=slot):
            def body(at):
                acc[at, :] += jnp.dot(lhs[slot, at, :], weights[k][...], preferred_element_type=F32)

            row_tiles(rows, body)


def begin_kernel(rows, where, *refs):
    toks, weights, (lhs, acc) = refs[:6], refs[6:10], refs[10:]
    for n, s in enumerate((0, 1, 2, 4, 5, 6)):
        copy_rows(rows, lhs.at[s], toks[n])
    first_half(rows, where, lhs, weights, acc)


def also_kernel(rows, where, *refs):
    lhs, weights, acc = refs[0], refs[1:5], refs[5]
    first_half(rows, where, lhs, weights, acc)


def begin(where, toks, weights, rows):
    vmem = pl.BlockSpec(memory_space=pltpu.VMEM)
    tall, width = rows + HALO, weights[0].shape[1]
    return pl.pallas_call(
        functools.partial(begin_kernel, rows),
        out_shape=[
            jax.ShapeDtypeStruct((8, tall, BLOCK), jnp.bfloat16),
            jax.ShapeDtypeStruct((tall, width), F32),
        ],
        in_specs=[pl.BlockSpec(memory_space=pltpu.SMEM)] + [vmem] * 10,
        out_specs=[vmem] * 2,
        compiler_params=pltpu.CompilerParams(vmem_limit_bytes=26 << 20),
        cost_estimate=pl.CostEstimate(
            flops=2 * tall * 3 * BLOCK * width, bytes_accessed=12 << 20, transcendentals=0
        ),
    )(where, *toks, *weights)


def also(where, lhs, weights, rows):
    vmem = pl.BlockSpec(memory_space=pltpu.VMEM)
    tall, width = rows + HALO, weights[0].shape[1]
    return pl.pallas_call(
        functools.partial(also_kernel, rows),
        out_shape=jax.ShapeDtypeStruct((tall, width), F32),
        in_specs=[pl.BlockSpec(memory_space=pltpu.SMEM)] + [vmem] * 5,
        out_specs=vmem,
        compiler_params=pltpu.CompilerParams(vmem_limit_bytes=26 << 20),
        cost_estimate=pl.CostEstimate(
            flops=2 * tall * 3 * BLOCK * width, bytes_accessed=12 << 20, transcendentals=0
        ),
    )(where, lhs, *weights)


def more_kernel(rows, where, *refs):
    lhs, part, weights, acc = refs[0], refs[1], refs[2:6], refs[6]
    copy_rows(rows, acc, part)
    for k in range(4):
        slot = where[4 + k]

        @pl.when(lax.rem(slot, 4) != 3)
        def _(k=k, slot=slot):
            def body(at):
                acc[at, :] += jnp.dot(lhs[slot, at, :], weights[k][...], preferred_element_type=F32)

            row_tiles(rows, body)


def more(where, lhs, part, weights, rows):
    vmem = pl.BlockSpec(memory_space=pltpu.VMEM)
    tall, width = rows + HALO, weights[0].shape[1]
    return pl.pallas_call(
        functools.partial(more_kernel, rows),
        out_shape=jax.ShapeDtypeStruct((tall, width), F32),
        in_specs=[pl.BlockSpec(memory_space=pltpu.SMEM)] + [vmem] * 6,
        out_specs=vmem,
        compiler_params=pltpu.CompilerParams(vmem_limit_bytes=26 << 20),
        cost_estimate=pl.CostEstimate(
            flops=2 * tall * 3 * BLOCK * width, bytes_accessed=12 << 20, transcendentals=0
        ),
    )(where, lhs, part, *weights)


def project_kernel(rows, where, *refs):
    near, far, part, *refs = refs
    weights, refs = refs[:8], refs[8:]
    prm, prod_ref, x1_ref, u_ref, end_ref, acc, proj = refs
    seg_len = rows // SEG
    for k in range(8):
        for s, ref in ((3, near), (7, far)):

            @pl.when(where[k] == s)
            def _(k=k, ref=ref):
                def body(at):
                    out = jnp.dot(ref[at, :], weights[k][...], preferred_element_type=F32)
                    if k < 4:
                        acc[at, :] = part[at, :] + out
                        return
                    out = (acc[at, :] + out).astype(jnp.bfloat16).astype(F32)
                    for n in range(6):
                        proj[n, at, :] = out[:, n * LANES:(n + 1) * LANES]

                row_tiles(rows, body)

    for q in range(2):
        lanes = pl.ds(q * LANES, LANES)
        bcast = lambda r: jnp.broadcast_to(prm[pl.ds(r, 1), lanes], (SEG, LANES))
        decay = [bcast(k) for k in range(MODES)]
        taps = [[bcast(2 * MODES + 3 * j + g) for g in range(3)] for j in range(3)]

        def load(g, at):
            return proj[2 * g + q, pl.ds(at, SEG, stride=seg_len), :]

        def step(i, carry):
            before, last, states = carry
            now = [load(g, HALO + i) for g in range(3)]
            feat = [
                taps[0][g] * now[g] + taps[1][g] * last[g] + taps[2][g] * before[g]
                for g in range(3)
            ]
            product = feat[1] * feat[2]
            at = pl.ds(pl.multiple_of(i * SEG, SEG), SEG)
            prod_ref[at, lanes] = product
            x1_ref[at, lanes] = feat[0]
            return (last, now, [decay[k] * states[k] + product for k in range(MODES)])

        zero = jnp.zeros((SEG, LANES), F32)
        first = ([load(g, HALO - 2) for g in range(3)], [load(g, HALO - 1) for g in range(3)])
        _, _, states = lax.fori_loop(0, seg_len, step, (*first, [zero] * MODES), unroll=4)
        for k in range(MODES):
            rate = prm[pl.ds(48 + k, 1), lanes]
            u = states[k]
            for n in (1, 2, 4):
                u = u + jnp.exp(-rate * (float(n) * seg_len)) * shift_down(u, n)
            u_ref[pl.ds(k * SEG, SEG), lanes] = u
            end_ref[pl.ds(k, 1), lanes] = u[SEG - 1:]


def project(where, near, far, part, weights, prm, rows):
    vmem = pl.BlockSpec(memory_space=pltpu.VMEM)
    wide, tall = 2 * LANES, rows + HALO
    return pl.pallas_call(
        functools.partial(project_kernel, rows),
        out_shape=[
            jax.ShapeDtypeStruct((rows, wide), F32),
            jax.ShapeDtypeStruct((rows, wide), F32),
            jax.ShapeDtypeStruct((MODES * SEG, wide), F32),
            jax.ShapeDtypeStruct((MODES, wide), F32),
        ],
        in_specs=[pl.BlockSpec(memory_space=pltpu.SMEM)] + [vmem] * 12,
        out_specs=[vmem] * 4,
        scratch_shapes=[
            pltpu.VMEM((tall, 3 * wide), F32),
            pltpu.VMEM((6, tall, LANES), F32),
        ],
        compiler_params=pltpu.CompilerParams(vmem_limit_bytes=26 << 20),
        cost_estimate=pl.CostEstimate(
            flops=2 * tall * 4 * BLOCK * 3 * wide, bytes_accessed=12 << 20, transcendentals=0
        ),
    )(where, near, far, part, *weights, prm)


def read_kernel(rows, prod_ref, u_ref, prm, y_ref):
    seg_len = rows // SEG
    for q in range(2):
        lanes = pl.ds(q * LANES, LANES)
        bcast = lambda r: jnp.broadcast_to(prm[pl.ds(r, 1), lanes], (SEG, LANES))
        decay = [bcast(k) for k in range(MODES)]
        amp = [bcast(MODES + k) for k in range(MODES)]
        gain = bcast(2 * MODES + 9)

        def step(i, states):
            at = pl.ds(pl.multiple_of(i * SEG, SEG), SEG)
            product = prod_ref[at, lanes]
            states = [decay[k] * states[k] + product for k in range(MODES)]
            terms = [amp[k] * states[k] for k in range(MODES)] + [gain * product]
            while len(terms) > 1:
                terms = [a + b for a, b in zip(terms[::2], terms[1::2])] + (
                    [terms[-1]] if len(terms) % 2 else []
                )
            y_ref[at, lanes] = terms[0]
            return states

        start = [shift_down(u_ref[pl.ds(k * SEG, SEG), lanes], 1) for k in range(MODES)]
        lax.fori_loop(0, seg_len, step, start, unroll=4)


def read(prod, u, prm, rows):
    vmem = pl.BlockSpec(memory_space=pltpu.VMEM)
    return pl.pallas_call(
        functools.partial(read_kernel, rows),
        out_shape=jax.ShapeDtypeStruct(prod.shape, F32),
        in_specs=[vmem] * 3,
        out_specs=vmem,
        compiler_params=pltpu.CompilerParams(vmem_limit_bytes=12 << 20),
        cost_estimate=pl.CostEstimate(
            flops=4 * MODES * prod.size, bytes_accessed=12 << 20, transcendentals=0
        ),
    )(prod, u, prm)


def gate_kernel(rows, core_ref, y0, y1, x0, x1, p0, p1, near, sent, same, cross, fades,
                out_ref, ybuf, xbuf, wide, sem):
    seg_len = rows // SEG
    core = core_ref[0]
    copies = []
    for o, (y, x) in enumerate(((y0, x0), (y1, x1))):
        copies.append(
            (
                pltpu.make_async_copy(y, ybuf.at[o], sem.at[2 * o]),
                pltpu.make_async_copy(x, xbuf.at[o], sem.at[2 * o + 1]),
            )
        )
        for copy in copies[o]:
            copy.start()
    seg = lax.broadcasted_iota(jnp.int32, (SEG, LANES), 0).astype(F32) * seg_len
    for o, prm in enumerate((p0, p1)):
        base = lax.rem(core + o, 2) * (2 * LANES)
        for q in range(2):
            lanes = pl.ds(q * LANES, LANES)
            to = pl.ds(pl.multiple_of(base + q * LANES, LANES), LANES)
            shard, straight, across = (
                fades[pl.ds(n * MODES, MODES), to] for n in range(3)
            )
            state = (
                shard * near[:, to] + sent[:, to] + straight * same[:, to] + across * cross[:, to]
            )
            decay, carried = [], []
            for k in range(MODES):
                d = jnp.broadcast_to(prm[pl.ds(k, 1), lanes], (SEG, LANES))
                rate = prm[pl.ds(48 + k, 1), lanes]
                start = jnp.exp(-rate * seg) * state[k:k + 1]
                decay.append(d)
                carried.append(prm[pl.ds(MODES + k, 1), lanes] * d * start)
            if q == 0:
                for copy in copies[o]:
                    copy.wait()

            def step(i, carried):
                terms = list(carried)
                while len(terms) > 1:
                    terms = [a + b for a, b in zip(terms[::2], terms[1::2])]
                at = pl.ds(pl.multiple_of(i * SEG, SEG), SEG)
                wide[pl.ds(i, SEG, stride=seg_len), :] = xbuf[o, at, lanes] * (
                    ybuf[o, at, lanes] + terms[0]
                )
                return [c * d for c, d in zip(carried, decay)]

            lax.fori_loop(0, seg_len, step, carried, unroll=4)
            out_ref[:, to] = wide[...].astype(out_ref.dtype)


def gate(core, ys, xs, prms, state, rows):
    vmem = pl.BlockSpec(memory_space=pltpu.VMEM)
    anywhere = pl.BlockSpec(memory_space=pl.ANY)
    wide = 2 * LANES
    return pl.pallas_call(
        functools.partial(gate_kernel, rows),
        out_shape=jax.ShapeDtypeStruct((rows, BLOCK), jnp.bfloat16),
        in_specs=[pl.BlockSpec(memory_space=pltpu.SMEM)] + [anywhere] * 4 + [vmem] * 7,
        out_specs=vmem,
        scratch_shapes=[
            pltpu.VMEM((2, rows, wide), F32),
            pltpu.VMEM((2, rows, wide), F32),
            pltpu.VMEM((rows, LANES), F32),
            pltpu.SemaphoreType.DMA((4,)),
        ],
        compiler_params=pltpu.CompilerParams(vmem_limit_bytes=20 << 20),
    )(core, *ys, *xs, *prms, *state)


def on_device(tokens, in_weight, short_filter, filter_residues, filter_rates, skip_gain):
    rows = tokens.shape[0]
    ctx, tp = lax.axis_index("ctx"), lax.axis_index("tp")
    y_lo, x, core = ctx // 8, (ctx // 2) % 4, ctx % 2
    y_hi, z = tp // 4, tp % 4
    wide = 2 * LANES

    base = tp * BLOCK
    rates = lax.dynamic_slice_in_dim(filter_rates, base, BLOCK, 0).T
    amps = lax.dynamic_slice_in_dim(filter_residues, base, BLOCK, 0).T * jnp.sqrt(rates)
    taps = lax.dynamic_slice_in_dim(short_filter, base, BLOCK, 2).reshape(9, BLOCK)
    gains = lax.dynamic_slice_in_dim(skip_gain, base, BLOCK, 0)[None]
    prm = jnp.concatenate(
        [jnp.exp(-rates), amps, taps, gains, jnp.zeros((6, BLOCK), F32), rates], axis=0
    )
    prms = [lax.dynamic_slice_in_dim(prm, (core + o) % 2 * wide, wide, 1) for o in range(2)]

    def fade(steps):
        return jnp.exp(-rates * jnp.asarray(steps).astype(F32))

    shard = fade(rows)
    behind = [jnp.where(x >= m, fade(2 * rows * (m - 1)), 0.0) for m in (1, 2, 3)]
    plane = [fade(2 * rows * (3 - (x - m) % 4)) for m in range(4)]
    chip = fade(2 * rows)
    lower = jnp.where(y_lo == 1, fade(2 * rows * x), 0.0)
    straight = lower * shard
    across = lower * jnp.where(core == 0, 1.0, shard * shard)
    fades = jnp.concatenate([shard, straight, across], axis=0)
    behind, plane = jnp.stack(behind), jnp.stack(plane)

    slots = []
    for of_y in (y_lo, 1 - y_lo):
        for ring in (0, -1, 1, 2):
            of_z = (x + ring - z) % 4
            step = (of_z - z) % 4
            place = jnp.where(step == 3, 1, jnp.where(step == 1, 2, jnp.where(step == 2, 3, 0)))
            slots.append(jnp.where(of_y == y_hi, 0, 4) + place)
    where = jnp.stack(slots + [core]).astype(jnp.int32)
    core_at = jnp.stack([core]).astype(jnp.int32)

    def next_ctx(yl, x, c, yh, z):
        n = (yl * 4 + x) * 2 + c + 1
        return None if n == 16 else (n // 8, (n // 2) % 4, n % 2, yh, z)

    w, tail = together((in_weight.reshape(BLOCK, 3 * wide), tokens[rows - HALO:]))
    b = transposed(w)
    t = jnp.concatenate([send(tail, next_ctx), tokens], axis=0)
    t, b, where, core_at, fades, behind, plane, chip, *prms = together(
        (t, b, where, core_at, fades, behind, plane, chip, *prms)
    )
    ty = other_yhi(t)
    tp_, tm = along_z(t, 1), along_z(t, -1)
    bp, bm = along_x(b, 1), along_x(b, -1)
    t, b, tp_, tm, ty, bp, bm = together((t, b, tp_, tm, ty, bp, bm))
    typ, tym = along_z(ty, 1), along_z(ty, -1)
    cb, cbp, cbm = other_core(b), other_core(bp), other_core(bm)
    b, bp, cb, cbp, cbm = together((b, bp, cb, cbp, cbm))
    bf, a = along_x(bp, 1), other_ylo(b)
    bf, a = together((bf, a))
    ap, am, af = along_x(a, 1), along_x(a, -1), other_ylo(bf)
    t, tp_, tm, ty, typ, tym, bf, a = together((t, tp_, tm, ty, typ, tym, bf, a))
    tf, tyf = along_z(tp_, 1), along_z(tym, -1)
    cbf, ca = other_core(bf), other_core(a)
    lhs, part = begin(where, [t, tp_, tm, ty, typ, tym], [b, bp, bm, bf], rows)
    part_too = also(where, lhs, [cb, cbp, cbm, cbf], rows)
    ap, am, af, part_too = together((ap, am, af, part_too))
    cap, cam, caf = other_core(ap), other_core(am), other_core(af)
    mine = [b, bp, bm, bf, a, ap, am, af]
    theirs = [cb, cbp, cbm, cbf, ca, cap, cam, caf]
    part = more(where, lhs, part, mine[4:], rows)
    part_too = more(where, lhs, part_too, theirs[4:], rows)
    tf, tyf, part, part_too = together((tf, tyf, part, part_too))

    products, xs, us, ends = [], [], [], []
    for o, (weights, done) in enumerate(((mine, part), (theirs, part_too))):
        product, x1, u, end = project(where, tf, tyf, done, weights, prms[o], rows)
        products.append(product)
        xs.append(x1)
        us.append(u)
        ends.append(end)

    total = jnp.concatenate(
        [jnp.where(core == 0, ends[0], ends[1]), jnp.where(core == 0, ends[1], ends[0])], axis=1
    )
    total, products[0] = together((total, products[0]))
    came = [total] + [along_x(total, m) for m in (1, 2, 3)]
    y0 = read(products[0], us[0], prms[0], rows)
    came, products[1], y0 = together((came, products[1], y0))
    total = came[0]
    near = behind[0] * came[1] + behind[1] * came[2] + behind[2] * came[3]
    whole = plane[0] * came[0] + plane[1] * came[1] + plane[2] * came[2] + plane[3] * came[3]
    sent = other_core(jnp.where(core == 0, chip * near + total, near))
    same, cross = other_ylo(whole), other_ylo_and_core(whole)
    y1 = read(products[1], us[1], prms[1], rows)
    return gate(core_at, [y0, y1], xs, prms, [near, sent, same, cross, fades], rows)


def solution(mesh):
    placed = (P("ctx", "tp"), P("tp", None, "ctx"), P(), P(), P(), P())
    return jax.shard_map(
        on_device, mesh=mesh, in_specs=placed, out_specs=P("ctx", "tp"), check_vma=False
    )
```

```python
import functools

import jax
import jax.numpy as jnp
from jax import lax
from jax.experimental import pallas as pl
from jax.experimental.pallas import tpu as pltpu
from jax.sharding import PartitionSpec as P

D = 4096
MODES = 16
BLOCK = 512
SEG = 8
HALO = 16
SIZES = (2, 4, 2, 2, 4)
LANES = 128
F32 = jnp.float32


def route(move):
    pairs = []
    for yl in range(2):
        for x in range(4):
            for c in range(2):
                for yh in range(2):
                    for z in range(4):
                        to = move(yl, x, c, yh, z)
                        if to is None:
                            continue
                        a, b, e, f, g = to
                        pairs.append(
                            (
                                ((yl * 4 + x) * 2 + c) * 8 + yh * 4 + z,
                                (((a % 2) * 4 + b % 4) * 2 + e % 2) * 8 + (f % 2) * 4 + g % 4,
                            )
                        )
    return pairs


def send(value, move):
    return lax.ppermute(value, ("ctx", "tp"), route(move))


def along_z(value, step):
    return send(value, lambda yl, x, c, yh, z: (yl, x, c, yh, z + step))


def along_x(value, step):
    return send(value, lambda yl, x, c, yh, z: (yl, x + step, c, yh, z))


def other_core(value):
    return send(value, lambda yl, x, c, yh, z: (yl, x, c + 1, yh, z))


def other_yhi(value):
    return send(value, lambda yl, x, c, yh, z: (yl, x, c, yh + 1, z))


def other_ylo(value):
    return send(value, lambda yl, x, c, yh, z: (yl + 1, x, c, yh, z))


def other_ylo_and_core(value):
    return send(value, lambda yl, x, c, yh, z: (yl + 1, x, c + 1, yh, z))


def transposed(value):
    return send(value, lambda yl, x, c, yh, z: (yh, x + z, c, yl, x))


together = lax.optimization_barrier


def shift_down(value, steps):
    rows = lax.broadcasted_iota(jnp.int32, value.shape, 0)
    return jnp.where(rows >= steps, pltpu.roll(value, steps, 0), 0.0)


def first_half(where, lhs, weights, acc):
    acc[...] = jnp.zeros_like(acc)
    for k in range(4):
        slot = where[k]

        @pl.when(lax.rem(slot, 4) != 3)
        def _(k=k, slot=slot):
            acc[...] += jnp.dot(lhs[slot], weights[k][...], preferred_element_type=F32)


def begin_kernel(where, *refs):
    toks, weights, (lhs, acc) = refs[:6], refs[6:10], refs[10:]
    for n, s in enumerate((0, 1, 2, 4, 5, 6)):
        lhs[s] = toks[n][...]
    first_half(where, lhs, weights, acc)


def also_kernel(where, *refs):
    lhs, weights, acc = refs[0], refs[1:5], refs[5]
    first_half(where, lhs, weights, acc)


def begin(where, toks, weights, rows):
    vmem = pl.BlockSpec(memory_space=pltpu.VMEM)
    tall, width = rows + HALO, weights[0].shape[1]
    return pl.pallas_call(
        begin_kernel,
        out_shape=[
            jax.ShapeDtypeStruct((8, tall, BLOCK), jnp.bfloat16),
            jax.ShapeDtypeStruct((tall, width), F32),
        ],
        in_specs=[pl.BlockSpec(memory_space=pltpu.SMEM)] + [vmem] * 10,
        out_specs=[vmem] * 2,
        compiler_params=pltpu.CompilerParams(vmem_limit_bytes=26 << 20),
        cost_estimate=pl.CostEstimate(
            flops=2 * tall * 3 * BLOCK * width, bytes_accessed=12 << 20, transcendentals=0
        ),
    )(where, *toks, *weights)


def also(where, lhs, weights, rows):
    vmem = pl.BlockSpec(memory_space=pltpu.VMEM)
    tall, width = rows + HALO, weights[0].shape[1]
    return pl.pallas_call(
        also_kernel,
        out_shape=jax.ShapeDtypeStruct((tall, width), F32),
        in_specs=[pl.BlockSpec(memory_space=pltpu.SMEM)] + [vmem] * 5,
        out_specs=vmem,
        compiler_params=pltpu.CompilerParams(vmem_limit_bytes=26 << 20),
        cost_estimate=pl.CostEstimate(
            flops=2 * tall * 3 * BLOCK * width, bytes_accessed=12 << 20, transcendentals=0
        ),
    )(where, lhs, *weights)


def project_kernel(rows, where, *refs):
    lhs, near, far, part, *refs = refs
    weights, refs = refs[:8], refs[8:]
    prm, prod_ref, x1_ref, u_ref, end_ref, last, wfar, proj = refs
    seg_len = rows // SEG
    for k in range(8):
        at = pl.ds(max(k - 3, 0) * BLOCK, BLOCK)
        for s, ref in ((3, near), (7, far)):

            @pl.when(where[k] == s)
            def _(k=k, ref=ref, at=at):
                last[:, at] = ref[...]
                if k < 4:
                    wfar[...] = weights[k][...]

        if k >= 4:

            @pl.when(lax.rem(where[k], 4) != 3)
            def _(k=k, at=at):
                last[:, at] = lhs[where[k]]

    for n in range(3):
        cols = pl.ds(n * 2 * LANES, 2 * LANES)
        right = jnp.concatenate([w[:, cols] for w in (wfar, *weights[4:])], axis=0)
        out = part[:, cols] + jnp.dot(last[...], right, preferred_element_type=F32)
        out = out.astype(jnp.bfloat16).astype(F32)
        for q in range(2):
            proj[2 * n + q] = out[:, q * LANES:(q + 1) * LANES]

    top = lax.broadcasted_iota(jnp.int32, (SEG, LANES), 0) == 0
    for q in range(2):
        lanes = pl.ds(q * LANES, LANES)
        bcast = lambda r: jnp.broadcast_to(prm[pl.ds(r, 1), lanes], (SEG, LANES))
        decay = [bcast(k) for k in range(MODES)]
        taps = [[bcast(2 * MODES + 3 * j + g) for g in range(3)] for j in range(3)]

        def load(g, i):
            return proj[2 * g + q, pl.ds(pl.multiple_of(HALO + i * SEG, SEG), SEG), :]

        def load_before(g, back):
            halo = proj[2 * g + q, pl.ds(HALO - back, 1), :]
            return jnp.where(top, halo, pltpu.roll(load(g, seg_len - back), 1, 0))

        def step(i, carry):
            before, last, states = carry
            now = [load(g, i) for g in range(3)]
            feat = [
                taps[0][g] * now[g] + taps[1][g] * last[g] + taps[2][g] * before[g]
                for g in range(3)
            ]
            product = feat[1] * feat[2]
            at = pl.ds(pl.multiple_of(i * SEG, SEG), SEG)
            prod_ref[at, lanes] = product
            x1_ref[at, lanes] = feat[0]
            return (last, now, [decay[k] * states[k] + product for k in range(MODES)])

        zero = jnp.zeros((SEG, LANES), F32)
        first = tuple([load_before(g, back) for g in range(3)] for back in (2, 1))
        _, _, states = lax.fori_loop(0, seg_len, step, (*first, [zero] * MODES), unroll=4)
        for k in range(MODES):
            rate = prm[pl.ds(48 + k, 1), lanes]
            u = states[k]
            for n in (1, 2, 4):
                u = u + jnp.exp(-rate * (float(n) * seg_len)) * shift_down(u, n)
            u_ref[pl.ds(k * SEG, SEG), lanes] = u
            end_ref[pl.ds(k, 1), lanes] = u[SEG - 1:]


def project(where, lhs, near, far, part, weights, prm, rows):
    vmem = pl.BlockSpec(memory_space=pltpu.VMEM)
    wide, tall = 2 * LANES, rows + HALO
    return pl.pallas_call(
        functools.partial(project_kernel, rows),
        out_shape=[
            jax.ShapeDtypeStruct((rows, wide), F32),
            jax.ShapeDtypeStruct((rows, wide), F32),
            jax.ShapeDtypeStruct((MODES * SEG, wide), F32),
            jax.ShapeDtypeStruct((MODES, wide), F32),
        ],
        in_specs=[pl.BlockSpec(memory_space=pltpu.SMEM)] + [vmem] * 13,
        out_specs=[vmem] * 4,
        scratch_shapes=[
            pltpu.VMEM((tall, 5 * BLOCK), jnp.bfloat16),
            pltpu.VMEM((BLOCK, 3 * wide), jnp.bfloat16),
            pltpu.VMEM((6, tall, LANES), F32),
        ],
        compiler_params=pltpu.CompilerParams(vmem_limit_bytes=26 << 20),
        cost_estimate=pl.CostEstimate(
            flops=2 * tall * 5 * BLOCK * 3 * wide, bytes_accessed=12 << 20, transcendentals=0
        ),
    )(where, lhs, near, far, part, *weights, prm)


def read_kernel(rows, prod_ref, u_ref, prm, y_ref):
    seg_len = rows // SEG
    for q in range(2):
        lanes = pl.ds(q * LANES, LANES)
        bcast = lambda r: jnp.broadcast_to(prm[pl.ds(r, 1), lanes], (SEG, LANES))
        decay = [bcast(k) for k in range(MODES)]
        amp = [bcast(MODES + k) for k in range(MODES)]
        gain = bcast(2 * MODES + 9)

        def step(i, states):
            at = pl.ds(pl.multiple_of(i * SEG, SEG), SEG)
            product = prod_ref[at, lanes]
            states = [decay[k] * states[k] + product for k in range(MODES)]
            terms = [amp[k] * states[k] for k in range(MODES)] + [gain * product]
            while len(terms) > 1:
                terms = [a + b for a, b in zip(terms[::2], terms[1::2])] + (
                    [terms[-1]] if len(terms) % 2 else []
                )
            y_ref[at, lanes] = terms[0]
            return states

        start = [shift_down(u_ref[pl.ds(k * SEG, SEG), lanes], 1) for k in range(MODES)]
        lax.fori_loop(0, seg_len, step, start, unroll=4)


def read(prod, u, prm, rows):
    vmem = pl.BlockSpec(memory_space=pltpu.VMEM)
    return pl.pallas_call(
        functools.partial(read_kernel, rows),
        out_shape=jax.ShapeDtypeStruct(prod.shape, F32),
        in_specs=[vmem] * 3,
        out_specs=vmem,
        compiler_params=pltpu.CompilerParams(vmem_limit_bytes=12 << 20),
        cost_estimate=pl.CostEstimate(
            flops=4 * MODES * prod.size, bytes_accessed=12 << 20, transcendentals=0
        ),
    )(prod, u, prm)


def gate_kernel(rows, core_ref, y0, y1, x0, x1, p0, p1, near, sent, same, cross, fades,
                out_ref, ybuf, xbuf, wide, sem):
    seg_len = rows // SEG
    core = core_ref[0]
    copies = []
    for o, (y, x) in enumerate(((y0, x0), (y1, x1))):
        copies.append(
            (
                pltpu.make_async_copy(y, ybuf.at[o], sem.at[2 * o]),
                pltpu.make_async_copy(x, xbuf.at[o], sem.at[2 * o + 1]),
            )
        )
        for copy in copies[o]:
            copy.start()
    seg = lax.broadcasted_iota(jnp.int32, (SEG, LANES), 0).astype(F32) * seg_len
    for o, prm in enumerate((p0, p1)):
        base = lax.rem(core + o, 2) * (2 * LANES)
        for q in range(2):
            lanes = pl.ds(q * LANES, LANES)
            to = pl.ds(pl.multiple_of(base + q * LANES, LANES), LANES)
            shard, straight, across = (
                fades[pl.ds(n * MODES, MODES), to] for n in range(3)
            )
            state = (
                shard * near[:, to] + sent[:, to] + straight * same[:, to] + across * cross[:, to]
            )
            decay, carried = [], []
            for k in range(MODES):
                d = jnp.broadcast_to(prm[pl.ds(k, 1), lanes], (SEG, LANES))
                rate = prm[pl.ds(48 + k, 1), lanes]
                start = jnp.exp(-rate * seg) * state[k:k + 1]
                decay.append(d)
                carried.append(prm[pl.ds(MODES + k, 1), lanes] * d * start)
            if q == 0:
                for copy in copies[o]:
                    copy.wait()

            def step(i, carried):
                terms = list(carried)
                while len(terms) > 1:
                    terms = [a + b for a, b in zip(terms[::2], terms[1::2])]
                at = pl.ds(pl.multiple_of(i * SEG, SEG), SEG)
                wide[pl.ds(i, SEG, stride=seg_len), :] = xbuf[o, at, lanes] * (
                    ybuf[o, at, lanes] + terms[0]
                )
                return [c * d for c, d in zip(carried, decay)]

            lax.fori_loop(0, seg_len, step, carried, unroll=4)
            out_ref[:, to] = wide[...].astype(out_ref.dtype)


def gate(core, ys, xs, prms, state, rows):
    vmem = pl.BlockSpec(memory_space=pltpu.VMEM)
    anywhere = pl.BlockSpec(memory_space=pl.ANY)
    wide = 2 * LANES
    return pl.pallas_call(
        functools.partial(gate_kernel, rows),
        out_shape=jax.ShapeDtypeStruct((rows, BLOCK), jnp.bfloat16),
        in_specs=[pl.BlockSpec(memory_space=pltpu.SMEM)] + [anywhere] * 4 + [vmem] * 7,
        out_specs=vmem,
        scratch_shapes=[
            pltpu.VMEM((2, rows, wide), F32),
            pltpu.VMEM((2, rows, wide), F32),
            pltpu.VMEM((rows, LANES), F32),
            pltpu.SemaphoreType.DMA((4,)),
        ],
        compiler_params=pltpu.CompilerParams(vmem_limit_bytes=20 << 20),
    )(core, *ys, *xs, *prms, *state)


def on_device(tokens, in_weight, short_filter, filter_residues, filter_rates, skip_gain):
    rows = tokens.shape[0]
    ctx, tp = lax.axis_index("ctx"), lax.axis_index("tp")
    y_lo, x, core = ctx // 8, (ctx // 2) % 4, ctx % 2
    y_hi, z = tp // 4, tp % 4
    wide = 2 * LANES

    base = tp * BLOCK
    rates = lax.dynamic_slice_in_dim(filter_rates, base, BLOCK, 0).T
    amps = lax.dynamic_slice_in_dim(filter_residues, base, BLOCK, 0).T * jnp.sqrt(rates)
    taps = lax.dynamic_slice_in_dim(short_filter, base, BLOCK, 2).reshape(9, BLOCK)
    gains = lax.dynamic_slice_in_dim(skip_gain, base, BLOCK, 0)[None]
    prm = jnp.concatenate(
        [jnp.exp(-rates), amps, taps, gains, jnp.zeros((6, BLOCK), F32), rates], axis=0
    )
    prms = [lax.dynamic_slice_in_dim(prm, (core + o) % 2 * wide, wide, 1) for o in range(2)]

    def fade(steps):
        return jnp.exp(-rates * jnp.asarray(steps).astype(F32))

    shard = fade(rows)
    behind = [jnp.where(x >= m, fade(2 * rows * (m - 1)), 0.0) for m in (1, 2, 3)]
    plane = [fade(2 * rows * (3 - (x - m) % 4)) for m in range(4)]
    chip = fade(2 * rows)
    lower = jnp.where(y_lo == 1, fade(2 * rows * x), 0.0)
    straight = lower * shard
    across = lower * jnp.where(core == 0, 1.0, shard * shard)
    fades = jnp.concatenate([shard, straight, across], axis=0)
    behind, plane = jnp.stack(behind), jnp.stack(plane)

    slots = []
    for of_y in (y_lo, 1 - y_lo):
        for ring in (0, -1, 1, 2):
            of_z = (x + ring - z) % 4
            step = (of_z - z) % 4
            place = jnp.where(step == 3, 1, jnp.where(step == 1, 2, jnp.where(step == 2, 3, 0)))
            slots.append(jnp.where(of_y == y_hi, 0, 4) + place)
    where = jnp.stack(slots + [core]).astype(jnp.int32)
    core_at = jnp.stack([core]).astype(jnp.int32)

    def next_ctx(yl, x, c, yh, z):
        n = (yl * 4 + x) * 2 + c + 1
        return None if n == 16 else (n // 8, (n // 2) % 4, n % 2, yh, z)

    w, tail = together((in_weight.reshape(BLOCK, 3 * wide), tokens[rows - HALO:]))
    b = transposed(w)
    steps = tokens.reshape(SEG, rows // SEG, BLOCK).transpose(1, 0, 2).reshape(rows, BLOCK)
    t = jnp.concatenate([send(tail, next_ctx), steps], axis=0)
    t, b, where, core_at, fades, behind, plane, chip, *prms = together(
        (t, b, where, core_at, fades, behind, plane, chip, *prms)
    )
    tp_, tm, ty = along_z(t, 1), along_z(t, -1), other_yhi(t)
    bp, bm = along_x(b, 1), along_x(b, -1)
    t, b, tp_, tm, ty, bp, bm = together((t, b, tp_, tm, ty, bp, bm))
    typ, tym = along_z(ty, 1), along_z(ty, -1)
    cb, cbp, cbm = other_core(b), other_core(bp), other_core(bm)
    b, bp, cb, cbp, cbm = together((b, bp, cb, cbp, cbm))
    bf, a = along_x(bp, 1), other_ylo(b)
    t, b, tp_, tm, ty, bp, bm, typ, tym, bf, a, cb, cbp, cbm = together(
        (t, b, tp_, tm, ty, bp, bm, typ, tym, bf, a, cb, cbp, cbm)
    )
    tf, tyf = along_z(tp_, 1), along_z(tym, -1)
    ap = along_x(a, 1)
    cbf, ca = other_core(bf), other_core(a)
    bf, a, cbf, ca = together((bf, a, cbf, ca))
    am, af = along_x(a, -1), other_ylo(bf)
    lhs, part = begin(where, [t, tp_, tm, ty, typ, tym], [b, bp, bm, bf], rows)
    part_too = also(where, lhs, [cb, cbp, cbm, cbf], rows)
    lhs, part, part_too, ap, am, af, tf, tyf = together(
        (lhs, part, part_too, ap, am, af, tf, tyf)
    )
    mine = [b, bp, bm, bf, a, ap, am, af]
    theirs = [cb, cbp, cbm, cbf, ca] + [other_core(w) for w in (ap, am, af)]

    products, xs, us, ends = [], [], [], []
    for o, (weights, done) in enumerate(((mine, part), (theirs, part_too))):
        product, x1, u, end = project(where, lhs, tf, tyf, done, weights, prms[o], rows)
        products.append(product)
        xs.append(x1)
        us.append(u)
        ends.append(end)

    total = jnp.concatenate(
        [jnp.where(core == 0, ends[0], ends[1]), jnp.where(core == 0, ends[1], ends[0])], axis=1
    )
    total, products[0] = together((total, products[0]))
    came = [total] + [along_x(total, m) for m in (1, 2, 3)]
    y0 = read(products[0], us[0], prms[0], rows)
    came, products[1], y0 = together((came, products[1], y0))
    total = came[0]
    near = behind[0] * came[1] + behind[1] * came[2] + behind[2] * came[3]
    whole = plane[0] * came[0] + plane[1] * came[1] + plane[2] * came[2] + plane[3] * came[3]
    sent = other_core(jnp.where(core == 0, chip * near + total, near))
    same, cross = other_ylo(whole), other_ylo_and_core(whole)
    y1 = read(products[1], us[1], prms[1], rows)
    return gate(core_at, [y0, y1], xs, prms, [near, sent, same, cross, fades], rows)


def solution(mesh):
    placed = (P("ctx", "tp"), P("tp", None, "ctx"), P(), P(), P(), P())
    return jax.shard_map(
        on_device, mesh=mesh, in_specs=placed, out_specs=P("ctx", "tp"), check_vma=False
    )
```

```python
import functools

import jax
import jax.numpy as jnp
from jax import lax
from jax.experimental import pallas as pl
from jax.experimental.pallas import tpu as pltpu
from jax.sharding import PartitionSpec as P

D = 4096
MODES = 16
BLOCK = 512
SEG = 8
HALO = 16
SIZES = (2, 4, 2, 2, 4)
LANES = 128
F32 = jnp.float32


def route(move):
    pairs = []
    for yl in range(2):
        for x in range(4):
            for c in range(2):
                for yh in range(2):
                    for z in range(4):
                        to = move(yl, x, c, yh, z)
                        if to is None:
                            continue
                        a, b, e, f, g = to
                        pairs.append(
                            (
                                ((yl * 4 + x) * 2 + c) * 8 + yh * 4 + z,
                                (((a % 2) * 4 + b % 4) * 2 + e % 2) * 8 + (f % 2) * 4 + g % 4,
                            )
                        )
    return pairs


def send(value, move):
    return lax.ppermute(value, ("ctx", "tp"), route(move))


def along_z(value, step):
    return send(value, lambda yl, x, c, yh, z: (yl, x, c, yh, z + step))


def along_x(value, step):
    return send(value, lambda yl, x, c, yh, z: (yl, x + step, c, yh, z))


def other_core(value):
    return send(value, lambda yl, x, c, yh, z: (yl, x, c + 1, yh, z))


def other_yhi(value):
    return send(value, lambda yl, x, c, yh, z: (yl, x, c, yh + 1, z))


def other_ylo(value):
    return send(value, lambda yl, x, c, yh, z: (yl + 1, x, c, yh, z))


def other_ylo_and_core(value):
    return send(value, lambda yl, x, c, yh, z: (yl + 1, x, c + 1, yh, z))


def transposed(value):
    return send(value, lambda yl, x, c, yh, z: (yh, x + z, c, yl, x))


together = lax.optimization_barrier


def shift_down(value, steps):
    rows = lax.broadcasted_iota(jnp.int32, value.shape, 0)
    return jnp.where(rows >= steps, pltpu.roll(value, steps, 0), 0.0)


def first_half(where, lhs, weights, acc):
    acc[...] = jnp.zeros_like(acc)
    for k in range(4):
        slot = where[k]

        @pl.when(lax.rem(slot, 4) != 3)
        def _(k=k, slot=slot):
            acc[...] += jnp.dot(lhs[slot], weights[k][...], preferred_element_type=F32)


def begin_kernel(where, *refs):
    toks, weights, (lhs, acc) = refs[:6], refs[6:10], refs[10:]
    for n, s in enumerate((0, 1, 2, 4, 5, 6)):
        lhs[s] = toks[n][...]
    first_half(where, lhs, weights, acc)


def also_kernel(where, *refs):
    lhs, weights, acc = refs[0], refs[1:5], refs[5]
    first_half(where, lhs, weights, acc)


def begin(where, toks, weights, rows):
    vmem = pl.BlockSpec(memory_space=pltpu.VMEM)
    tall, width = rows + HALO, weights[0].shape[1]
    return pl.pallas_call(
        begin_kernel,
        out_shape=[
            jax.ShapeDtypeStruct((8, tall, BLOCK), jnp.bfloat16),
            jax.ShapeDtypeStruct((tall, width), F32),
        ],
        in_specs=[pl.BlockSpec(memory_space=pltpu.SMEM)] + [vmem] * 10,
        out_specs=[vmem] * 2,
        compiler_params=pltpu.CompilerParams(vmem_limit_bytes=26 << 20),
        cost_estimate=pl.CostEstimate(
            flops=2 * tall * 3 * BLOCK * width, bytes_accessed=12 << 20, transcendentals=0
        ),
    )(where, *toks, *weights)


def also(where, lhs, weights, rows):
    vmem = pl.BlockSpec(memory_space=pltpu.VMEM)
    tall, width = rows + HALO, weights[0].shape[1]
    return pl.pallas_call(
        also_kernel,
        out_shape=jax.ShapeDtypeStruct((tall, width), F32),
        in_specs=[pl.BlockSpec(memory_space=pltpu.SMEM)] + [vmem] * 5,
        out_specs=vmem,
        compiler_params=pltpu.CompilerParams(vmem_limit_bytes=26 << 20),
        cost_estimate=pl.CostEstimate(
            flops=2 * tall * 3 * BLOCK * width, bytes_accessed=12 << 20, transcendentals=0
        ),
    )(where, lhs, *weights)


def project_kernel(rows, where, *refs):
    lhs, near, far, part, *refs = refs
    weights, refs = refs[:8], refs[8:]
    prm, prod_ref, x1_ref, u_ref, end_ref, last, wfar, proj = refs
    seg_len = rows // SEG
    for k in range(8):
        at = pl.ds(max(k - 3, 0) * BLOCK, BLOCK)
        for s, ref in ((3, near), (7, far)):

            @pl.when(where[k] == s)
            def _(k=k, ref=ref, at=at):
                last[:, at] = ref[...]
                if k < 4:
                    wfar[...] = weights[k][...]

        if k >= 4:

            @pl.when(lax.rem(where[k], 4) != 3)
            def _(k=k, at=at):
                last[:, at] = lhs[where[k]]

    for n in range(3):
        cols = pl.ds(n * 2 * LANES, 2 * LANES)
        right = jnp.concatenate([w[:, cols] for w in (wfar, *weights[4:])], axis=0)
        out = part[:, cols] + jnp.dot(last[...], right, preferred_element_type=F32)
        out = out.astype(jnp.bfloat16).astype(F32)
        for q in range(2):
            proj[2 * n + q] = out[:, q * LANES:(q + 1) * LANES]

    top = lax.broadcasted_iota(jnp.int32, (SEG, LANES), 0) == 0
    for q in range(2):
        lanes = pl.ds(q * LANES, LANES)
        bcast = lambda r: jnp.broadcast_to(prm[pl.ds(r, 1), lanes], (SEG, LANES))
        decay = [bcast(k) for k in range(MODES)]
        taps = [[bcast(2 * MODES + 3 * j + g) for g in range(3)] for j in range(3)]

        def load(g, i):
            return proj[2 * g + q, pl.ds(pl.multiple_of(HALO + i * SEG, SEG), SEG), :]

        def load_before(g, back):
            halo = proj[2 * g + q, pl.ds(HALO - back, 1), :]
            return jnp.where(top, halo, pltpu.roll(load(g, seg_len - back), 1, 0))

        def step(i, carry):
            before, last, states = carry
            now = [load(g, i) for g in range(3)]
            feat = [
                taps[0][g] * now[g] + taps[1][g] * last[g] + taps[2][g] * before[g]
                for g in range(3)
            ]
            product = feat[1] * feat[2]
            at = pl.ds(pl.multiple_of(i * SEG, SEG), SEG)
            prod_ref[at, lanes] = product
            x1_ref[at, lanes] = feat[0]
            return (last, now, [decay[k] * states[k] + product for k in range(MODES)])

        zero = jnp.zeros((SEG, LANES), F32)
        first = tuple([load_before(g, back) for g in range(3)] for back in (2, 1))
        _, _, states = lax.fori_loop(0, seg_len, step, (*first, [zero] * MODES), unroll=4)
        for k in range(MODES):
            rate = prm[pl.ds(48 + k, 1), lanes]
            u = states[k]
            for n in (1, 2, 4):
                u = u + jnp.exp(-rate * (float(n) * seg_len)) * shift_down(u, n)
            u_ref[pl.ds(k * SEG, SEG), lanes] = u
            end_ref[pl.ds(k, 1), lanes] = u[SEG - 1:]


def project(where, lhs, near, far, part, weights, prm, rows):
    vmem = pl.BlockSpec(memory_space=pltpu.VMEM)
    wide, tall = 2 * LANES, rows + HALO
    return pl.pallas_call(
        functools.partial(project_kernel, rows),
        out_shape=[
            jax.ShapeDtypeStruct((rows, wide), F32),
            jax.ShapeDtypeStruct((rows, wide), F32),
            jax.ShapeDtypeStruct((MODES * SEG, wide), F32),
            jax.ShapeDtypeStruct((MODES, wide), F32),
        ],
        in_specs=[pl.BlockSpec(memory_space=pltpu.SMEM)] + [vmem] * 13,
        out_specs=[vmem] * 4,
        scratch_shapes=[
            pltpu.VMEM((tall, 5 * BLOCK), jnp.bfloat16),
            pltpu.VMEM((BLOCK, 3 * wide), jnp.bfloat16),
            pltpu.VMEM((6, tall, LANES), F32),
        ],
        compiler_params=pltpu.CompilerParams(vmem_limit_bytes=26 << 20),
        cost_estimate=pl.CostEstimate(
            flops=2 * tall * 5 * BLOCK * 3 * wide, bytes_accessed=12 << 20, transcendentals=0
        ),
    )(where, lhs, near, far, part, *weights, prm)


def read_kernel(rows, prod_ref, u_ref, prm, y_ref):
    seg_len = rows // SEG
    for q in range(2):
        lanes = pl.ds(q * LANES, LANES)
        bcast = lambda r: jnp.broadcast_to(prm[pl.ds(r, 1), lanes], (SEG, LANES))
        decay = [bcast(k) for k in range(MODES)]
        amp = [bcast(MODES + k) for k in range(MODES)]
        gain = bcast(2 * MODES + 9)

        def step(i, states):
            at = pl.ds(pl.multiple_of(i * SEG, SEG), SEG)
            product = prod_ref[at, lanes]
            states = [decay[k] * states[k] + product for k in range(MODES)]
            terms = [amp[k] * states[k] for k in range(MODES)] + [gain * product]
            while len(terms) > 1:
                terms = [a + b for a, b in zip(terms[::2], terms[1::2])] + (
                    [terms[-1]] if len(terms) % 2 else []
                )
            y_ref[at, lanes] = terms[0]
            return states

        start = [shift_down(u_ref[pl.ds(k * SEG, SEG), lanes], 1) for k in range(MODES)]
        lax.fori_loop(0, seg_len, step, start, unroll=4)


def read(prod, u, prm, rows):
    vmem = pl.BlockSpec(memory_space=pltpu.VMEM)
    return pl.pallas_call(
        functools.partial(read_kernel, rows),
        out_shape=jax.ShapeDtypeStruct(prod.shape, F32),
        in_specs=[vmem] * 3,
        out_specs=vmem,
        compiler_params=pltpu.CompilerParams(vmem_limit_bytes=12 << 20),
        cost_estimate=pl.CostEstimate(
            flops=4 * MODES * prod.size, bytes_accessed=12 << 20, transcendentals=0
        ),
    )(prod, u, prm)


def gate_kernel(rows, core_ref, y0, y1, x0, x1, p0, p1, near, sent, same, cross, fades, out_ref, wide):
    seg_len = rows // SEG
    core = core_ref[0]
    seg = lax.broadcasted_iota(jnp.int32, (SEG, LANES), 0).astype(F32) * seg_len
    for o, (y, x, prm) in enumerate(((y0, x0, p0), (y1, x1, p1))):
        base = lax.rem(core + o, 2) * (2 * LANES)
        for q in range(2):
            lanes = pl.ds(q * LANES, LANES)
            to = pl.ds(pl.multiple_of(base + q * LANES, LANES), LANES)
            shard, straight, across = (
                fades[pl.ds(n * MODES, MODES), to] for n in range(3)
            )
            state = (
                shard * near[:, to] + sent[:, to] + straight * same[:, to] + across * cross[:, to]
            )
            decay, carried = [], []
            for k in range(MODES):
                d = jnp.broadcast_to(prm[pl.ds(k, 1), lanes], (SEG, LANES))
                rate = prm[pl.ds(48 + k, 1), lanes]
                start = jnp.exp(-rate * seg) * state[k:k + 1]
                decay.append(d)
                carried.append(prm[pl.ds(MODES + k, 1), lanes] * d * start)

            def step(i, carried):
                terms = list(carried)
                while len(terms) > 1:
                    terms = [a + b for a, b in zip(terms[::2], terms[1::2])]
                at = pl.ds(pl.multiple_of(i * SEG, SEG), SEG)
                wide[pl.ds(i, SEG, stride=seg_len), :] = x[at, lanes] * (
                    y[at, lanes] + terms[0]
                )
                return [c * d for c, d in zip(carried, decay)]

            lax.fori_loop(0, seg_len, step, carried, unroll=4)
            out_ref[:, to] = wide[...].astype(out_ref.dtype)


def gate(core, ys, xs, prms, state, rows):
    vmem = pl.BlockSpec(memory_space=pltpu.VMEM)
    return pl.pallas_call(
        functools.partial(gate_kernel, rows),
        out_shape=jax.ShapeDtypeStruct((rows, BLOCK), jnp.bfloat16),
        in_specs=[pl.BlockSpec(memory_space=pltpu.SMEM)] + [vmem] * 11,
        out_specs=vmem,
        scratch_shapes=[pltpu.VMEM((rows, LANES), F32)],
        compiler_params=pltpu.CompilerParams(vmem_limit_bytes=20 << 20),
    )(core, *ys, *xs, *prms, *state)


def on_device(tokens, in_weight, short_filter, filter_residues, filter_rates, skip_gain):
    rows = tokens.shape[0]
    ctx, tp = lax.axis_index("ctx"), lax.axis_index("tp")
    y_lo, x, core = ctx // 8, (ctx // 2) % 4, ctx % 2
    y_hi, z = tp // 4, tp % 4
    wide = 2 * LANES

    base = tp * BLOCK
    rates = lax.dynamic_slice_in_dim(filter_rates, base, BLOCK, 0).T
    amps = lax.dynamic_slice_in_dim(filter_residues, base, BLOCK, 0).T * jnp.sqrt(rates)
    taps = lax.dynamic_slice_in_dim(short_filter, base, BLOCK, 2).reshape(9, BLOCK)
    gains = lax.dynamic_slice_in_dim(skip_gain, base, BLOCK, 0)[None]
    prm = jnp.concatenate(
        [jnp.exp(-rates), amps, taps, gains, jnp.zeros((6, BLOCK), F32), rates], axis=0
    )
    prms = [lax.dynamic_slice_in_dim(prm, (core + o) % 2 * wide, wide, 1) for o in range(2)]

    def fade(steps):
        return jnp.exp(-rates * jnp.asarray(steps).astype(F32))

    shard = fade(rows)
    behind = [jnp.where(x >= m, fade(2 * rows * (m - 1)), 0.0) for m in (1, 2, 3)]
    plane = [fade(2 * rows * (3 - (x - m) % 4)) for m in range(4)]
    chip = fade(2 * rows)
    lower = jnp.where(y_lo == 1, fade(2 * rows * x), 0.0)
    straight = lower * shard
    across = lower * jnp.where(core == 0, 1.0, shard * shard)
    fades = jnp.concatenate([shard, straight, across], axis=0)
    behind, plane = jnp.stack(behind), jnp.stack(plane)

    slots = []
    for of_y in (y_lo, 1 - y_lo):
        for ring in (0, -1, 1, 2):
            of_z = (x + ring - z) % 4
            step = (of_z - z) % 4
            place = jnp.where(step == 3, 1, jnp.where(step == 1, 2, jnp.where(step == 2, 3, 0)))
            slots.append(jnp.where(of_y == y_hi, 0, 4) + place)
    where = jnp.stack(slots + [core]).astype(jnp.int32)
    core_at = jnp.stack([core]).astype(jnp.int32)

    def next_ctx(yl, x, c, yh, z):
        n = (yl * 4 + x) * 2 + c + 1
        return None if n == 16 else (n // 8, (n // 2) % 4, n % 2, yh, z)

    w = in_weight.reshape(BLOCK, 3 * wide)
    b = transposed(w)
    shard_tokens, *prms = together((tokens, *prms))
    steps = shard_tokens.reshape(SEG, rows // SEG, BLOCK).transpose(1, 0, 2).reshape(rows, BLOCK)
    t = jnp.concatenate([send(shard_tokens[rows - HALO:], next_ctx), steps], axis=0)
    t, b, where, core_at, fades, behind, plane, chip, *prms = together(
        (t, b, where, core_at, fades, behind, plane, chip, *prms)
    )
    tp_, tm, ty = along_z(t, 1), along_z(t, -1), other_yhi(t)
    bp, bm = along_x(b, 1), along_x(b, -1)
    t, b, tp_, tm, ty, bp, bm = together((t, b, tp_, tm, ty, bp, bm))
    typ, tym = along_z(ty, 1), along_z(ty, -1)
    cb, cbp, cbm = other_core(b), other_core(bp), other_core(bm)
    b, bp, cb, cbp, cbm = together((b, bp, cb, cbp, cbm))
    bf, a = along_x(bp, 1), other_ylo(b)
    t, b, tp_, tm, ty, bp, bm, typ, tym, bf, a, cb, cbp, cbm = together(
        (t, b, tp_, tm, ty, bp, bm, typ, tym, bf, a, cb, cbp, cbm)
    )
    tf, tyf = along_z(tp_, 1), along_z(tym, -1)
    ap = along_x(a, 1)
    cbf, ca = other_core(bf), other_core(a)
    bf, a, cbf, ca = together((bf, a, cbf, ca))
    am, af = along_x(a, -1), other_ylo(bf)
    lhs, part = begin(where, [t, tp_, tm, ty, typ, tym], [b, bp, bm, bf], rows)
    part_too = also(where, lhs, [cb, cbp, cbm, cbf], rows)
    lhs, part, part_too, ap, am, af, tf, tyf = together(
        (lhs, part, part_too, ap, am, af, tf, tyf)
    )
    mine = [b, bp, bm, bf, a, ap, am, af]
    theirs = [cb, cbp, cbm, cbf, ca] + [other_core(w) for w in (ap, am, af)]

    products, xs, us, ends = [], [], [], []
    for o, (weights, done) in enumerate(((mine, part), (theirs, part_too))):
        product, x1, u, end = project(where, lhs, tf, tyf, done, weights, prms[o], rows)
        products.append(product)
        xs.append(x1)
        us.append(u)
        ends.append(end)

    total = jnp.concatenate(
        [jnp.where(core == 0, ends[0], ends[1]), jnp.where(core == 0, ends[1], ends[0])], axis=1
    )
    total, products[0] = together((total, products[0]))
    came = [total] + [along_x(total, m) for m in (1, 2, 3)]
    y0 = read(products[0], us[0], prms[0], rows)
    came, products[1], y0 = together((came, products[1], y0))
    total = came[0]
    near = behind[0] * came[1] + behind[1] * came[2] + behind[2] * came[3]
    whole = plane[0] * came[0] + plane[1] * came[1] + plane[2] * came[2] + plane[3] * came[3]
    sent = other_core(jnp.where(core == 0, chip * near + total, near))
    same, cross = other_ylo(whole), other_ylo_and_core(whole)
    y1 = read(products[1], us[1], prms[1], rows)
    return gate(core_at, [y0, y1], xs, prms, [near, sent, same, cross, fades], rows)


def solution(mesh):
    placed = (P("ctx", "tp"), P("tp", None, "ctx"), P(), P(), P(), P())
    return jax.shard_map(
        on_device, mesh=mesh, in_specs=placed, out_specs=P("ctx", "tp"), check_vma=False
    )
```

```python
import functools

import jax
import jax.numpy as jnp
from jax import lax
from jax.experimental import pallas as pl
from jax.experimental.pallas import tpu as pltpu
from jax.sharding import PartitionSpec as P

D = 4096
MODES = 16
BLOCK = 512
SEG = 8
HALO = 16
SIZES = (2, 4, 2, 2, 4)
LANES = 128
F32 = jnp.float32


def route(move):
    pairs = []
    for yl in range(2):
        for x in range(4):
            for c in range(2):
                for yh in range(2):
                    for z in range(4):
                        to = move(yl, x, c, yh, z)
                        if to is None:
                            continue
                        a, b, e, f, g = to
                        pairs.append(
                            (
                                ((yl * 4 + x) * 2 + c) * 8 + yh * 4 + z,
                                (((a % 2) * 4 + b % 4) * 2 + e % 2) * 8 + (f % 2) * 4 + g % 4,
                            )
                        )
    return pairs


def send(value, move):
    return lax.ppermute(value, ("ctx", "tp"), route(move))


def along_z(value, step):
    return send(value, lambda yl, x, c, yh, z: (yl, x, c, yh, z + step))


def along_x(value, step):
    return send(value, lambda yl, x, c, yh, z: (yl, x + step, c, yh, z))


def other_core(value):
    return send(value, lambda yl, x, c, yh, z: (yl, x, c + 1, yh, z))


def other_yhi(value):
    return send(value, lambda yl, x, c, yh, z: (yl, x, c, yh + 1, z))


def other_ylo(value):
    return send(value, lambda yl, x, c, yh, z: (yl + 1, x, c, yh, z))


def other_ylo_and_core(value):
    return send(value, lambda yl, x, c, yh, z: (yl + 1, x, c + 1, yh, z))


def transposed(value):
    return send(value, lambda yl, x, c, yh, z: (yh, x + z, c, yl, x))


together = lax.optimization_barrier


def shift_down(value, steps):
    rows = lax.broadcasted_iota(jnp.int32, value.shape, 0)
    return jnp.where(rows >= steps, pltpu.roll(value, steps, 0), 0.0)


def first_half(where, lhs, weights, acc):
    acc[...] = jnp.zeros_like(acc)
    for k in range(4):
        slot = where[k]

        @pl.when(lax.rem(slot, 4) != 3)
        def _(k=k, slot=slot):
            acc[...] += jnp.dot(lhs[slot], weights[k][...], preferred_element_type=F32)


def begin_kernel(where, *refs):
    toks, weights, (lhs, acc) = refs[:6], refs[6:10], refs[10:]
    for n, s in enumerate((0, 1, 2, 4, 5, 6)):
        lhs[s] = toks[n][...]
    first_half(where, lhs, weights, acc)


def also_kernel(where, *refs):
    lhs, weights, acc = refs[0], refs[1:5], refs[5]
    first_half(where, lhs, weights, acc)


def begin(where, toks, weights, rows):
    vmem = pl.BlockSpec(memory_space=pltpu.VMEM)
    tall, width = rows + HALO, weights[0].shape[1]
    return pl.pallas_call(
        begin_kernel,
        out_shape=[
            jax.ShapeDtypeStruct((8, tall, BLOCK), jnp.bfloat16),
            jax.ShapeDtypeStruct((tall, width), F32),
        ],
        in_specs=[pl.BlockSpec(memory_space=pltpu.SMEM)] + [vmem] * 10,
        out_specs=[vmem] * 2,
        compiler_params=pltpu.CompilerParams(vmem_limit_bytes=26 << 20),
        cost_estimate=pl.CostEstimate(
            flops=2 * tall * 3 * BLOCK * width, bytes_accessed=12 << 20, transcendentals=0
        ),
    )(where, *toks, *weights)


def also(where, lhs, weights, rows):
    vmem = pl.BlockSpec(memory_space=pltpu.VMEM)
    tall, width = rows + HALO, weights[0].shape[1]
    return pl.pallas_call(
        also_kernel,
        out_shape=jax.ShapeDtypeStruct((tall, width), F32),
        in_specs=[pl.BlockSpec(memory_space=pltpu.SMEM)] + [vmem] * 5,
        out_specs=vmem,
        compiler_params=pltpu.CompilerParams(vmem_limit_bytes=26 << 20),
        cost_estimate=pl.CostEstimate(
            flops=2 * tall * 3 * BLOCK * width, bytes_accessed=12 << 20, transcendentals=0
        ),
    )(where, lhs, *weights)


def project_kernel(rows, where, *refs):
    lhs, near, far, part, *refs = refs
    weights, refs = refs[:8], refs[8:]
    prm, prod_ref, x1_ref, u_ref, end_ref, last, wfar, proj = refs
    seg_len = rows // SEG
    for k in range(8):
        at = pl.ds(max(k - 3, 0) * BLOCK, BLOCK)
        for s, ref in ((3, near), (7, far)):

            @pl.when(where[k] == s)
            def _(k=k, ref=ref, at=at):
                last[:, at] = ref[...]
                if k < 4:
                    wfar[...] = weights[k][...]

        if k >= 4:

            @pl.when(lax.rem(where[k], 4) != 3)
            def _(k=k, at=at):
                last[:, at] = lhs[where[k]]

    for n in range(3):
        cols = pl.ds(n * 2 * LANES, 2 * LANES)
        right = jnp.concatenate([w[:, cols] for w in (wfar, *weights[4:])], axis=0)
        out = part[:, cols] + jnp.dot(last[...], right, preferred_element_type=F32)
        out = out.astype(jnp.bfloat16).astype(F32)
        for q in range(2):
            proj[2 * n + q] = out[:, q * LANES:(q + 1) * LANES]

    top = lax.broadcasted_iota(jnp.int32, (SEG, LANES), 0) == 0
    for q in range(2):
        lanes = pl.ds(q * LANES, LANES)
        bcast = lambda r: jnp.broadcast_to(prm[pl.ds(r, 1), lanes], (SEG, LANES))
        decay = [bcast(k) for k in range(MODES)]
        taps = [[bcast(2 * MODES + 3 * j + g) for g in range(3)] for j in range(3)]

        def load(g, i):
            return proj[2 * g + q, pl.ds(pl.multiple_of(HALO + i * SEG, SEG), SEG), :]

        def load_before(g, back):
            halo = proj[2 * g + q, pl.ds(HALO - back, 1), :]
            return jnp.where(top, halo, pltpu.roll(load(g, seg_len - back), 1, 0))

        def step(i, carry):
            before, last, states = carry
            now = [load(g, i) for g in range(3)]
            feat = [
                taps[0][g] * now[g] + taps[1][g] * last[g] + taps[2][g] * before[g]
                for g in range(3)
            ]
            product = feat[1] * feat[2]
            at = pl.ds(pl.multiple_of(i * SEG, SEG), SEG)
            prod_ref[at, lanes] = product
            x1_ref[at, lanes] = feat[0]
            return (last, now, [decay[k] * states[k] + product for k in range(MODES)])

        zero = jnp.zeros((SEG, LANES), F32)
        first = tuple([load_before(g, back) for g in range(3)] for back in (2, 1))
        _, _, states = lax.fori_loop(0, seg_len, step, (*first, [zero] * MODES), unroll=4)
        for k in range(MODES):
            rate = prm[pl.ds(48 + k, 1), lanes]
            u = states[k]
            for n in (1, 2, 4):
                u = u + jnp.exp(-rate * (float(n) * seg_len)) * shift_down(u, n)
            u_ref[pl.ds(k * SEG, SEG), lanes] = u
            end_ref[pl.ds(k, 1), lanes] = u[SEG - 1:]


def project(where, lhs, near, far, part, weights, prm, rows):
    vmem = pl.BlockSpec(memory_space=pltpu.VMEM)
    wide, tall = 2 * LANES, rows + HALO
    return pl.pallas_call(
        functools.partial(project_kernel, rows),
        out_shape=[
            jax.ShapeDtypeStruct((rows, wide), F32),
            jax.ShapeDtypeStruct((rows, wide), F32),
            jax.ShapeDtypeStruct((MODES * SEG, wide), F32),
            jax.ShapeDtypeStruct((MODES, wide), F32),
        ],
        in_specs=[pl.BlockSpec(memory_space=pltpu.SMEM)] + [vmem] * 13,
        out_specs=[vmem] * 4,
        scratch_shapes=[
            pltpu.VMEM((tall, 5 * BLOCK), jnp.bfloat16),
            pltpu.VMEM((BLOCK, 3 * wide), jnp.bfloat16),
            pltpu.VMEM((6, tall, LANES), F32),
        ],
        compiler_params=pltpu.CompilerParams(vmem_limit_bytes=26 << 20),
        cost_estimate=pl.CostEstimate(
            flops=2 * tall * 5 * BLOCK * 3 * wide, bytes_accessed=12 << 20, transcendentals=0
        ),
    )(where, lhs, near, far, part, *weights, prm)


def read_kernel(rows, prod_ref, u_ref, prm, y_ref):
    seg_len = rows // SEG
    for q in range(2):
        lanes = pl.ds(q * LANES, LANES)
        bcast = lambda r: jnp.broadcast_to(prm[pl.ds(r, 1), lanes], (SEG, LANES))
        decay = [bcast(k) for k in range(MODES)]
        amp = [bcast(MODES + k) for k in range(MODES)]
        gain = bcast(2 * MODES + 9)

        def step(i, states):
            at = pl.ds(pl.multiple_of(i * SEG, SEG), SEG)
            product = prod_ref[at, lanes]
            states = [decay[k] * states[k] + product for k in range(MODES)]
            terms = [amp[k] * states[k] for k in range(MODES)] + [gain * product]
            while len(terms) > 1:
                terms = [a + b for a, b in zip(terms[::2], terms[1::2])] + (
                    [terms[-1]] if len(terms) % 2 else []
                )
            y_ref[at, lanes] = terms[0]
            return states

        start = [shift_down(u_ref[pl.ds(k * SEG, SEG), lanes], 1) for k in range(MODES)]
        lax.fori_loop(0, seg_len, step, start, unroll=4)


def read(prod, u, prm, rows):
    vmem = pl.BlockSpec(memory_space=pltpu.VMEM)
    return pl.pallas_call(
        functools.partial(read_kernel, rows),
        out_shape=jax.ShapeDtypeStruct(prod.shape, F32),
        in_specs=[vmem] * 3,
        out_specs=vmem,
        compiler_params=pltpu.CompilerParams(vmem_limit_bytes=12 << 20),
        cost_estimate=pl.CostEstimate(
            flops=4 * MODES * prod.size, bytes_accessed=12 << 20, transcendentals=0
        ),
    )(prod, u, prm)


def gate_kernel(rows, core_ref, y0, y1, x0, x1, p0, p1, local, up, two, down, first, scale, out_ref, wide):
    seg_len = rows // SEG
    core = core_ref[0]
    seg = lax.broadcasted_iota(jnp.int32, (SEG, LANES), 0).astype(F32) * seg_len
    for o, (y, x, prm) in enumerate(((y0, x0, p0), (y1, x1, p1))):
        base = lax.rem(core + o, 2) * (2 * LANES)
        for q in range(2):
            lanes = pl.ds(q * LANES, LANES)
            to = pl.ds(pl.multiple_of(base + q * LANES, LANES), LANES)
            state = local[:, to] + up[:, to] + two[:, to] + down[:, to]
            state = scale[:, to] * state + first[:, to]
            decay, carried = [], []
            for k in range(MODES):
                d = jnp.broadcast_to(prm[pl.ds(k, 1), lanes], (SEG, LANES))
                rate = prm[pl.ds(48 + k, 1), lanes]
                start = jnp.exp(-rate * seg) * state[k:k + 1]
                decay.append(d)
                carried.append(prm[pl.ds(MODES + k, 1), lanes] * d * start)

            def step(i, carried):
                terms = list(carried)
                while len(terms) > 1:
                    terms = [a + b for a, b in zip(terms[::2], terms[1::2])]
                at = pl.ds(pl.multiple_of(i * SEG, SEG), SEG)
                wide[pl.ds(i, SEG, stride=seg_len), :] = x[at, lanes] * (
                    y[at, lanes] + terms[0]
                )
                return [c * d for c, d in zip(carried, decay)]

            lax.fori_loop(0, seg_len, step, carried, unroll=4)
            out_ref[:, to] = wide[...].astype(out_ref.dtype)


def gate(core, ys, xs, prms, state, rows):
    vmem = pl.BlockSpec(memory_space=pltpu.VMEM)
    return pl.pallas_call(
        functools.partial(gate_kernel, rows),
        out_shape=jax.ShapeDtypeStruct((rows, BLOCK), jnp.bfloat16),
        in_specs=[pl.BlockSpec(memory_space=pltpu.SMEM)] + [vmem] * 12,
        out_specs=vmem,
        scratch_shapes=[pltpu.VMEM((rows, LANES), F32)],
        compiler_params=pltpu.CompilerParams(vmem_limit_bytes=20 << 20),
    )(core, *ys, *xs, *prms, *state)


def on_device(tokens, in_weight, short_filter, filter_residues, filter_rates, skip_gain):
    rows = tokens.shape[0]
    ctx, tp = lax.axis_index("ctx"), lax.axis_index("tp")
    y_lo, x, core = ctx // 8, (ctx // 2) % 4, ctx % 2
    y_hi, z = tp // 4, tp % 4
    wide = 2 * LANES

    base = tp * BLOCK
    rates = lax.dynamic_slice_in_dim(filter_rates, base, BLOCK, 0).T
    amps = lax.dynamic_slice_in_dim(filter_residues, base, BLOCK, 0).T * jnp.sqrt(rates)
    taps = lax.dynamic_slice_in_dim(short_filter, base, BLOCK, 2).reshape(9, BLOCK)
    gains = lax.dynamic_slice_in_dim(skip_gain, base, BLOCK, 0)[None]
    prm = jnp.concatenate(
        [jnp.exp(-rates), amps, taps, gains, jnp.zeros((6, BLOCK), F32), rates], axis=0
    )
    prms = [lax.dynamic_slice_in_dim(prm, (core + o) % 2 * wide, wide, 1) for o in range(2)]

    def fade(steps):
        return jnp.exp(-rates * jnp.asarray(steps).astype(F32))

    shard = fade(rows)
    scale = jnp.where(core == 0, 1.0, shard)
    own, lower = [], []
    for m in range(4):
        to = (x + m) % 4
        own.append(jnp.where(to > x, fade(2 * rows * jnp.maximum(to - x - 1, 0)), 0.0))
        lower.append(jnp.where(y_lo == 1, fade(2 * rows * (to + 3 - x)), 0.0))
    own, lower = jnp.stack(own), jnp.stack(lower)

    slots = []
    for of_y in (y_lo, 1 - y_lo):
        for ring in (0, -1, 1, 2):
            of_z = (x + ring - z) % 4
            step = (of_z - z) % 4
            place = jnp.where(step == 3, 1, jnp.where(step == 1, 2, jnp.where(step == 2, 3, 0)))
            slots.append(jnp.where(of_y == y_hi, 0, 4) + place)
    where = jnp.stack(slots + [core]).astype(jnp.int32)
    core_at = jnp.stack([core]).astype(jnp.int32)

    def next_ctx(yl, x, c, yh, z):
        n = (yl * 4 + x) * 2 + c + 1
        return None if n == 16 else (n // 8, (n // 2) % 4, n % 2, yh, z)

    w = jnp.concatenate([in_weight[:, g] for g in range(3)], axis=1)
    b = transposed(w)
    shard_tokens, *prms = together((tokens, *prms))
    steps = shard_tokens.reshape(SEG, rows // SEG, BLOCK).transpose(1, 0, 2).reshape(rows, BLOCK)
    t = jnp.concatenate([send(shard_tokens[rows - HALO:], next_ctx), steps], axis=0)
    t, b, where, core_at, shard, scale, own, lower, *prms = together(
        (t, b, where, core_at, shard, scale, own, lower, *prms)
    )
    tp_, tm, ty = along_z(t, 1), along_z(t, -1), other_yhi(t)
    bp, bm = along_x(b, 1), along_x(b, -1)
    t, b, tp_, tm, ty, bp, bm = together((t, b, tp_, tm, ty, bp, bm))
    typ, tym = along_z(ty, 1), along_z(ty, -1)
    cb, cbp, cbm = other_core(b), other_core(bp), other_core(bm)
    b, bp, cb, cbp, cbm = together((b, bp, cb, cbp, cbm))
    bf, a = along_x(bp, 1), other_ylo(b)
    t, b, tp_, tm, ty, bp, bm, typ, tym, bf, a, cb, cbp, cbm = together(
        (t, b, tp_, tm, ty, bp, bm, typ, tym, bf, a, cb, cbp, cbm)
    )
    tf, tyf = along_z(tp_, 1), along_z(tym, -1)
    ap = along_x(a, 1)
    cbf, ca = other_core(bf), other_core(a)
    bf, a, cbf, ca = together((bf, a, cbf, ca))
    am, af = along_x(a, -1), other_ylo(bf)
    lhs, part = begin(where, [t, tp_, tm, ty, typ, tym], [b, bp, bm, bf], rows)
    part_too = also(where, lhs, [cb, cbp, cbm, cbf], rows)
    lhs, part, part_too, ap, am, af, tf, tyf = together(
        (lhs, part, part_too, ap, am, af, tf, tyf)
    )
    mine = [b, bp, bm, bf, a, ap, am, af]
    theirs = [cb, cbp, cbm, cbf, ca] + [other_core(w) for w in (ap, am, af)]

    products, xs, us, ends = [], [], [], []
    for o, (weights, done) in enumerate(((mine, part), (theirs, part_too))):
        product, x1, u, end = project(where, lhs, tf, tyf, done, weights, prms[o], rows)
        products.append(product)
        xs.append(x1)
        us.append(u)
        ends.append(end)

    total = jnp.concatenate(
        [jnp.where(core == 0, ends[0], ends[1]), jnp.where(core == 0, ends[1], ends[0])], axis=1
    )
    total, products[0] = together((total, products[0]))
    came = [total, other_core(total), other_ylo(total), other_ylo_and_core(total)]
    y0 = read(products[0], us[0], prms[0], rows)
    came, products[1], y0 = together((came, products[1], y0))

    def chip_end(mine, other):
        return shard * jnp.where(core == 0, mine, other) + jnp.where(core == 0, other, mine)

    here, there = chip_end(*came[:2]), chip_end(*came[2:])
    ends = [own[m] * here + lower[m] * there for m in range(4)]
    state = ends[:1] + [along_x(ends[m], m) for m in (1, 2, 3)]
    first = jnp.where(core == 0, 0.0, came[1])
    y1 = read(products[1], us[1], prms[1], rows)
    return gate(core_at, [y0, y1], xs, prms, [*state, first, scale], rows)


def solution(mesh):
    placed = (P("ctx", "tp"), P("tp", None, "ctx"), P(), P(), P(), P())
    return jax.shard_map(
        on_device, mesh=mesh, in_specs=placed, out_specs=P("ctx", "tp"), check_vma=False
    )
```

```python
import functools

import jax
import jax.numpy as jnp
from jax import lax
from jax.experimental import pallas as pl
from jax.experimental.pallas import tpu as pltpu
from jax.sharding import PartitionSpec as P

D = 4096
MODES = 16
BLOCK = 512
SEG = 8
HALO = 16
SIZES = (2, 4, 2, 2, 4)
LANES = 128
F32 = jnp.float32


def route(move):
    pairs = []
    for yl in range(2):
        for x in range(4):
            for c in range(2):
                for yh in range(2):
                    for z in range(4):
                        to = move(yl, x, c, yh, z)
                        if to is None:
                            continue
                        a, b, e, f, g = to
                        pairs.append(
                            (
                                ((yl * 4 + x) * 2 + c) * 8 + yh * 4 + z,
                                (((a % 2) * 4 + b % 4) * 2 + e % 2) * 8 + (f % 2) * 4 + g % 4,
                            )
                        )
    return pairs


def send(value, move):
    return lax.ppermute(value, ("ctx", "tp"), route(move))


def along_z(value, step):
    return send(value, lambda yl, x, c, yh, z: (yl, x, c, yh, z + step))


def along_x(value, step):
    return send(value, lambda yl, x, c, yh, z: (yl, x + step, c, yh, z))


def other_core(value):
    return send(value, lambda yl, x, c, yh, z: (yl, x, c + 1, yh, z))


def other_yhi(value):
    return send(value, lambda yl, x, c, yh, z: (yl, x, c, yh + 1, z))


def other_ylo(value):
    return send(value, lambda yl, x, c, yh, z: (yl + 1, x, c, yh, z))


def other_ylo_and_core(value):
    return send(value, lambda yl, x, c, yh, z: (yl + 1, x, c + 1, yh, z))


def transposed(value):
    return send(value, lambda yl, x, c, yh, z: (yh, x + z, c, yl, x))


together = lax.optimization_barrier


def shift_down(value, steps):
    rows = lax.broadcasted_iota(jnp.int32, value.shape, 0)
    return jnp.where(rows >= steps, pltpu.roll(value, steps, 0), 0.0)


def first_half(where, lhs, weights, acc):
    acc[...] = jnp.zeros_like(acc)
    for k in range(4):
        slot = where[k]

        @pl.when(lax.rem(slot, 4) != 3)
        def _(k=k, slot=slot):
            acc[...] += jnp.dot(lhs[slot], weights[k][...], preferred_element_type=F32)


def begin_kernel(where, *refs):
    toks, weights, (lhs, acc) = refs[:6], refs[6:10], refs[10:]
    for n, s in enumerate((0, 1, 2, 4, 5, 6)):
        lhs[s] = toks[n][...]
    first_half(where, lhs, weights, acc)


def also_kernel(where, *refs):
    lhs, weights, acc = refs[0], refs[1:5], refs[5]
    first_half(where, lhs, weights, acc)


def begin(where, toks, weights, rows):
    vmem = pl.BlockSpec(memory_space=pltpu.VMEM)
    tall, width = rows + HALO, weights[0].shape[1]
    return pl.pallas_call(
        begin_kernel,
        out_shape=[
            jax.ShapeDtypeStruct((8, tall, BLOCK), jnp.bfloat16),
            jax.ShapeDtypeStruct((tall, width), F32),
        ],
        in_specs=[pl.BlockSpec(memory_space=pltpu.SMEM)] + [vmem] * 10,
        out_specs=[vmem] * 2,
        compiler_params=pltpu.CompilerParams(vmem_limit_bytes=26 << 20),
        cost_estimate=pl.CostEstimate(
            flops=2 * tall * 3 * BLOCK * width, bytes_accessed=12 << 20, transcendentals=0
        ),
    )(where, *toks, *weights)


def also(where, lhs, weights, rows):
    vmem = pl.BlockSpec(memory_space=pltpu.VMEM)
    tall, width = rows + HALO, weights[0].shape[1]
    return pl.pallas_call(
        also_kernel,
        out_shape=jax.ShapeDtypeStruct((tall, width), F32),
        in_specs=[pl.BlockSpec(memory_space=pltpu.SMEM)] + [vmem] * 5,
        out_specs=vmem,
        compiler_params=pltpu.CompilerParams(vmem_limit_bytes=26 << 20),
        cost_estimate=pl.CostEstimate(
            flops=2 * tall * 3 * BLOCK * width, bytes_accessed=12 << 20, transcendentals=0
        ),
    )(where, lhs, *weights)


def more_kernel(where, lhs, part, *refs):
    weights, acc = refs[:4], refs[4]
    is_near = [lax.rem(where[4 + k], 4) != 3 for k in range(4)]

    def product(k):
        return jnp.dot(lhs[where[4 + k]], weights[k][...], preferred_element_type=F32)

    def start(k):
        acc[...] = part[...] + product(k)

    def add(k):
        acc[...] += product(k)

    pl.when(is_near[0])(functools.partial(start, 0))
    pl.when(jnp.logical_not(is_near[0]))(functools.partial(start, 1))
    pl.when(jnp.logical_and(is_near[0], is_near[1]))(functools.partial(add, 1))
    pl.when(is_near[2])(functools.partial(add, 2))
    pl.when(is_near[3])(functools.partial(add, 3))


def more(where, lhs, part, weights, rows):
    vmem = pl.BlockSpec(memory_space=pltpu.VMEM)
    tall, width = rows + HALO, weights[0].shape[1]
    return pl.pallas_call(
        more_kernel,
        out_shape=jax.ShapeDtypeStruct((tall, width), F32),
        in_specs=[pl.BlockSpec(memory_space=pltpu.SMEM)] + [vmem] * 6,
        out_specs=vmem,
        compiler_params=pltpu.CompilerParams(vmem_limit_bytes=26 << 20),
        cost_estimate=pl.CostEstimate(
            flops=2 * tall * 3 * BLOCK * width, bytes_accessed=12 << 20, transcendentals=0
        ),
    )(where, lhs, part, *weights)


def project_kernel(rows, few, where, *refs):
    lhs, near, far, part, *refs = refs
    weights, refs = refs[:8], refs[8:]
    prm, prod_ref, x1_ref, u_ref, end_ref, last, late, proj = refs
    seg_len = rows // SEG
    for k in range(8):
        at = pl.ds((k // 4 if few else max(k - 3, 0)) * BLOCK, BLOCK)
        for s, ref in ((3, near), (7, far)):

            @pl.when(where[k] == s)
            def _(k=k, ref=ref, at=at):
                last[:, at] = ref[...]
                if few or k < 4:
                    late[at, :] = weights[k][...]

        if k >= 4 and not few:

            @pl.when(lax.rem(where[k], 4) != 3)
            def _(k=k, at=at):
                last[:, at] = lhs[where[k]]

    for n in range(3):
        cols = pl.ds(n * 2 * LANES, 2 * LANES)
        right = jnp.concatenate([w[:, cols] for w in ((late,) if few else (late, *weights[4:]))], axis=0)
        out = part[:, cols] + jnp.dot(last[...], right, preferred_element_type=F32)
        out = out.astype(jnp.bfloat16).astype(F32)
        for q in range(2):
            proj[2 * n + q] = out[:, q * LANES:(q + 1) * LANES]

    top = lax.broadcasted_iota(jnp.int32, (SEG, LANES), 0) == 0
    for q in range(2):
        lanes = pl.ds(q * LANES, LANES)
        bcast = lambda r: jnp.broadcast_to(prm[pl.ds(r, 1), lanes], (SEG, LANES))
        decay = [bcast(k) for k in range(MODES)]
        taps = [[bcast(2 * MODES + 3 * j + g) for g in range(3)] for j in range(3)]

        def load(g, i):
            return proj[2 * g + q, pl.ds(pl.multiple_of(HALO + i * SEG, SEG), SEG), :]

        def load_before(g, back):
            halo = proj[2 * g + q, pl.ds(HALO - back, 1), :]
            return jnp.where(top, halo, pltpu.roll(load(g, seg_len - back), 1, 0))

        def step(i, carry):
            before, last, states = carry
            now = [load(g, i) for g in range(3)]
            feat = [
                taps[0][g] * now[g] + taps[1][g] * last[g] + taps[2][g] * before[g]
                for g in range(3)
            ]
            product = feat[1] * feat[2]
            at = pl.ds(pl.multiple_of(i * SEG, SEG), SEG)
            prod_ref[at, lanes] = product
            x1_ref[at, lanes] = feat[0]
            return (last, now, [decay[k] * states[k] + product for k in range(MODES)])

        zero = jnp.zeros((SEG, LANES), F32)
        first = tuple([load_before(g, back) for g in range(3)] for back in (2, 1))
        _, _, states = lax.fori_loop(0, seg_len, step, (*first, [zero] * MODES), unroll=4)
        for k in range(MODES):
            rate = prm[pl.ds(48 + k, 1), lanes]
            u = states[k]
            for n in (1, 2, 4):
                u = u + jnp.exp(-rate * (float(n) * seg_len)) * shift_down(u, n)
            u_ref[pl.ds(k * SEG, SEG), lanes] = u
            end_ref[pl.ds(k, 1), lanes] = u[SEG - 1:]


def project(few, where, lhs, near, far, part, weights, prm, rows):
    vmem = pl.BlockSpec(memory_space=pltpu.VMEM)
    wide, tall = 2 * LANES, rows + HALO
    return pl.pallas_call(
        functools.partial(project_kernel, rows, few),
        out_shape=[
            jax.ShapeDtypeStruct((rows, wide), F32),
            jax.ShapeDtypeStruct((rows, wide), F32),
            jax.ShapeDtypeStruct((MODES * SEG, wide), F32),
            jax.ShapeDtypeStruct((MODES, wide), F32),
        ],
        in_specs=[pl.BlockSpec(memory_space=pltpu.SMEM)] + [vmem] * 13,
        out_specs=[vmem] * 4,
        scratch_shapes=[
            pltpu.VMEM((tall, (2 if few else 5) * BLOCK), jnp.bfloat16),
            pltpu.VMEM(((2 if few else 1) * BLOCK, 3 * wide), jnp.bfloat16),
            pltpu.VMEM((6, tall, LANES), F32),
        ],
        compiler_params=pltpu.CompilerParams(vmem_limit_bytes=26 << 20),
        cost_estimate=pl.CostEstimate(
            flops=2 * tall * 5 * BLOCK * 3 * wide, bytes_accessed=12 << 20, transcendentals=0
        ),
    )(where, lhs, near, far, part, *weights, prm)


def read_kernel(rows, prod_ref, u_ref, prm, y_ref):
    seg_len = rows // SEG
    for q in range(2):
        lanes = pl.ds(q * LANES, LANES)
        bcast = lambda r: jnp.broadcast_to(prm[pl.ds(r, 1), lanes], (SEG, LANES))
        decay = [bcast(k) for k in range(MODES)]
        amp = [bcast(MODES + k) for k in range(MODES)]
        gain = bcast(2 * MODES + 9)

        def step(i, states):
            at = pl.ds(pl.multiple_of(i * SEG, SEG), SEG)
            product = prod_ref[at, lanes]
            states = [decay[k] * states[k] + product for k in range(MODES)]
            terms = [amp[k] * states[k] for k in range(MODES)] + [gain * product]
            while len(terms) > 1:
                terms = [a + b for a, b in zip(terms[::2], terms[1::2])] + (
                    [terms[-1]] if len(terms) % 2 else []
                )
            y_ref[at, lanes] = terms[0]
            return states

        start = [shift_down(u_ref[pl.ds(k * SEG, SEG), lanes], 1) for k in range(MODES)]
        lax.fori_loop(0, seg_len, step, start, unroll=4)


def read(prod, u, prm, rows):
    vmem = pl.BlockSpec(memory_space=pltpu.VMEM)
    return pl.pallas_call(
        functools.partial(read_kernel, rows),
        out_shape=jax.ShapeDtypeStruct(prod.shape, F32),
        in_specs=[vmem] * 3,
        out_specs=vmem,
        compiler_params=pltpu.CompilerParams(vmem_limit_bytes=12 << 20),
        cost_estimate=pl.CostEstimate(
            flops=4 * MODES * prod.size, bytes_accessed=12 << 20, transcendentals=0
        ),
    )(prod, u, prm)


def gate_kernel(rows, core_ref, y0, y1, x0, x1, p0, p1, local, up, two, down, first, scale, out_ref, wide):
    seg_len = rows // SEG
    core = core_ref[0]
    seg = lax.broadcasted_iota(jnp.int32, (SEG, LANES), 0).astype(F32) * seg_len
    for o, (y, x, prm) in enumerate(((y0, x0, p0), (y1, x1, p1))):
        base = lax.rem(core + o, 2) * (2 * LANES)
        for q in range(2):
            lanes = pl.ds(q * LANES, LANES)
            to = pl.ds(pl.multiple_of(base + q * LANES, LANES), LANES)
            state = local[:, to] + up[:, to] + two[:, to] + down[:, to]
            state = scale[:, to] * state + first[:, to]
            decay, carried = [], []
            for k in range(MODES):
                d = jnp.broadcast_to(prm[pl.ds(k, 1), lanes], (SEG, LANES))
                rate = prm[pl.ds(48 + k, 1), lanes]
                start = jnp.exp(-rate * seg) * state[k:k + 1]
                decay.append(d)
                carried.append(prm[pl.ds(MODES + k, 1), lanes] * d * start)

            def step(i, carried):
                terms = list(carried)
                while len(terms) > 1:
                    terms = [a + b for a, b in zip(terms[::2], terms[1::2])]
                at = pl.ds(pl.multiple_of(i * SEG, SEG), SEG)
                wide[pl.ds(i, SEG, stride=seg_len), :] = x[at, lanes] * (
                    y[at, lanes] + terms[0]
                )
                return [c * d for c, d in zip(carried, decay)]

            lax.fori_loop(0, seg_len, step, carried, unroll=8)
            out_ref[:, to] = wide[...].astype(out_ref.dtype)


def gate(core, ys, xs, prms, state, rows):
    vmem = pl.BlockSpec(memory_space=pltpu.VMEM)
    return pl.pallas_call(
        functools.partial(gate_kernel, rows),
        out_shape=jax.ShapeDtypeStruct((rows, BLOCK), jnp.bfloat16),
        in_specs=[pl.BlockSpec(memory_space=pltpu.SMEM)] + [vmem] * 12,
        out_specs=vmem,
        scratch_shapes=[pltpu.VMEM((rows, LANES), F32)],
        compiler_params=pltpu.CompilerParams(vmem_limit_bytes=20 << 20),
    )(core, *ys, *xs, *prms, *state)


def on_device(tokens, in_weight, short_filter, filter_residues, filter_rates, skip_gain):
    rows = tokens.shape[0]
    ctx, tp = lax.axis_index("ctx"), lax.axis_index("tp")
    y_lo, x, core = ctx // 8, (ctx // 2) % 4, ctx % 2
    y_hi, z = tp // 4, tp % 4
    wide = 2 * LANES

    base = tp * BLOCK
    rates = lax.dynamic_slice_in_dim(filter_rates, base, BLOCK, 0).T
    amps = lax.dynamic_slice_in_dim(filter_residues, base, BLOCK, 0).T * jnp.sqrt(rates)
    taps = lax.dynamic_slice_in_dim(short_filter, base, BLOCK, 2).reshape(9, BLOCK)
    gains = lax.dynamic_slice_in_dim(skip_gain, base, BLOCK, 0)[None]
    prm = jnp.concatenate(
        [jnp.exp(-rates), amps, taps, gains, jnp.zeros((6, BLOCK), F32), rates], axis=0
    )
    prms = [lax.dynamic_slice_in_dim(prm, (core + o) % 2 * wide, wide, 1) for o in range(2)]

    def fade(steps):
        return jnp.exp(-rates * jnp.asarray(steps).astype(F32))

    shard = fade(rows)
    scale = jnp.where(core == 0, 1.0, shard)
    own, lower = [], []
    for m in range(4):
        to = (x + m) % 4
        own.append(jnp.where(to > x, fade(2 * rows * jnp.maximum(to - x - 1, 0)), 0.0))
        lower.append(jnp.where(y_lo == 1, fade(2 * rows * (to + 3 - x)), 0.0))
    own, lower = jnp.stack(own), jnp.stack(lower)

    slots = []
    for of_y in (y_lo, 1 - y_lo):
        for ring in (0, -1, 1, 2):
            of_z = (x + ring - z) % 4
            step = (of_z - z) % 4
            place = jnp.where(step == 3, 1, jnp.where(step == 1, 2, jnp.where(step == 2, 3, 0)))
            slots.append(jnp.where(of_y == y_hi, 0, 4) + place)
    where = jnp.stack(slots + [core]).astype(jnp.int32)
    core_at = jnp.stack([core]).astype(jnp.int32)

    def next_ctx(yl, x, c, yh, z):
        n = (yl * 4 + x) * 2 + c + 1
        return None if n == 16 else (n // 8, (n // 2) % 4, n % 2, yh, z)

    w = jnp.concatenate([in_weight[:, g] for g in range(3)], axis=1)
    b = transposed(w)
    shard_tokens, *prms = together((tokens, *prms))
    steps = shard_tokens.reshape(SEG, rows // SEG, BLOCK).transpose(1, 0, 2).reshape(rows, BLOCK)
    t = jnp.concatenate([send(shard_tokens[rows - HALO:], next_ctx), steps], axis=0)
    t, b, where, core_at, shard, scale, own, lower, *prms = together(
        (t, b, where, core_at, shard, scale, own, lower, *prms)
    )
    tp_, tm, ty = along_z(t, 1), along_z(t, -1), other_yhi(t)
    bp, bm = along_x(b, 1), along_x(b, -1)
    t, b, tp_, tm, ty, bp, bm = together((t, b, tp_, tm, ty, bp, bm))
    typ, tym = along_z(ty, 1), along_z(ty, -1)
    cb, cbp, cbm = other_core(b), other_core(bp), other_core(bm)
    b, bp, cb, cbp, cbm = together((b, bp, cb, cbp, cbm))
    bf, a = along_x(bp, 1), other_ylo(b)
    t, b, tp_, tm, ty, bp, bm, typ, tym, bf, a, cb, cbp, cbm = together(
        (t, b, tp_, tm, ty, bp, bm, typ, tym, bf, a, cb, cbp, cbm)
    )
    tf, tyf = along_z(tp_, 1), along_z(tym, -1)
    ap = along_x(a, 1)
    cbf, ca = other_core(bf), other_core(a)
    bf, a, cbf, ca = together((bf, a, cbf, ca))
    am, af = along_x(a, -1), other_ylo(bf)
    lhs, part = begin(where, [t, tp_, tm, ty, typ, tym], [b, bp, bm, bf], rows)
    part_too = also(where, lhs, [cb, cbp, cbm, cbf], rows)
    part = more(where, lhs, part, [a, ap, am, af], rows)
    lhs, part, part_too, ap, am, af, tf, tyf = together(
        (lhs, part, part_too, ap, am, af, tf, tyf)
    )
    mine = [b, bp, bm, bf, a, ap, am, af]
    theirs = [cb, cbp, cbm, cbf, ca] + [other_core(w) for w in (ap, am, af)]

    products, xs, us, ends = [], [], [], []
    for o, (weights, done) in enumerate(((mine, part), (theirs, part_too))):
        product, x1, u, end = project(o == 0, where, lhs, tf, tyf, done, weights, prms[o], rows)
        products.append(product)
        xs.append(x1)
        us.append(u)
        ends.append(end)

    total = jnp.concatenate(
        [jnp.where(core == 0, ends[0], ends[1]), jnp.where(core == 0, ends[1], ends[0])], axis=1
    )
    total, products[0] = together((total, products[0]))
    came = [total, other_core(total), other_ylo(total), other_ylo_and_core(total)]
    y0 = read(products[0], us[0], prms[0], rows)
    came, products[1], y0 = together((came, products[1], y0))

    def chip_end(mine, other):
        return shard * jnp.where(core == 0, mine, other) + jnp.where(core == 0, other, mine)

    here, there = chip_end(*came[:2]), chip_end(*came[2:])
    ends = [own[m] * here + lower[m] * there for m in range(4)]
    state = ends[:1] + [along_x(ends[m], m) for m in (1, 2, 3)]
    first = jnp.where(core == 0, 0.0, came[1])
    y1 = read(products[1], us[1], prms[1], rows)
    return gate(core_at, [y0, y1], xs, prms, [*state, first, scale], rows)


def solution(mesh):
    placed = (P("ctx", "tp"), P("tp", None, "ctx"), P(), P(), P(), P())
    return jax.shard_map(
        on_device, mesh=mesh, in_specs=placed, out_specs=P("ctx", "tp"), check_vma=False
    )
```

```python
import functools

import jax
import jax.numpy as jnp
from jax import lax
from jax.experimental import pallas as pl
from jax.experimental.pallas import tpu as pltpu
from jax.sharding import PartitionSpec as P

D = 4096
MODES = 16
BLOCK = 512
SEG = 8
HALO = 16
SIZES = (2, 4, 2, 2, 4)
LANES = 128
F32 = jnp.float32


def route(move):
    pairs = []
    for yl in range(2):
        for x in range(4):
            for c in range(2):
                for yh in range(2):
                    for z in range(4):
                        to = move(yl, x, c, yh, z)
                        if to is None:
                            continue
                        a, b, e, f, g = to
                        pairs.append(
                            (
                                ((yl * 4 + x) * 2 + c) * 8 + yh * 4 + z,
                                (((a % 2) * 4 + b % 4) * 2 + e % 2) * 8 + (f % 2) * 4 + g % 4,
                            )
                        )
    return pairs


def send(value, move):
    return lax.ppermute(value, ("ctx", "tp"), route(move))


def along_z(value, step):
    return send(value, lambda yl, x, c, yh, z: (yl, x, c, yh, z + step))


def along_x(value, step):
    return send(value, lambda yl, x, c, yh, z: (yl, x + step, c, yh, z))


def other_core(value):
    return send(value, lambda yl, x, c, yh, z: (yl, x, c + 1, yh, z))


def other_yhi(value):
    return send(value, lambda yl, x, c, yh, z: (yl, x, c, yh + 1, z))


def other_ylo(value):
    return send(value, lambda yl, x, c, yh, z: (yl + 1, x, c, yh, z))


def other_ylo_and_core(value):
    return send(value, lambda yl, x, c, yh, z: (yl + 1, x, c + 1, yh, z))


def transposed(value):
    return send(value, lambda yl, x, c, yh, z: (yh, x + z, c, yl, x))


together = lax.optimization_barrier


def shift_down(value, steps):
    rows = lax.broadcasted_iota(jnp.int32, value.shape, 0)
    return jnp.where(rows >= steps, pltpu.roll(value, steps, 0), 0.0)


def side_by_side(weight):
    return jnp.concatenate([weight[g] for g in range(3)], axis=1)


def first_half(where, lhs, weights, acc):
    acc[...] = jnp.zeros_like(acc)
    for k in range(4):
        slot = where[k]

        @pl.when(lax.rem(slot, 4) != 3)
        def _(k=k, slot=slot):
            acc[...] += jnp.dot(lhs[slot], side_by_side(weights[k]), preferred_element_type=F32)


def begin_kernel(where, *refs):
    toks, weights, (lhs, acc) = refs[:6], refs[6:10], refs[10:]
    for n, s in enumerate((0, 1, 2, 4, 5, 6)):
        lhs[s] = toks[n][...]
    first_half(where, lhs, weights, acc)


def also_kernel(where, *refs):
    lhs, weights, acc = refs[0], refs[1:5], refs[5]
    first_half(where, lhs, weights, acc)


def begin(where, toks, weights, rows):
    vmem = pl.BlockSpec(memory_space=pltpu.VMEM)
    tall, width = rows + HALO, 3 * weights[0].shape[2]
    return pl.pallas_call(
        begin_kernel,
        out_shape=[
            jax.ShapeDtypeStruct((8, tall, BLOCK), jnp.bfloat16),
            jax.ShapeDtypeStruct((tall, width), F32),
        ],
        in_specs=[pl.BlockSpec(memory_space=pltpu.SMEM)] + [vmem] * 10,
        out_specs=[vmem] * 2,
        compiler_params=pltpu.CompilerParams(vmem_limit_bytes=26 << 20),
        cost_estimate=pl.CostEstimate(
            flops=2 * tall * 3 * BLOCK * width, bytes_accessed=12 << 20, transcendentals=0
        ),
    )(where, *toks, *weights)


def also(where, lhs, weights, rows):
    vmem = pl.BlockSpec(memory_space=pltpu.VMEM)
    tall, width = rows + HALO, 3 * weights[0].shape[2]
    return pl.pallas_call(
        also_kernel,
        out_shape=jax.ShapeDtypeStruct((tall, width), F32),
        in_specs=[pl.BlockSpec(memory_space=pltpu.SMEM)] + [vmem] * 5,
        out_specs=vmem,
        compiler_params=pltpu.CompilerParams(vmem_limit_bytes=26 << 20),
        cost_estimate=pl.CostEstimate(
            flops=2 * tall * 3 * BLOCK * width, bytes_accessed=12 << 20, transcendentals=0
        ),
    )(where, lhs, *weights)


def more_kernel(where, lhs, part, *refs):
    weights, acc = refs[:4], refs[4]
    is_near = [lax.rem(where[4 + k], 4) != 3 for k in range(4)]

    def product(k):
        return jnp.dot(lhs[where[4 + k]], side_by_side(weights[k]), preferred_element_type=F32)

    def start(k):
        acc[...] = part[...] + product(k)

    def add(k):
        acc[...] += product(k)

    pl.when(is_near[0])(functools.partial(start, 0))
    pl.when(jnp.logical_not(is_near[0]))(functools.partial(start, 1))
    pl.when(jnp.logical_and(is_near[0], is_near[1]))(functools.partial(add, 1))
    pl.when(is_near[2])(functools.partial(add, 2))
    pl.when(is_near[3])(functools.partial(add, 3))


def more(where, lhs, part, weights, rows):
    vmem = pl.BlockSpec(memory_space=pltpu.VMEM)
    tall, width = rows + HALO, 3 * weights[0].shape[2]
    return pl.pallas_call(
        more_kernel,
        out_shape=jax.ShapeDtypeStruct((tall, width), F32),
        in_specs=[pl.BlockSpec(memory_space=pltpu.SMEM)] + [vmem] * 6,
        out_specs=vmem,
        compiler_params=pltpu.CompilerParams(vmem_limit_bytes=26 << 20),
        cost_estimate=pl.CostEstimate(
            flops=2 * tall * 3 * BLOCK * width, bytes_accessed=12 << 20, transcendentals=0
        ),
    )(where, lhs, part, *weights)


def project_kernel(rows, few, where, *refs):
    lhs, near, far, part, *refs = refs
    weights, refs = refs[:8], refs[8:]
    prm, prod_ref, x1_ref, u_ref, end_ref, last, late, proj = refs
    seg_len = rows // SEG
    for k in range(8):
        at = pl.ds((k // 4 if few else max(k - 3, 0)) * BLOCK, BLOCK)
        for s, ref in ((3, near), (7, far)):

            @pl.when(where[k] == s)
            def _(k=k, ref=ref, at=at):
                last[:, at] = ref[...]
                if few or k < 4:
                    late[at, :] = side_by_side(weights[k])

        if k >= 4 and not few:

            @pl.when(lax.rem(where[k], 4) != 3)
            def _(k=k, at=at):
                last[:, at] = lhs[where[k]]

    for n in range(3):
        cols = pl.ds(n * 2 * LANES, 2 * LANES)
        right = jnp.concatenate([late[:, cols]] + [w[n] for w in ([] if few else weights[4:])], axis=0)
        out = part[:, cols] + jnp.dot(last[...], right, preferred_element_type=F32)
        out = out.astype(jnp.bfloat16).astype(F32)
        for q in range(2):
            proj[2 * n + q] = out[:, q * LANES:(q + 1) * LANES]

    top = lax.broadcasted_iota(jnp.int32, (SEG, LANES), 0) == 0
    for q in range(2):
        lanes = pl.ds(q * LANES, LANES)
        bcast = lambda r: jnp.broadcast_to(prm[pl.ds(r, 1), lanes], (SEG, LANES))
        decay = [bcast(k) for k in range(MODES)]
        taps = [[bcast(2 * MODES + 3 * j + g) for g in range(3)] for j in range(3)]

        def load(g, i):
            return proj[2 * g + q, pl.ds(pl.multiple_of(HALO + i * SEG, SEG), SEG), :]

        def load_before(g, back):
            halo = proj[2 * g + q, pl.ds(HALO - back, 1), :]
            return jnp.where(top, halo, pltpu.roll(load(g, seg_len - back), 1, 0))

        def step(i, carry):
            before, last, states = carry
            now = [load(g, i) for g in range(3)]
            feat = [
                taps[0][g] * now[g] + taps[1][g] * last[g] + taps[2][g] * before[g]
                for g in range(3)
            ]
            product = feat[1] * feat[2]
            at = pl.ds(pl.multiple_of(i * SEG, SEG), SEG)
            prod_ref[at, lanes] = product
            x1_ref[at, lanes] = feat[0]
            return (last, now, [decay[k] * states[k] + product for k in range(MODES)])

        zero = jnp.zeros((SEG, LANES), F32)
        first = tuple([load_before(g, back) for g in range(3)] for back in (2, 1))
        _, _, states = lax.fori_loop(0, seg_len, step, (*first, [zero] * MODES), unroll=4)
        for k in range(MODES):
            rate = prm[pl.ds(48 + k, 1), lanes]
            u = states[k]
            for n in (1, 2, 4):
                u = u + jnp.exp(-rate * (float(n) * seg_len)) * shift_down(u, n)
            u_ref[pl.ds(k * SEG, SEG), lanes] = u
            end_ref[pl.ds(k, 1), lanes] = u[SEG - 1:]


def project(few, where, lhs, near, far, part, weights, prm, rows):
    vmem = pl.BlockSpec(memory_space=pltpu.VMEM)
    wide, tall = 2 * LANES, rows + HALO
    return pl.pallas_call(
        functools.partial(project_kernel, rows, few),
        out_shape=[
            jax.ShapeDtypeStruct((rows, wide), F32),
            jax.ShapeDtypeStruct((rows, wide), F32),
            jax.ShapeDtypeStruct((MODES * SEG, wide), F32),
            jax.ShapeDtypeStruct((MODES, wide), F32),
        ],
        in_specs=[pl.BlockSpec(memory_space=pltpu.SMEM)] + [vmem] * 13,
        out_specs=[vmem] * 4,
        scratch_shapes=[
            pltpu.VMEM((tall, (2 if few else 5) * BLOCK), jnp.bfloat16),
            pltpu.VMEM(((2 if few else 1) * BLOCK, 3 * wide), jnp.bfloat16),
            pltpu.VMEM((6, tall, LANES), F32),
        ],
        compiler_params=pltpu.CompilerParams(vmem_limit_bytes=26 << 20),
        cost_estimate=pl.CostEstimate(
            flops=2 * tall * 5 * BLOCK * 3 * wide, bytes_accessed=12 << 20, transcendentals=0
        ),
    )(where, lhs, near, far, part, *weights, prm)


def read_kernel(rows, prod_ref, u_ref, prm, y_ref):
    seg_len = rows // SEG
    for q in range(2):
        lanes = pl.ds(q * LANES, LANES)
        bcast = lambda r: jnp.broadcast_to(prm[pl.ds(r, 1), lanes], (SEG, LANES))
        decay = [bcast(k) for k in range(MODES)]
        amp = [bcast(MODES + k) for k in range(MODES)]
        gain = bcast(2 * MODES + 9)

        def step(i, states):
            at = pl.ds(pl.multiple_of(i * SEG, SEG), SEG)
            product = prod_ref[at, lanes]
            states = [decay[k] * states[k] + product for k in range(MODES)]
            terms = [amp[k] * states[k] for k in range(MODES)] + [gain * product]
            while len(terms) > 1:
                terms = [a + b for a, b in zip(terms[::2], terms[1::2])] + (
                    [terms[-1]] if len(terms) % 2 else []
                )
            y_ref[at, lanes] = terms[0]
            return states

        start = [shift_down(u_ref[pl.ds(k * SEG, SEG), lanes], 1) for k in range(MODES)]
        lax.fori_loop(0, seg_len, step, start, unroll=4)


def read(prod, u, prm, rows):
    vmem = pl.BlockSpec(memory_space=pltpu.VMEM)
    return pl.pallas_call(
        functools.partial(read_kernel, rows),
        out_shape=jax.ShapeDtypeStruct(prod.shape, F32),
        in_specs=[vmem] * 3,
        out_specs=vmem,
        compiler_params=pltpu.CompilerParams(vmem_limit_bytes=12 << 20),
        cost_estimate=pl.CostEstimate(
            flops=4 * MODES * prod.size, bytes_accessed=12 << 20, transcendentals=0
        ),
    )(prod, u, prm)


def gate_kernel(rows, core_ref, y0, y1, x0, x1, p0, p1, local, up, two, down, first, scale, out_ref, wide):
    seg_len = rows // SEG
    core = core_ref[0]
    seg = lax.broadcasted_iota(jnp.int32, (SEG, LANES), 0).astype(F32) * seg_len
    for o, (y, x, prm) in enumerate(((y0, x0, p0), (y1, x1, p1))):
        base = lax.rem(core + o, 2) * (2 * LANES)
        for q in range(2):
            lanes = pl.ds(q * LANES, LANES)
            to = pl.ds(pl.multiple_of(base + q * LANES, LANES), LANES)
            state = local[:, to] + up[:, to] + two[:, to] + down[:, to]
            state = scale[:, to] * state + first[:, to]
            decay, carried = [], []
            for k in range(MODES):
                d = jnp.broadcast_to(prm[pl.ds(k, 1), lanes], (SEG, LANES))
                rate = prm[pl.ds(48 + k, 1), lanes]
                start = jnp.exp(-rate * seg) * state[k:k + 1]
                decay.append(d)
                carried.append(prm[pl.ds(MODES + k, 1), lanes] * d * start)

            def step(i, carried):
                terms = list(carried)
                while len(terms) > 1:
                    terms = [a + b for a, b in zip(terms[::2], terms[1::2])]
                at = pl.ds(pl.multiple_of(i * SEG, SEG), SEG)
                wide[pl.ds(i, SEG, stride=seg_len), :] = x[at, lanes] * (
                    y[at, lanes] + terms[0]
                )
                return [c * d for c, d in zip(carried, decay)]

            lax.fori_loop(0, seg_len, step, carried, unroll=8)
            out_ref[:, to] = wide[...].astype(out_ref.dtype)


def gate(core, ys, xs, prms, state, rows):
    vmem = pl.BlockSpec(memory_space=pltpu.VMEM)
    return pl.pallas_call(
        functools.partial(gate_kernel, rows),
        out_shape=jax.ShapeDtypeStruct((rows, BLOCK), jnp.bfloat16),
        in_specs=[pl.BlockSpec(memory_space=pltpu.SMEM)] + [vmem] * 12,
        out_specs=vmem,
        scratch_shapes=[pltpu.VMEM((rows, LANES), F32)],
        compiler_params=pltpu.CompilerParams(vmem_limit_bytes=20 << 20),
    )(core, *ys, *xs, *prms, *state)


def on_device(tokens, in_weight, short_filter, filter_residues, filter_rates, skip_gain):
    rows = tokens.shape[0]
    ctx, tp = lax.axis_index("ctx"), lax.axis_index("tp")
    y_lo, x, core = ctx // 8, (ctx // 2) % 4, ctx % 2
    y_hi, z = tp // 4, tp % 4
    wide = 2 * LANES

    base = tp * BLOCK
    rates = lax.dynamic_slice_in_dim(filter_rates, base, BLOCK, 0).T
    amps = lax.dynamic_slice_in_dim(filter_residues, base, BLOCK, 0).T * jnp.sqrt(rates)
    taps = lax.dynamic_slice_in_dim(short_filter, base, BLOCK, 2).reshape(9, BLOCK)
    gains = lax.dynamic_slice_in_dim(skip_gain, base, BLOCK, 0)[None]
    prm = jnp.concatenate(
        [jnp.exp(-rates), amps, taps, gains, jnp.zeros((6, BLOCK), F32), rates], axis=0
    )
    prms = [lax.dynamic_slice_in_dim(prm, (core + o) % 2 * wide, wide, 1) for o in range(2)]

    def fade(steps):
        return jnp.exp(-rates * jnp.asarray(steps).astype(F32))

    shard = fade(rows)
    scale = jnp.where(core == 0, 1.0, shard)
    own, lower = [], []
    for m in range(4):
        to = (x + m) % 4
        own.append(jnp.where(to > x, fade(2 * rows * jnp.maximum(to - x - 1, 0)), 0.0))
        lower.append(jnp.where(y_lo == 1, fade(2 * rows * (to + 3 - x)), 0.0))
    own, lower = jnp.stack(own), jnp.stack(lower)

    slots = []
    for of_y in (y_lo, 1 - y_lo):
        for ring in (0, -1, 1, 2):
            of_z = (x + ring - z) % 4
            step = (of_z - z) % 4
            place = jnp.where(step == 3, 1, jnp.where(step == 1, 2, jnp.where(step == 2, 3, 0)))
            slots.append(jnp.where(of_y == y_hi, 0, 4) + place)
    where = jnp.stack(slots + [core]).astype(jnp.int32)
    core_at = jnp.stack([core]).astype(jnp.int32)

    def next_ctx(yl, x, c, yh, z):
        n = (yl * 4 + x) * 2 + c + 1
        return None if n == 16 else (n // 8, (n // 2) % 4, n % 2, yh, z)

    w = in_weight.transpose(1, 0, 2)
    b = transposed(w)
    shard_tokens, *prms = together((tokens, *prms))
    steps = shard_tokens.reshape(SEG, rows // SEG, BLOCK).transpose(1, 0, 2).reshape(rows, BLOCK)
    t = jnp.concatenate([send(shard_tokens[rows - HALO:], next_ctx), steps], axis=0)
    t, b, where, core_at, shard, scale, own, lower, *prms = together(
        (t, b, where, core_at, shard, scale, own, lower, *prms)
    )
    tp_, tm, ty = along_z(t, 1), along_z(t, -1), other_yhi(t)
    bp, bm = along_x(b, 1), along_x(b, -1)
    t, b, tp_, tm, ty, bp, bm = together((t, b, tp_, tm, ty, bp, bm))
    typ, tym = along_z(ty, 1), along_z(ty, -1)
    cb, cbp, cbm = other_core(b), other_core(bp), other_core(bm)
    b, bp, cb, cbp, cbm = together((b, bp, cb, cbp, cbm))
    bf, a = along_x(bp, 1), other_ylo(b)
    t, b, tp_, tm, ty, bp, bm, typ, tym, bf, a, cb, cbp, cbm = together(
        (t, b, tp_, tm, ty, bp, bm, typ, tym, bf, a, cb, cbp, cbm)
    )
    tf, tyf = along_z(tp_, 1), along_z(tym, -1)
    ap = along_x(a, 1)
    cbf, ca = other_core(bf), other_core(a)
    bf, a, cbf, ca = together((bf, a, cbf, ca))
    am, af = along_x(a, -1), other_ylo(bf)
    lhs, part = begin(where, [t, tp_, tm, ty, typ, tym], [b, bp, bm, bf], rows)
    part_too = also(where, lhs, [cb, cbp, cbm, cbf], rows)
    part = more(where, lhs, part, [a, ap, am, af], rows)
    lhs, part, part_too, ap, am, af, tf, tyf = together(
        (lhs, part, part_too, ap, am, af, tf, tyf)
    )
    mine = [b, bp, bm, bf, a, ap, am, af]
    theirs = [cb, cbp, cbm, cbf, ca] + [other_core(w) for w in (ap, am, af)]

    products, xs, us, ends = [], [], [], []
    for o, (weights, done) in enumerate(((mine, part), (theirs, part_too))):
        product, x1, u, end = project(o == 0, where, lhs, tf, tyf, done, weights, prms[o], rows)
        products.append(product)
        xs.append(x1)
        us.append(u)
        ends.append(end)

    total = jnp.concatenate(
        [jnp.where(core == 0, ends[0], ends[1]), jnp.where(core == 0, ends[1], ends[0])], axis=1
    )
    total, products[0] = together((total, products[0]))
    came = [total, other_core(total), other_ylo(total), other_ylo_and_core(total)]
    y0 = read(products[0], us[0], prms[0], rows)
    came, products[1], y0 = together((came, products[1], y0))

    def chip_end(mine, other):
        return shard * jnp.where(core == 0, mine, other) + jnp.where(core == 0, other, mine)

    here, there = chip_end(*came[:2]), chip_end(*came[2:])
    ends = [own[m] * here + lower[m] * there for m in range(4)]
    state = ends[:1] + [along_x(ends[m], m) for m in (1, 2, 3)]
    first = jnp.where(core == 0, 0.0, came[1])
    y1 = read(products[1], us[1], prms[1], rows)
    return gate(core_at, [y0, y1], xs, prms, [*state, first, scale], rows)


def solution(mesh):
    placed = (P("ctx", "tp"), P("tp", None, "ctx"), P(), P(), P(), P())
    return jax.shard_map(
        on_device, mesh=mesh, in_specs=placed, out_specs=P("ctx", "tp"), check_vma=False
    )
```

```python
import functools

import jax
import jax.numpy as jnp
from jax import lax
from jax.experimental import pallas as pl
from jax.experimental.pallas import tpu as pltpu
from jax.sharding import PartitionSpec as P

D = 4096
MODES = 16
BLOCK = 512
SEG = 8
HALO = 16
SIZES = (2, 4, 2, 2, 4)
LANES = 128
F32 = jnp.float32


def route(move):
    pairs = []
    for yl in range(2):
        for x in range(4):
            for c in range(2):
                for yh in range(2):
                    for z in range(4):
                        to = move(yl, x, c, yh, z)
                        if to is None:
                            continue
                        a, b, e, f, g = to
                        pairs.append(
                            (
                                ((yl * 4 + x) * 2 + c) * 8 + yh * 4 + z,
                                (((a % 2) * 4 + b % 4) * 2 + e % 2) * 8 + (f % 2) * 4 + g % 4,
                            )
                        )
    return pairs


def send(value, move):
    return lax.ppermute(value, ("ctx", "tp"), route(move))


def along_z(value, step):
    return send(value, lambda yl, x, c, yh, z: (yl, x, c, yh, z + step))


def along_x(value, step):
    return send(value, lambda yl, x, c, yh, z: (yl, x + step, c, yh, z))


def other_core(value):
    return send(value, lambda yl, x, c, yh, z: (yl, x, c + 1, yh, z))


def other_yhi(value):
    return send(value, lambda yl, x, c, yh, z: (yl, x, c, yh + 1, z))


def other_ylo(value):
    return send(value, lambda yl, x, c, yh, z: (yl + 1, x, c, yh, z))


def other_ylo_and_core(value):
    return send(value, lambda yl, x, c, yh, z: (yl + 1, x, c + 1, yh, z))


def transposed(value):
    return send(value, lambda yl, x, c, yh, z: (yh, x + z, c, yl, x))


together = lax.optimization_barrier


def shift_down(value, steps):
    rows = lax.broadcasted_iota(jnp.int32, value.shape, 0)
    return jnp.where(rows >= steps, pltpu.roll(value, steps, 0), 0.0)


def side_by_side(weight):
    return jnp.concatenate([weight[g] for g in range(3)], axis=1)


def first_half(where, lhs, weights, acc):
    acc[...] = jnp.zeros_like(acc)
    for k in range(4):
        slot = where[k]

        @pl.when(lax.rem(slot, 4) != 3)
        def _(k=k, slot=slot):
            acc[...] += jnp.dot(lhs[slot], side_by_side(weights[k]), preferred_element_type=F32)


def begin_kernel(where, *refs):
    toks, weights, (lhs, acc) = refs[:6], refs[6:10], refs[10:]
    for n, s in enumerate((0, 1, 2, 4, 5, 6)):
        lhs[s] = toks[n][...]
    first_half(where, lhs, weights, acc)


def also_kernel(where, *refs):
    lhs, weights, acc = refs[0], refs[1:5], refs[5]
    first_half(where, lhs, weights, acc)


def begin(where, toks, weights, rows):
    vmem = pl.BlockSpec(memory_space=pltpu.VMEM)
    tall, width = rows + HALO, 3 * weights[0].shape[2]
    return pl.pallas_call(
        begin_kernel,
        out_shape=[
            jax.ShapeDtypeStruct((8, tall, BLOCK), jnp.bfloat16),
            jax.ShapeDtypeStruct((tall, width), F32),
        ],
        in_specs=[pl.BlockSpec(memory_space=pltpu.SMEM)] + [vmem] * 10,
        out_specs=[vmem] * 2,
        compiler_params=pltpu.CompilerParams(vmem_limit_bytes=26 << 20),
        cost_estimate=pl.CostEstimate(
            flops=2 * tall * 3 * BLOCK * width, bytes_accessed=12 << 20, transcendentals=0
        ),
    )(where, *toks, *weights)


def also(where, lhs, weights, rows):
    vmem = pl.BlockSpec(memory_space=pltpu.VMEM)
    tall, width = rows + HALO, 3 * weights[0].shape[2]
    return pl.pallas_call(
        also_kernel,
        out_shape=jax.ShapeDtypeStruct((tall, width), F32),
        in_specs=[pl.BlockSpec(memory_space=pltpu.SMEM)] + [vmem] * 5,
        out_specs=vmem,
        compiler_params=pltpu.CompilerParams(vmem_limit_bytes=26 << 20),
        cost_estimate=pl.CostEstimate(
            flops=2 * tall * 3 * BLOCK * width, bytes_accessed=12 << 20, transcendentals=0
        ),
    )(where, lhs, *weights)


def more_kernel(where, lhs, part, *refs):
    weights, acc = refs[:4], refs[4]
    is_near = [lax.rem(where[4 + k], 4) != 3 for k in range(4)]

    def product(k):
        return jnp.dot(lhs[where[4 + k]], side_by_side(weights[k]), preferred_element_type=F32)

    def start(k):
        acc[...] = part[...] + product(k)

    def add(k):
        acc[...] += product(k)

    pl.when(is_near[0])(functools.partial(start, 0))
    pl.when(jnp.logical_not(is_near[0]))(functools.partial(start, 1))
    pl.when(jnp.logical_and(is_near[0], is_near[1]))(functools.partial(add, 1))
    pl.when(is_near[2])(functools.partial(add, 2))
    pl.when(is_near[3])(functools.partial(add, 3))


def more(where, lhs, part, weights, rows):
    vmem = pl.BlockSpec(memory_space=pltpu.VMEM)
    tall, width = rows + HALO, 3 * weights[0].shape[2]
    return pl.pallas_call(
        more_kernel,
        out_shape=jax.ShapeDtypeStruct((tall, width), F32),
        in_specs=[pl.BlockSpec(memory_space=pltpu.SMEM)] + [vmem] * 6,
        out_specs=vmem,
        compiler_params=pltpu.CompilerParams(vmem_limit_bytes=26 << 20),
        cost_estimate=pl.CostEstimate(
            flops=2 * tall * 3 * BLOCK * width, bytes_accessed=12 << 20, transcendentals=0
        ),
    )(where, lhs, part, *weights)


def project_kernel(rows, few, where, *refs):
    lhs, near, far, part, *refs = refs
    weights, refs = refs[:8], refs[8:]
    prm, prod_ref, x1_ref, u_ref, end_ref, last, late, proj = refs
    seg_len = rows // SEG
    for k in range(8):
        at = pl.ds((k // 4 if few else max(k - 3, 0)) * BLOCK, BLOCK)
        for s, ref in ((3, near), (7, far)):

            @pl.when(where[k] == s)
            def _(k=k, ref=ref, at=at):
                last[:, at] = ref[...]
                if few or k < 4:
                    late[at, :] = side_by_side(weights[k])

        if k >= 4 and not few:

            @pl.when(lax.rem(where[k], 4) != 3)
            def _(k=k, at=at):
                last[:, at] = lhs[where[k]]

    for n in range(3):
        cols = pl.ds(n * 2 * LANES, 2 * LANES)
        right = jnp.concatenate([late[:, cols]] + [w[n] for w in ([] if few else weights[4:])], axis=0)
        out = part[:, cols] + jnp.dot(last[...], right, preferred_element_type=F32)
        out = out.astype(jnp.bfloat16).astype(F32)
        for q in range(2):
            proj[2 * n + q] = out[:, q * LANES:(q + 1) * LANES]

    top = lax.broadcasted_iota(jnp.int32, (SEG, LANES), 0) == 0
    for q in range(2):
        lanes = pl.ds(q * LANES, LANES)
        bcast = lambda r: jnp.broadcast_to(prm[pl.ds(r, 1), lanes], (SEG, LANES))
        decay = [bcast(k) for k in range(MODES)]
        taps = [[bcast(2 * MODES + 3 * j + g) for g in range(3)] for j in range(3)]

        def load(g, i):
            return proj[2 * g + q, pl.ds(pl.multiple_of(HALO + i * SEG, SEG), SEG), :]

        def load_before(g, back):
            halo = proj[2 * g + q, pl.ds(HALO - back, 1), :]
            return jnp.where(top, halo, pltpu.roll(load(g, seg_len - back), 1, 0))

        def step(i, carry):
            before, last, states = carry
            now = [load(g, i) for g in range(3)]
            feat = [
                taps[0][g] * now[g] + taps[1][g] * last[g] + taps[2][g] * before[g]
                for g in range(3)
            ]
            product = feat[1] * feat[2]
            at = pl.ds(pl.multiple_of(i * SEG, SEG), SEG)
            prod_ref[at, lanes] = product
            x1_ref[at, lanes] = feat[0]
            return (last, now, [decay[k] * states[k] + product for k in range(MODES)])

        zero = jnp.zeros((SEG, LANES), F32)
        first = tuple([load_before(g, back) for g in range(3)] for back in (2, 1))
        _, _, states = lax.fori_loop(0, seg_len, step, (*first, [zero] * MODES), unroll=4)
        for k in range(MODES):
            rate = prm[pl.ds(48 + k, 1), lanes]
            u = states[k]
            for n in (1, 2, 4):
                u = u + jnp.exp(-rate * (float(n) * seg_len)) * shift_down(u, n)
            u_ref[pl.ds(k * SEG, SEG), lanes] = u
            end_ref[pl.ds(k, 1), lanes] = u[SEG - 1:]


def project(few, where, lhs, near, far, part, weights, prm, rows):
    vmem = pl.BlockSpec(memory_space=pltpu.VMEM)
    wide, tall = 2 * LANES, rows + HALO
    return pl.pallas_call(
        functools.partial(project_kernel, rows, few),
        out_shape=[
            jax.ShapeDtypeStruct((rows, wide), F32),
            jax.ShapeDtypeStruct((rows, wide), F32),
            jax.ShapeDtypeStruct((MODES * SEG, wide), F32),
            jax.ShapeDtypeStruct((MODES, wide), F32),
        ],
        in_specs=[pl.BlockSpec(memory_space=pltpu.SMEM)] + [vmem] * 13,
        out_specs=[vmem] * 4,
        scratch_shapes=[
            pltpu.VMEM((tall, (2 if few else 5) * BLOCK), jnp.bfloat16),
            pltpu.VMEM(((2 if few else 1) * BLOCK, 3 * wide), jnp.bfloat16),
            pltpu.VMEM((6, tall, LANES), F32),
        ],
        compiler_params=pltpu.CompilerParams(vmem_limit_bytes=26 << 20),
        cost_estimate=pl.CostEstimate(
            flops=2 * tall * 5 * BLOCK * 3 * wide, bytes_accessed=12 << 20, transcendentals=0
        ),
    )(where, lhs, near, far, part, *weights, prm)


def read_kernel(rows, prod_ref, u_ref, prm, y_ref):
    seg_len = rows // SEG
    for q in range(2):
        lanes = pl.ds(q * LANES, LANES)
        bcast = lambda r: jnp.broadcast_to(prm[pl.ds(r, 1), lanes], (SEG, LANES))
        decay = [bcast(k) for k in range(MODES)]
        amp = [bcast(MODES + k) for k in range(MODES)]
        gain = bcast(2 * MODES + 9)

        def step(i, states):
            at = pl.ds(pl.multiple_of(i * SEG, SEG), SEG)
            product = prod_ref[at, lanes]
            states = [decay[k] * states[k] + product for k in range(MODES)]
            terms = [amp[k] * states[k] for k in range(MODES)] + [gain * product]
            while len(terms) > 1:
                terms = [a + b for a, b in zip(terms[::2], terms[1::2])] + (
                    [terms[-1]] if len(terms) % 2 else []
                )
            y_ref[at, lanes] = terms[0]
            return states

        start = [shift_down(u_ref[pl.ds(k * SEG, SEG), lanes], 1) for k in range(MODES)]
        lax.fori_loop(0, seg_len, step, start, unroll=4)


def read(prod, u, prm, rows):
    vmem = pl.BlockSpec(memory_space=pltpu.VMEM)
    return pl.pallas_call(
        functools.partial(read_kernel, rows),
        out_shape=jax.ShapeDtypeStruct(prod.shape, F32),
        in_specs=[vmem] * 3,
        out_specs=vmem,
        compiler_params=pltpu.CompilerParams(vmem_limit_bytes=12 << 20),
        cost_estimate=pl.CostEstimate(
            flops=4 * MODES * prod.size, bytes_accessed=12 << 20, transcendentals=0
        ),
    )(prod, u, prm)


def gate_kernel(rows, core_ref, y0, y1, x0, x1, p0, p1, local, up, two, down, first, scale, out_ref, wide):
    seg_len = rows // SEG
    core = core_ref[0]
    seg = lax.broadcasted_iota(jnp.int32, (SEG, LANES), 0).astype(F32) * seg_len
    for o, (y, x, prm) in enumerate(((y0, x0, p0), (y1, x1, p1))):
        base = lax.rem(core + o, 2) * (2 * LANES)
        for q in range(2):
            lanes = pl.ds(q * LANES, LANES)
            to = pl.ds(pl.multiple_of(base + q * LANES, LANES), LANES)
            state = local[:, to] + up[:, to] + two[:, to] + down[:, to]
            state = scale[:, to] * state + first[:, to]
            decay, carried = [], []
            for k in range(MODES):
                d = jnp.broadcast_to(prm[pl.ds(k, 1), lanes], (SEG, LANES))
                rate = prm[pl.ds(48 + k, 1), lanes]
                start = jnp.exp(-rate * seg) * state[k:k + 1]
                decay.append(d)
                carried.append(prm[pl.ds(MODES + k, 1), lanes] * d * start)

            def step(i, carried):
                terms = list(carried)
                while len(terms) > 1:
                    terms = [a + b for a, b in zip(terms[::2], terms[1::2])]
                at = pl.ds(pl.multiple_of(i * SEG, SEG), SEG)
                wide[pl.ds(i, SEG, stride=seg_len), :] = x[at, lanes] * (
                    y[at, lanes] + terms[0]
                )
                return [c * d for c, d in zip(carried, decay)]

            lax.fori_loop(0, seg_len, step, carried, unroll=8)
            out_ref[:, to] = wide[...].astype(out_ref.dtype)


def gate(core, ys, xs, prms, state, rows):
    vmem = pl.BlockSpec(memory_space=pltpu.VMEM)
    return pl.pallas_call(
        functools.partial(gate_kernel, rows),
        out_shape=jax.ShapeDtypeStruct((rows, BLOCK), jnp.bfloat16),
        in_specs=[pl.BlockSpec(memory_space=pltpu.SMEM)] + [vmem] * 12,
        out_specs=vmem,
        scratch_shapes=[pltpu.VMEM((rows, LANES), F32)],
        compiler_params=pltpu.CompilerParams(vmem_limit_bytes=20 << 20),
    )(core, *ys, *xs, *prms, *state)


def on_device(tokens, in_weight, short_filter, filter_residues, filter_rates, skip_gain):
    rows = tokens.shape[0]
    ctx, tp = lax.axis_index("ctx"), lax.axis_index("tp")
    y_lo, x, core = ctx // 8, (ctx // 2) % 4, ctx % 2
    y_hi, z = tp // 4, tp % 4
    wide = 2 * LANES

    base = tp * BLOCK
    rates = lax.dynamic_slice_in_dim(filter_rates, base, BLOCK, 0).T
    amps = lax.dynamic_slice_in_dim(filter_residues, base, BLOCK, 0).T * jnp.sqrt(rates)
    taps = lax.dynamic_slice_in_dim(short_filter, base, BLOCK, 2).reshape(9, BLOCK)
    gains = lax.dynamic_slice_in_dim(skip_gain, base, BLOCK, 0)[None]
    prm = jnp.concatenate(
        [jnp.exp(-rates), amps, taps, gains, jnp.zeros((6, BLOCK), F32), rates], axis=0
    )
    prms = [lax.dynamic_slice_in_dim(prm, (core + o) % 2 * wide, wide, 1) for o in range(2)]

    def fade(steps):
        return jnp.exp(-rates * jnp.asarray(steps).astype(F32))

    shard = fade(rows)
    scale = jnp.where(core == 0, 1.0, shard)
    own, lower = [], []
    for m in range(4):
        to = (x + m) % 4
        own.append(jnp.where(to > x, fade(2 * rows * jnp.maximum(to - x - 1, 0)), 0.0))
        lower.append(jnp.where(y_lo == 1, fade(2 * rows * (to + 3 - x)), 0.0))
    own, lower = jnp.stack(own), jnp.stack(lower)

    slots = []
    for of_y in (y_lo, 1 - y_lo):
        for ring in (0, -1, 1, 2):
            of_z = (x + ring - z) % 4
            step = (of_z - z) % 4
            place = jnp.where(step == 3, 1, jnp.where(step == 1, 2, jnp.where(step == 2, 3, 0)))
            slots.append(jnp.where(of_y == y_hi, 0, 4) + place)
    where = jnp.stack(slots + [core]).astype(jnp.int32)
    core_at = jnp.stack([core]).astype(jnp.int32)

    def next_ctx(yl, x, c, yh, z):
        n = (yl * 4 + x) * 2 + c + 1
        return None if n == 16 else (n // 8, (n // 2) % 4, n % 2, yh, z)

    w = in_weight.transpose(1, 0, 2)
    b = transposed(w)
    shard_tokens, *prms = together((tokens, *prms))
    steps = shard_tokens.reshape(SEG, rows // SEG, BLOCK).transpose(1, 0, 2).reshape(rows, BLOCK)
    t = jnp.concatenate([send(shard_tokens[rows - HALO:], next_ctx), steps], axis=0)
    t, b, where, core_at, shard, scale, own, lower, *prms = together(
        (t, b, where, core_at, shard, scale, own, lower, *prms)
    )
    ty = other_yhi(t)
    tp_, tm = along_z(t, 1), along_z(t, -1)
    bp, bm = along_x(b, 1), along_x(b, -1)
    ty, t, b, tp_, tm, bp, bm = together((ty, t, b, tp_, tm, bp, bm))
    typ, tym = along_z(ty, 1), along_z(ty, -1)
    cb, cbp, cbm = other_core(b), other_core(bp), other_core(bm)
    b, bp, cb, cbp, cbm = together((b, bp, cb, cbp, cbm))
    bf, a = along_x(bp, 1), other_ylo(b)
    t, b, tp_, tm, ty, bp, bm, typ, tym, bf, a, cb, cbp, cbm = together(
        (t, b, tp_, tm, ty, bp, bm, typ, tym, bf, a, cb, cbp, cbm)
    )
    tf, tyf = along_z(tp_, 1), along_z(tym, -1)
    ap = along_x(a, 1)
    cbf, ca = other_core(bf), other_core(a)
    bf, a, cbf, ca = together((bf, a, cbf, ca))
    am, af = along_x(a, -1), other_ylo(bf)
    lhs, part = begin(where, [t, tp_, tm, ty, typ, tym], [b, bp, bm, bf], rows)
    part_too = also(where, lhs, [cb, cbp, cbm, cbf], rows)
    part = more(where, lhs, part, [a, ap, am, af], rows)
    lhs, part, part_too, ap, am, af, tf, tyf = together(
        (lhs, part, part_too, ap, am, af, tf, tyf)
    )
    mine = [b, bp, bm, bf, a, ap, am, af]
    theirs = [cb, cbp, cbm, cbf, ca] + [other_core(w) for w in (ap, am, af)]

    products, xs, us, ends = [], [], [], []
    for o, (weights, done) in enumerate(((mine, part), (theirs, part_too))):
        product, x1, u, end = project(o == 0, where, lhs, tf, tyf, done, weights, prms[o], rows)
        products.append(product)
        xs.append(x1)
        us.append(u)
        ends.append(end)

    total = jnp.concatenate(
        [jnp.where(core == 0, ends[0], ends[1]), jnp.where(core == 0, ends[1], ends[0])], axis=1
    )
    total, products[0] = together((total, products[0]))
    came = [total, other_core(total), other_ylo(total), other_ylo_and_core(total)]
    y0 = read(products[0], us[0], prms[0], rows)
    came, products[1], y0 = together((came, products[1], y0))

    def chip_end(mine, other):
        return shard * jnp.where(core == 0, mine, other) + jnp.where(core == 0, other, mine)

    here, there = chip_end(*came[:2]), chip_end(*came[2:])
    ends = [own[m] * here + lower[m] * there for m in range(4)]
    state = ends[:1] + [along_x(ends[m], m) for m in (1, 2, 3)]
    first = jnp.where(core == 0, 0.0, came[1])
    y1 = read(products[1], us[1], prms[1], rows)
    return gate(core_at, [y0, y1], xs, prms, [*state, first, scale], rows)


def solution(mesh):
    placed = (P("ctx", "tp"), P("tp", None, "ctx"), P(), P(), P(), P())
    return jax.shard_map(
        on_device, mesh=mesh, in_specs=placed, out_specs=P("ctx", "tp"), check_vma=False
    )
```

```python
import functools

import jax
import jax.numpy as jnp
from jax import lax
from jax.experimental import pallas as pl
from jax.experimental.pallas import tpu as pltpu
from jax.sharding import PartitionSpec as P

D = 4096
MODES = 16
BLOCK = 512
SEG = 8
HALO = 16
SIZES = (2, 4, 2, 2, 4)
LANES = 128
F32 = jnp.float32


def route(move):
    pairs = []
    for yl in range(2):
        for x in range(4):
            for c in range(2):
                for yh in range(2):
                    for z in range(4):
                        to = move(yl, x, c, yh, z)
                        if to is None:
                            continue
                        a, b, e, f, g = to
                        pairs.append(
                            (
                                ((yl * 4 + x) * 2 + c) * 8 + yh * 4 + z,
                                (((a % 2) * 4 + b % 4) * 2 + e % 2) * 8 + (f % 2) * 4 + g % 4,
                            )
                        )
    return pairs


def send(value, move):
    return lax.ppermute(value, ("ctx", "tp"), route(move))


def along_z(value, step):
    return send(value, lambda yl, x, c, yh, z: (yl, x, c, yh, z + step))


def along_x(value, step):
    return send(value, lambda yl, x, c, yh, z: (yl, x + step, c, yh, z))


def other_core(value):
    return send(value, lambda yl, x, c, yh, z: (yl, x, c + 1, yh, z))


def other_yhi(value):
    return send(value, lambda yl, x, c, yh, z: (yl, x, c, yh + 1, z))


def other_ylo(value):
    return send(value, lambda yl, x, c, yh, z: (yl + 1, x, c, yh, z))


def other_ylo_and_core(value):
    return send(value, lambda yl, x, c, yh, z: (yl + 1, x, c + 1, yh, z))


def transposed(value):
    return send(value, lambda yl, x, c, yh, z: (yh, x + z, c, yl, x))


together = lax.optimization_barrier


def shift_down(value, steps):
    rows = lax.broadcasted_iota(jnp.int32, value.shape, 0)
    return jnp.where(rows >= steps, pltpu.roll(value, steps, 0), 0.0)


def side_by_side(weight):
    return jnp.concatenate([weight[g] for g in range(3)], axis=1)


def first_half(where, lhs, weights, acc):
    acc[...] = jnp.zeros_like(acc)
    for k in range(4):
        slot = where[k]

        @pl.when(lax.rem(slot, 4) != 3)
        def _(k=k, slot=slot):
            acc[...] += jnp.dot(lhs[slot], side_by_side(weights[k]), preferred_element_type=F32)


def begin_kernel(where, *refs):
    toks, weights, (lhs, acc) = refs[:6], refs[6:10], refs[10:]
    for n, s in enumerate((0, 1, 2, 4, 5, 6)):
        lhs[s] = toks[n][...]
    first_half(where, lhs, weights, acc)


def also_kernel(where, *refs):
    lhs, weights, acc = refs[0], refs[1:5], refs[5]
    first_half(where, lhs, weights, acc)


def begin(where, toks, weights, rows):
    vmem = pl.BlockSpec(memory_space=pltpu.VMEM)
    tall, width = rows + HALO, 3 * weights[0].shape[2]
    return pl.pallas_call(
        begin_kernel,
        out_shape=[
            jax.ShapeDtypeStruct((8, tall, BLOCK), jnp.bfloat16),
            jax.ShapeDtypeStruct((tall, width), F32),
        ],
        in_specs=[pl.BlockSpec(memory_space=pltpu.SMEM)] + [vmem] * 10,
        out_specs=[vmem] * 2,
        compiler_params=pltpu.CompilerParams(vmem_limit_bytes=26 << 20),
        cost_estimate=pl.CostEstimate(
            flops=2 * tall * 3 * BLOCK * width, bytes_accessed=12 << 20, transcendentals=0
        ),
    )(where, *toks, *weights)


def also(where, lhs, weights, rows):
    vmem = pl.BlockSpec(memory_space=pltpu.VMEM)
    tall, width = rows + HALO, 3 * weights[0].shape[2]
    return pl.pallas_call(
        also_kernel,
        out_shape=jax.ShapeDtypeStruct((tall, width), F32),
        in_specs=[pl.BlockSpec(memory_space=pltpu.SMEM)] + [vmem] * 5,
        out_specs=vmem,
        compiler_params=pltpu.CompilerParams(vmem_limit_bytes=26 << 20),
        cost_estimate=pl.CostEstimate(
            flops=2 * tall * 3 * BLOCK * width, bytes_accessed=12 << 20, transcendentals=0
        ),
    )(where, lhs, *weights)


def more_kernel(where, lhs, part, *refs):
    weights, acc = refs[:4], refs[4]
    is_near = [lax.rem(where[4 + k], 4) != 3 for k in range(4)]

    def product(k):
        return jnp.dot(lhs[where[4 + k]], side_by_side(weights[k]), preferred_element_type=F32)

    def start(k):
        acc[...] = part[...] + product(k)

    def add(k):
        acc[...] += product(k)

    pl.when(is_near[0])(functools.partial(start, 0))
    pl.when(jnp.logical_not(is_near[0]))(functools.partial(start, 1))
    pl.when(jnp.logical_and(is_near[0], is_near[1]))(functools.partial(add, 1))
    pl.when(is_near[2])(functools.partial(add, 2))
    pl.when(is_near[3])(functools.partial(add, 3))


def more(where, lhs, part, weights, rows):
    vmem = pl.BlockSpec(memory_space=pltpu.VMEM)
    tall, width = rows + HALO, 3 * weights[0].shape[2]
    return pl.pallas_call(
        more_kernel,
        out_shape=jax.ShapeDtypeStruct((tall, width), F32),
        in_specs=[pl.BlockSpec(memory_space=pltpu.SMEM)] + [vmem] * 6,
        out_specs=vmem,
        compiler_params=pltpu.CompilerParams(vmem_limit_bytes=26 << 20),
        cost_estimate=pl.CostEstimate(
            flops=2 * tall * 3 * BLOCK * width, bytes_accessed=12 << 20, transcendentals=0
        ),
    )(where, lhs, part, *weights)


def project_kernel(rows, few, where, *refs):
    lhs, near, far, part, *refs = refs
    weights, refs = refs[:8], refs[8:]
    prm, prod_ref, x1_ref, u_ref, end_ref, last, late, proj = refs
    seg_len = rows // SEG
    for k in range(8):
        at = pl.ds((k // 4 if few else max(k - 3, 0)) * BLOCK, BLOCK)
        for s, ref in ((3, near), (7, far)):

            @pl.when(where[k] == s)
            def _(k=k, ref=ref, at=at):
                last[:, at] = ref[...]
                if few or k < 4:
                    late[at, :] = side_by_side(weights[k])

        if k >= 4 and not few:

            @pl.when(lax.rem(where[k], 4) != 3)
            def _(k=k, at=at):
                last[:, at] = lhs[where[k]]

    for n in range(3):
        cols = pl.ds(n * 2 * LANES, 2 * LANES)
        right = jnp.concatenate([late[:, cols]] + [w[n] for w in ([] if few else weights[4:])], axis=0)
        out = part[:, cols] + jnp.dot(last[...], right, preferred_element_type=F32)
        out = out.astype(jnp.bfloat16).astype(F32)
        for q in range(2):
            proj[2 * n + q] = out[:, q * LANES:(q + 1) * LANES]

    top = lax.broadcasted_iota(jnp.int32, (SEG, LANES), 0) == 0
    for q in range(2):
        lanes = pl.ds(q * LANES, LANES)
        bcast = lambda r: jnp.broadcast_to(prm[pl.ds(r, 1), lanes], (SEG, LANES))
        decay = [bcast(k) for k in range(MODES)]
        taps = [[bcast(2 * MODES + 3 * j + g) for g in range(3)] for j in range(3)]

        def load(g, i):
            return proj[2 * g + q, pl.ds(pl.multiple_of(HALO + i * SEG, SEG), SEG), :]

        def load_before(g, back):
            halo = proj[2 * g + q, pl.ds(HALO - back, 1), :]
            return jnp.where(top, halo, pltpu.roll(load(g, seg_len - back), 1, 0))

        def step(i, carry):
            before, last, states = carry
            now = [load(g, i) for g in range(3)]
            feat = [
                taps[0][g] * now[g] + taps[1][g] * last[g] + taps[2][g] * before[g]
                for g in range(3)
            ]
            product = feat[1] * feat[2]
            at = pl.ds(pl.multiple_of(i * SEG, SEG), SEG)
            prod_ref[at, lanes] = product
            x1_ref[at, lanes] = feat[0]
            return (last, now, [decay[k] * states[k] + product for k in range(MODES)])

        zero = jnp.zeros((SEG, LANES), F32)
        first = tuple([load_before(g, back) for g in range(3)] for back in (2, 1))
        _, _, states = lax.fori_loop(0, seg_len, step, (*first, [zero] * MODES), unroll=8)
        for k in range(MODES):
            rate = prm[pl.ds(48 + k, 1), lanes]
            u = states[k]
            for n in (1, 2, 4):
                u = u + jnp.exp(-rate * (float(n) * seg_len)) * shift_down(u, n)
            u_ref[pl.ds(k * SEG, SEG), lanes] = u
            end_ref[pl.ds(k, 1), lanes] = u[SEG - 1:]


def project(few, where, lhs, near, far, part, weights, prm, rows):
    vmem = pl.BlockSpec(memory_space=pltpu.VMEM)
    wide, tall = 2 * LANES, rows + HALO
    return pl.pallas_call(
        functools.partial(project_kernel, rows, few),
        out_shape=[
            jax.ShapeDtypeStruct((rows, wide), F32),
            jax.ShapeDtypeStruct((rows, wide), F32),
            jax.ShapeDtypeStruct((MODES * SEG, wide), F32),
            jax.ShapeDtypeStruct((MODES, wide), F32),
        ],
        in_specs=[pl.BlockSpec(memory_space=pltpu.SMEM)] + [vmem] * 13,
        out_specs=[vmem] * 4,
        scratch_shapes=[
            pltpu.VMEM((tall, (2 if few else 5) * BLOCK), jnp.bfloat16),
            pltpu.VMEM(((2 if few else 1) * BLOCK, 3 * wide), jnp.bfloat16),
            pltpu.VMEM((6, tall, LANES), F32),
        ],
        compiler_params=pltpu.CompilerParams(vmem_limit_bytes=26 << 20),
        cost_estimate=pl.CostEstimate(
            flops=2 * tall * 5 * BLOCK * 3 * wide, bytes_accessed=12 << 20, transcendentals=0
        ),
    )(where, lhs, near, far, part, *weights, prm)


def read_kernel(rows, prod_ref, u_ref, prm, y_ref):
    seg_len = rows // SEG
    for q in range(2):
        lanes = pl.ds(q * LANES, LANES)
        bcast = lambda r: jnp.broadcast_to(prm[pl.ds(r, 1), lanes], (SEG, LANES))
        decay = [bcast(k) for k in range(MODES)]
        amp = [bcast(MODES + k) for k in range(MODES)]
        gain = bcast(2 * MODES + 9)

        def step(i, states):
            at = pl.ds(pl.multiple_of(i * SEG, SEG), SEG)
            product = prod_ref[at, lanes]
            states = [decay[k] * states[k] + product for k in range(MODES)]
            terms = [amp[k] * states[k] for k in range(MODES)] + [gain * product]
            while len(terms) > 1:
                terms = [a + b for a, b in zip(terms[::2], terms[1::2])] + (
                    [terms[-1]] if len(terms) % 2 else []
                )
            y_ref[at, lanes] = terms[0]
            return states

        start = [shift_down(u_ref[pl.ds(k * SEG, SEG), lanes], 1) for k in range(MODES)]
        lax.fori_loop(0, seg_len, step, start, unroll=8)


def read(prod, u, prm, rows):
    vmem = pl.BlockSpec(memory_space=pltpu.VMEM)
    return pl.pallas_call(
        functools.partial(read_kernel, rows),
        out_shape=jax.ShapeDtypeStruct(prod.shape, F32),
        in_specs=[vmem] * 3,
        out_specs=vmem,
        compiler_params=pltpu.CompilerParams(vmem_limit_bytes=12 << 20),
        cost_estimate=pl.CostEstimate(
            flops=4 * MODES * prod.size, bytes_accessed=12 << 20, transcendentals=0
        ),
    )(prod, u, prm)


def gate_kernel(rows, core_ref, y0, y1, x0, x1, p0, p1, local, up, two, down, first, scale, out_ref, wide):
    seg_len = rows // SEG
    core = core_ref[0]
    seg = lax.broadcasted_iota(jnp.int32, (SEG, LANES), 0).astype(F32) * seg_len
    for o, (y, x, prm) in enumerate(((y0, x0, p0), (y1, x1, p1))):
        base = lax.rem(core + o, 2) * (2 * LANES)
        for q in range(2):
            lanes = pl.ds(q * LANES, LANES)
            to = pl.ds(pl.multiple_of(base + q * LANES, LANES), LANES)
            state = local[:, to] + up[:, to] + two[:, to] + down[:, to]
            state = scale[:, to] * state + first[:, to]
            decay, carried = [], []
            for k in range(MODES):
                d = jnp.broadcast_to(prm[pl.ds(k, 1), lanes], (SEG, LANES))
                rate = prm[pl.ds(48 + k, 1), lanes]
                start = jnp.exp(-rate * seg) * state[k:k + 1]
                decay.append(d)
                carried.append(prm[pl.ds(MODES + k, 1), lanes] * d * start)

            def step(i, carried):
                terms = list(carried)
                while len(terms) > 1:
                    terms = [a + b for a, b in zip(terms[::2], terms[1::2])]
                at = pl.ds(pl.multiple_of(i * SEG, SEG), SEG)
                wide[pl.ds(i, SEG, stride=seg_len), :] = x[at, lanes] * (
                    y[at, lanes] + terms[0]
                )
                return [c * d for c, d in zip(carried, decay)]

            lax.fori_loop(0, seg_len, step, carried, unroll=8)
            out_ref[:, to] = wide[...].astype(out_ref.dtype)


def gate(core, ys, xs, prms, state, rows):
    vmem = pl.BlockSpec(memory_space=pltpu.VMEM)
    return pl.pallas_call(
        functools.partial(gate_kernel, rows),
        out_shape=jax.ShapeDtypeStruct((rows, BLOCK), jnp.bfloat16),
        in_specs=[pl.BlockSpec(memory_space=pltpu.SMEM)] + [vmem] * 12,
        out_specs=vmem,
        scratch_shapes=[pltpu.VMEM((rows, LANES), F32)],
        compiler_params=pltpu.CompilerParams(vmem_limit_bytes=20 << 20),
    )(core, *ys, *xs, *prms, *state)


def on_device(tokens, in_weight, short_filter, filter_residues, filter_rates, skip_gain):
    rows = tokens.shape[0]
    ctx, tp = lax.axis_index("ctx"), lax.axis_index("tp")
    y_lo, x, core = ctx // 8, (ctx // 2) % 4, ctx % 2
    y_hi, z = tp // 4, tp % 4
    wide = 2 * LANES

    base = tp * BLOCK
    rates = lax.dynamic_slice_in_dim(filter_rates, base, BLOCK, 0).T
    amps = lax.dynamic_slice_in_dim(filter_residues, base, BLOCK, 0).T * jnp.sqrt(rates)
    taps = lax.dynamic_slice_in_dim(short_filter, base, BLOCK, 2).reshape(9, BLOCK)
    gains = lax.dynamic_slice_in_dim(skip_gain, base, BLOCK, 0)[None]
    prm = jnp.concatenate(
        [jnp.exp(-rates), amps, taps, gains, jnp.zeros((6, BLOCK), F32), rates], axis=0
    )
    prms = [lax.dynamic_slice_in_dim(prm, (core + o) % 2 * wide, wide, 1) for o in range(2)]

    def fade(steps):
        return jnp.exp(-rates * jnp.asarray(steps).astype(F32))

    shard = fade(rows)
    scale = jnp.where(core == 0, 1.0, shard)
    own, lower = [], []
    for m in range(4):
        to = (x + m) % 4
        own.append(jnp.where(to > x, fade(2 * rows * jnp.maximum(to - x - 1, 0)), 0.0))
        lower.append(jnp.where(y_lo == 1, fade(2 * rows * (to + 3 - x)), 0.0))
    own, lower = jnp.stack(own), jnp.stack(lower)

    slots = []
    for of_y in (y_lo, 1 - y_lo):
        for ring in (0, -1, 1, 2):
            of_z = (x + ring - z) % 4
            step = (of_z - z) % 4
            place = jnp.where(step == 3, 1, jnp.where(step == 1, 2, jnp.where(step == 2, 3, 0)))
            slots.append(jnp.where(of_y == y_hi, 0, 4) + place)
    where = jnp.stack(slots + [core]).astype(jnp.int32)
    core_at = jnp.stack([core]).astype(jnp.int32)

    def next_ctx(yl, x, c, yh, z):
        n = (yl * 4 + x) * 2 + c + 1
        return None if n == 16 else (n // 8, (n // 2) % 4, n % 2, yh, z)

    w = in_weight.transpose(1, 0, 2)
    b = transposed(w)
    shard_tokens, *prms = together((tokens, *prms))
    steps = shard_tokens.reshape(SEG, rows // SEG, BLOCK).transpose(1, 0, 2).reshape(rows, BLOCK)
    t = jnp.concatenate([send(shard_tokens[rows - HALO:], next_ctx), steps], axis=0)
    t, b, where, core_at, shard, scale, own, lower, *prms = together(
        (t, b, where, core_at, shard, scale, own, lower, *prms)
    )
    ty = other_yhi(t)
    tp_, tm = along_z(t, 1), along_z(t, -1)
    bp, bm = along_x(b, 1), along_x(b, -1)
    ty, t, b, tp_, tm, bp, bm = together((ty, t, b, tp_, tm, bp, bm))
    typ, tym = along_z(ty, 1), along_z(ty, -1)
    cb, cbp, cbm = other_core(b), other_core(bp), other_core(bm)
    b, bp, cb, cbp, cbm = together((b, bp, cb, cbp, cbm))
    bf, a = along_x(bp, 1), other_ylo(b)
    t, b, tp_, tm, ty, bp, bm, typ, tym, bf, a, cb, cbp, cbm = together(
        (t, b, tp_, tm, ty, bp, bm, typ, tym, bf, a, cb, cbp, cbm)
    )
    tf, tyf = along_z(tp_, 1), along_z(tym, -1)
    ap = along_x(a, 1)
    cbf, ca = other_core(bf), other_core(a)
    bf, a, cbf, ca = together((bf, a, cbf, ca))
    am, af = along_x(a, -1), other_ylo(bf)
    lhs, part = begin(where, [t, tp_, tm, ty, typ, tym], [b, bp, bm, bf], rows)
    part_too = also(where, lhs, [cb, cbp, cbm, cbf], rows)
    part = more(where, lhs, part, [a, ap, am, af], rows)
    lhs, part, part_too, ap, am, af, tf, tyf = together(
        (lhs, part, part_too, ap, am, af, tf, tyf)
    )
    mine = [b, bp, bm, bf, a, ap, am, af]
    theirs = [cb, cbp, cbm, cbf, ca] + [other_core(w) for w in (ap, am, af)]

    products, xs, us, ends = [], [], [], []
    for o, (weights, done) in enumerate(((mine, part), (theirs, part_too))):
        product, x1, u, end = project(o == 0, where, lhs, tf, tyf, done, weights, prms[o], rows)
        products.append(product)
        xs.append(x1)
        us.append(u)
        ends.append(end)

    total = jnp.concatenate(
        [jnp.where(core == 0, ends[0], ends[1]), jnp.where(core == 0, ends[1], ends[0])], axis=1
    )
    total, products[0] = together((total, products[0]))
    came = [total, other_core(total), other_ylo(total), other_ylo_and_core(total)]
    y0 = read(products[0], us[0], prms[0], rows)
    came, products[1], y0 = together((came, products[1], y0))

    def chip_end(mine, other):
        return shard * jnp.where(core == 0, mine, other) + jnp.where(core == 0, other, mine)

    here, there = chip_end(*came[:2]), chip_end(*came[2:])
    ends = [own[m] * here + lower[m] * there for m in range(4)]
    state = ends[:1] + [along_x(ends[m], m) for m in (1, 2, 3)]
    first = jnp.where(core == 0, 0.0, came[1])
    y1 = read(products[1], us[1], prms[1], rows)
    return gate(core_at, [y0, y1], xs, prms, [*state, first, scale], rows)


def solution(mesh):
    placed = (P("ctx", "tp"), P("tp", None, "ctx"), P(), P(), P(), P())
    return jax.shard_map(
        on_device, mesh=mesh, in_specs=placed, out_specs=P("ctx", "tp"), check_vma=False
    )
```
